256 devices in a mesh: tm: 16 (over z, core), blk: 16 (over y, x).
Axes of the slice: x: 4, y: 4, z: 8, core: 2. Of those that a mesh axis runs over, the one named last changes fastest.
Arguments:
- interior_inverse: bfloat16 [16, 2048, 2048], P('tm', 'blk'), may hold values from -1 to 2
- coupling: bfloat16 [16, 2048, 2048], P('tm', 'blk'), may hold values from -0.125 to 0.125
- separator: float32 [16, 2048, 2048], P('tm', 'blk'), may hold values from -1 to 5
- link: bfloat16 [16, 2048, 2048], P('tm', 'blk'), may hold values from -0.125 to 0.125
- source: float32 [16, 64, 2048], P('tm', None, 'blk'), may hold values from -3 to 3
- weights: float32 [16, 2048], P('tm', 'blk'), may hold values from 0.5 to 1.5
Outputs:
- schur: float32 [16, 2048, 2048], P('tm', 'blk')
- sweep: float32 [16, 64, 2048], P('tm', None, 'blk')
- residual: float32 [16, 64, 2048], P('tm', None, 'blk')
The draws below stay inside these ranges and needn't reach their ends.
All inputs are finite; a program needn't handle non-finite values.
Results may differ from the reference program's by a relative error of at most 0.024.
Values may be sent and summed in bfloat16 or wider, within the bound.
No kernel may reach another device: no remote copies, remote signals or barrier semaphores. Data moves between devices by JAX's collectives and lax.ppermute only.
A program may use at most 128 MiB of HBM per device.

```python
import math
import jax
import jax.numpy as jnp
from jax import lax

B = 2048
K = 64
NT = 16


def draw_interior_inverse(key, part):
    key = jax.random.fold_in(key, 11)
    noise = jax.random.truncated_normal(key, -6.0, 6.0, (NT, B, B), jnp.float32)
    matrix = jnp.eye(B, dtype=jnp.float32)[None] + 0.4 * noise / math.sqrt(B)
    return matrix.astype(jnp.bfloat16)


def draw_separator(key, part):
    key = jax.random.fold_in(key, 12)
    diag_key, noise_key = jax.random.split(key)
    diagonal = jax.random.uniform(diag_key, (NT, B), jnp.float32, 2.5, 4.5)
    noise = jax.random.truncated_normal(noise_key, -6.0, 6.0, (NT, B, B), jnp.float32)
    eye_matrix = jnp.eye(B, dtype=jnp.float32)[None]
    return eye_matrix * diagonal[:, :, None] + 0.5 * noise / math.sqrt(B)


def steps_of(own_key, dims, shards, smallest, top_value):
    factor_of = 1.0
    for position, blocks in shards:
        draws = jax.random.uniform(jax.random.fold_in(jax.random.fold_in(own_key, 6), position), (blocks,), jnp.float32, smallest / len(shards), top_value / len(shards))
        factor_of = factor_of * jnp.repeat(jnp.exp(draws), dims[position] // blocks).reshape((-1,) + (1,) * (len(dims) - 1 - position))
    return factor_of


def centred(rng, extent, width, limit, shards=(), held_as=jnp.bfloat16):
    factor_of = steps_of(rng, extent, shards, -0.22, 0.18) if shards else 1.0
    array = jax.random.normal(rng, extent, jnp.float32) * width * factor_of
    return jnp.minimum(jnp.maximum(array, -limit), limit).astype(held_as)


def setup_inputs(seed: int = 0) -> dict:
    streams_of = jax.random.split(jax.random.key(seed), 7)
    interior_inverse = draw_interior_inverse(jax.random.fold_in(streams_of[6], 71), 0)
    coupling = centred(streams_of[1], (NT, B, B), B ** -0.5, 0.125, ((0, 16), (1, 16)))
    separator = draw_separator(jax.random.fold_in(streams_of[6], 71), 0)
    link = centred(streams_of[3], (NT, B, B), B ** -0.5, 0.125, ((0, 16), (1, 16)))
    source = centred(streams_of[4], (NT, K, B), 0.5, 3.0, ((0, 16), (2, 16)), jnp.float32)
    weights = jnp.clip(jnp.exp(math.log(1.5) - 1.0986123 * jax.random.uniform(streams_of[5], (NT, B), jnp.float32) ** steps_of(streams_of[5], (NT, B), ((0, 16), (1, 16)), -0.2, 0.2)), 0.5, 1.5)
    return {"interior_inverse": interior_inverse, "coupling": coupling, "separator": separator, "link": link, "source": source, "weights": weights}


def schur_one(blocks):
    inverse_block, coupling_block, separator_block = blocks
    inner = jnp.dot(inverse_block, coupling_block.T, preferred_element_type=jnp.float32)
    return separator_block - jnp.dot(coupling_block.astype(jnp.float32), inner, precision=lax.Precision.HIGHEST)


def sweep_step(rounded_prev, items):
    link_block, weight_row, source_block = items
    product = jnp.dot(rounded_prev, link_block.T, preferred_element_type=jnp.float32)
    current = weight_row[None, :] * (source_block - product)
    rounded = current.astype(jnp.bfloat16)
    return rounded, (current, product, rounded)


def backward_one(items):
    rounded, link_block = items
    return jnp.dot(rounded, link_block, preferred_element_type=jnp.float32)


def own_one(items):
    rounded, schur_block = items
    return jnp.dot(rounded.astype(jnp.float32), schur_block.T, precision=lax.Precision.HIGHEST)


def reference(interior_inverse, coupling, separator, link, source, weights):
    schur = lax.map(schur_one, (interior_inverse, coupling, separator))
    start_value = jnp.zeros((K, B), jnp.bfloat16)
    last_value, outputs = lax.scan(sweep_step, start_value, (link, weights, source))
    sweep, product, rounded = outputs
    backward = lax.map(backward_one, (rounded, link))
    following = jnp.concatenate([backward[1:], jnp.zeros((1, K, B), jnp.float32)], axis=0)
    own_terms = lax.map(own_one, (rounded, schur))
    residual = source - own_terms - product - following
    return schur, sweep, residual
```

```python
import jax
import jax.numpy as jnp
from jax import lax
from jax.sharding import PartitionSpec as P

AXES = ("tm", "blk")
SIDE = 4


def moved(p, b, along_reduce, step):
    y, x = divmod(b, SIDE)
    if (p % 2 == 0) == along_reduce:
        x ^= step
    else:
        y ^= step
    return y * SIDE + x


def send(value, partitions, shift, along_reduce, step):
    plane = SIDE * SIDE
    pairs = [
        (p * plane + b, (p + shift) * plane + moved(p, b, along_reduce, step))
        for p in partitions
        for b in range(plane)
    ]
    return lax.ppermute(value, AXES, pairs)


def shards(interior_inverse, coupling, separator, link, source, weights):
    f32, bf16 = jnp.float32, jnp.bfloat16
    count = lax.axis_size("tm")
    everyone = range(count)
    inverse_rows, coupling_rows, separator_rows = interior_inverse[0], coupling[0], separator[0]
    source_rows, weight_row = source[0], weights[0]
    rows, nodes = link.shape[1:]
    keys = source_rows.shape[0]
    group = SIDE * rows
    p = lax.axis_index("tm")
    b = lax.axis_index("blk")
    y, x = b // SIDE, b % SIDE
    even = p % 2 == 0
    r = jnp.where(even, x, y)
    q = jnp.where(even, y, x)

    coupling_all = lax.all_gather(coupling_rows, "blk", axis=0, tiled=True)
    inverse_all = lax.all_gather(inverse_rows, "blk", axis=0, tiled=True)

    shaped = link[0].reshape(rows, SIDE, SIDE, rows)
    chunks = jnp.where(
        even,
        shaped.transpose(2, 0, 1, 3).reshape(SIDE, rows, group),
        shaped.transpose(1, 0, 2, 3).reshape(SIDE, rows, group),
    )
    high = weight_row.astype(bf16)
    rest = weight_row - high.astype(f32)
    middle = rest.astype(bf16)
    low = (rest - middle.astype(f32)).astype(bf16)
    packed = jnp.zeros((16, group), bf16)
    packed = packed.at[:3, :rows].set(jnp.stack([high, middle, low]))

    def chunk(step):
        part = lax.dynamic_index_in_dim(chunks, r ^ step, 0, keepdims=False)
        return jnp.concatenate([part, packed], axis=0)

    pieces = [chunk(0)]
    for step in range(1, SIDE):
        pieces.append(send(chunk(step), everyone, 0, True, step))
    pieces = jnp.stack(pieces)
    order = r ^ jnp.arange(SIDE)
    pieces = pieces[order]
    block = pieces[:, :rows].reshape(group, group)
    weight_group = pieces[:, rows : rows + 3, :rows].astype(f32).sum(axis=1).reshape(1, group)

    own = lax.dynamic_update_slice(
        jnp.zeros((keys, group), f32), weight_row[None, :] * source_rows, (0, r * rows)
    )

    message = own.astype(bf16)
    final = message
    for turn in range(1, count):
        parts = [send(message, [turn - 1], 1, True, step).astype(f32) for step in range(SIDE)]
        previous = (parts[0] + parts[1] + parts[2] + parts[3]).astype(bf16)
        product = lax.dot_general(
            previous, block, (((1,), (1,)), ((), ())), preferred_element_type=f32
        )
        message = (own - weight_group * product).astype(bf16)
        final = jnp.where(p == turn, message, final)

    total = final.astype(f32)
    for step in range(1, SIDE):
        total = total + send(final, everyone, 0, True, step).astype(f32)
    rounded = total.astype(bf16)
    sweep = lax.dynamic_slice(total, (0, r * rows), (keys, rows))

    back = jnp.dot(rounded, block, preferred_element_type=f32).astype(bf16)
    back = back.reshape(keys, SIDE, rows)
    following = jnp.zeros((keys, rows), f32)
    for step in range(SIDE):
        piece = lax.dynamic_index_in_dim(back, q ^ step, 1, keepdims=False)
        following = following + send(piece, range(1, count), -1, False, step).astype(f32)

    folded = jnp.dot(coupling_rows, inverse_all, preferred_element_type=f32).astype(bf16)
    schur_rows = separator_rows - lax.dot_general(
        folded, coupling_all, (((1,), (1,)), ((), ())), preferred_element_type=f32
    )
    columns = schur_rows.astype(bf16).reshape(rows, SIDE, SIDE, rows)
    columns = jnp.where(
        even,
        columns.reshape(rows, SIDE, group).transpose(1, 0, 2),
        columns.transpose(2, 0, 1, 3).reshape(SIDE, rows, group),
    )
    own_terms = jnp.zeros((keys, rows), f32)
    for step in range(SIDE):
        seen = rounded if step == 0 else send(rounded, everyone, 0, False, step)
        part = lax.dynamic_index_in_dim(columns, q ^ step, 0, keepdims=False)
        own_terms = own_terms + lax.dot_general(
            seen, part, (((1,), (1,)), ((), ())), preferred_element_type=f32
        )
    residual = sweep / weight_row[None, :] - own_terms - following
    return schur_rows[None], sweep[None], residual[None]


def solution(mesh):
    in_specs = (
        P("tm", "blk", None),
        P("tm", "blk", None),
        P("tm", "blk", None),
        P("tm", "blk", None),
        P("tm", None, "blk"),
        P("tm", "blk"),
    )
    out_specs = (P("tm", "blk", None), P("tm", None, "blk"), P("tm", None, "blk"))
    return jax.shard_map(shards, mesh=mesh, in_specs=in_specs, out_specs=out_specs, check_vma=False)
```

```python
import jax
import jax.numpy as jnp
from jax import lax
from jax.sharding import PartitionSpec as P

AXES = ("tm", "blk")
SIDE = 4
PLANE = SIDE * SIDE


def moved(p, b, along_reduce, step):
    y, x = divmod(b, SIDE)
    if (p % 2 == 0) == along_reduce:
        x ^= step
    else:
        y ^= step
    return y * SIDE + x


def send(value, partitions, shift, along_reduce, step):
    pairs = [
        (p * PLANE + b, (p + shift) * PLANE + moved(p, b, along_reduce, step))
        for p in partitions
        for b in range(PLANE)
    ]
    return lax.ppermute(value, AXES, pairs)


def swap_cores(value, count):
    pairs = [(p * PLANE + b, (p ^ 1) * PLANE + b) for p in range(count) for b in range(PLANE)]
    return lax.ppermute(value, AXES, pairs)


def turn_messages(message, turn, count):
    last = turn - 1
    period = 4 if last % 2 == 0 else 8
    senders = range(last % period, count - 1, period)
    if last % 2 == 0:
        first = swap_cores(message, count)
    else:
        first = send(message, senders, 1, True, 0)
    return [send(message, senders, 1, True, step) for step in (2, 1, 3)] + [first]


def tie(values, *others):
    return lax.optimization_barrier((values, others))[0]


def shards(interior_inverse, coupling, separator, link, source, weights):
    f32, bf16 = jnp.float32, jnp.bfloat16
    count = lax.axis_size("tm")
    everyone = range(count)
    inverse_rows, coupling_rows, separator_rows = interior_inverse[0], coupling[0], separator[0]
    link_rows, source_rows, weight_row = link[0], source[0], weights[0]
    rows, nodes = link_rows.shape
    keys = source_rows.shape[0]
    group = SIDE * rows
    p = lax.axis_index("tm")
    b = lax.axis_index("blk")
    y, x = b // SIDE, b % SIDE
    even = p % 2 == 0
    r = jnp.where(even, x, y)
    q = jnp.where(even, y, x)

    def shard_at(place_q, place_r):
        return jnp.where(even, SIDE * place_q + place_r, SIDE * place_r + place_q)

    def strips(array, shard_indices):
        return jnp.concatenate(
            [lax.dynamic_slice(array, (0, s * rows), (array.shape[0], rows)) for s in shard_indices],
            axis=1,
        )

    def output_columns(array, place_q):
        return strips(array, [shard_at(place_q, j) for j in range(SIDE)])

    def input_columns(array, place_r):
        return strips(array, [shard_at(j, place_r) for j in range(SIDE)])

    def ordered(pieces, place):
        stacked = jnp.stack(pieces)
        return jnp.stack(
            [lax.dynamic_index_in_dim(stacked, place ^ k, 0, keepdims=False) for k in range(SIDE)]
        )

    def gathered(array, along_reduce):
        return [array] + [send(array, everyone, 0, along_reduce, step) for step in (1, 2, 3)]

    high = weight_row.astype(bf16)
    rest = weight_row - high.astype(f32)
    middle = rest.astype(bf16)
    low = (rest - middle.astype(f32)).astype(bf16)
    packed = jnp.zeros((16, group), bf16)
    packed = packed.at[:3, :rows].set(jnp.stack([high, middle, low]))

    def chunk(step):
        return jnp.concatenate([input_columns(link_rows, r ^ step), packed], axis=0)

    pieces = [chunk(0)] + [send(chunk(step), everyone, 0, True, step) for step in (1, 2, 3)]
    pieces = ordered(pieces, r)
    block = pieces[:, :rows].reshape(group, group)
    weight_group = pieces[:, rows : rows + 3, :rows].astype(f32).sum(axis=1).reshape(1, group)
    own = lax.dynamic_update_slice(
        jnp.zeros((keys, group), f32), weight_row[None, :] * source_rows, (0, r * rows)
    )
    block, own, weight_group = tie((block, own, weight_group))

    turned = strips(coupling_rows, [shard_at(q ^ k, j) for k in range(SIDE) for j in range(SIDE)])
    bulk_inverse, bulk_coupling, bulk_turned = tie((inverse_rows, coupling_rows, turned), block)
    inverse_out = gathered(bulk_inverse, True)
    coupling_in = gathered(bulk_coupling, False)
    coupling_out = gathered(bulk_turned, True)

    message = own.astype(bf16)
    final = message
    for turn in range(1, count):
        parts = [part.astype(f32) for part in turn_messages(message, turn, count)]
        previous = (parts[0] + parts[1] + parts[2] + parts[3]).astype(bf16)
        if turn == 5:
            inverse_out, coupling_in = tie((inverse_out, coupling_in), message)
            inner = lax.dot_general(
                jnp.concatenate(inverse_out),
                jnp.concatenate(coupling_in),
                (((1,), (1,)), ((), ())),
                preferred_element_type=f32,
            ).astype(bf16)
            inner = strips(inner, [q ^ k for k in range(SIDE)])
            inner_all = gathered(inner, False)
            previous = tie(previous, inner)
        if turn == 9:
            coupling_out, inner_all = tie((coupling_out, inner_all), message)
            inner_rows = jnp.concatenate(
                [
                    lax.dynamic_slice(piece, ((r ^ j) * rows, 0), (rows, group))
                    for piece in inner_all
                    for j in range(SIDE)
                ]
            )
            folded = jnp.dot(
                jnp.concatenate(coupling_out), inner_rows, preferred_element_type=f32
            ).astype(bf16)
            back_rows = [folded[:rows]] + [
                send(folded[step * rows : (step + 1) * rows], everyone, 0, True, step)
                for step in (1, 2, 3)
            ]
            previous = tie(previous, folded)
        if turn == 12:
            back_rows = tie(back_rows, message)
            placed = ordered(back_rows, r).reshape(SIDE, rows, SIDE, rows)
            product_rows = jnp.where(
                even, placed.transpose(1, 2, 0, 3), placed.transpose(1, 0, 2, 3)
            ).reshape(rows, nodes)
            schur_rows = separator_rows - product_rows.astype(f32)
            columns = strips(
                schur_rows.astype(bf16),
                [shard_at(q ^ k, j) for k in range(SIDE) for j in range(SIDE)],
            )
            previous = tie(previous, schur_rows, columns)
        product = lax.dot_general(
            previous, block, (((1,), (1,)), ((), ())), preferred_element_type=f32
        )
        message = (own - weight_group * product).astype(bf16)
        final = jnp.where(p == turn, message, final)

    total = final.astype(f32)
    for step in (2, 1, 3):
        total = total + send(final, everyone, 0, True, step).astype(f32)
    rounded = total.astype(bf16)
    sweep = lax.dynamic_slice(total, (0, r * rows), (keys, rows))

    back = jnp.dot(rounded, block, preferred_element_type=f32).astype(bf16)
    following = jnp.zeros((keys, rows), f32)
    for step in (2, 1, 3, 0):
        piece = lax.dynamic_slice(back, (0, (q ^ step) * rows), (keys, rows))
        following = following + send(piece, range(1, count), -1, False, step).astype(f32)

    own_terms = jnp.zeros((keys, rows), f32)
    for step, seen in enumerate(gathered(rounded, False)):
        own_terms = own_terms + lax.dot_general(
            seen,
            columns[:, step * group : (step + 1) * group],
            (((1,), (1,)), ((), ())),
            preferred_element_type=f32,
        )
    residual = sweep / weight_row[None, :] - own_terms - following
    return schur_rows[None], sweep[None], residual[None]


def solution(mesh):
    in_specs = (
        P("tm", "blk", None),
        P("tm", "blk", None),
        P("tm", "blk", None),
        P("tm", "blk", None),
        P("tm", None, "blk"),
        P("tm", "blk"),
    )
    out_specs = (P("tm", "blk", None), P("tm", None, "blk"), P("tm", None, "blk"))
    return jax.shard_map(shards, mesh=mesh, in_specs=in_specs, out_specs=out_specs, check_vma=False)
```

```python
import jax
import jax.numpy as jnp
from jax import lax
from jax.experimental import pallas as pl
from jax.experimental.pallas import tpu as pltpu
from jax.sharding import PartitionSpec as P

AXES = ("tm", "blk")
SIDE = 4
PLANE = SIDE * SIDE
PARTITIONS = 16
f32, bf16 = jnp.float32, jnp.bfloat16


def partner(p, y):
    return y ^ 1 if p % 2 == 0 else y ^ 3


def other(p, y):
    return y ^ 3 if p % 2 == 0 else y ^ 1


def permuted(value, rule, partitions=range(PARTITIONS)):
    pairs = []
    for p in partitions:
        for b in range(PLANE):
            target, y, x = rule(p, *divmod(b, SIDE))
            pairs.append((p * PLANE + b, target * PLANE + y * SIDE + x))
    return lax.ppermute(value, AXES, pairs)


def along_x(value, step):
    return permuted(value, lambda p, y, x: (p, y, x ^ step))


def along_y(value, step):
    return permuted(value, lambda p, y, x: (p, y ^ step, x))


def turn_messages(message, last):
    if last % 2 == 0:
        far = permuted(message, lambda p, y, x: (p ^ 1, y ^ 1, x))
        near = permuted(message, lambda p, y, x: (p ^ 1, y, x))
    else:
        far = permuted(message, lambda p, y, x: (p + 1, partner(p, y), x), [last])
        near = permuted(message, lambda p, y, x: (p + 1, y, x), [last])
    return far, near


def tie(values, *others):
    return lax.optimization_barrier((values, others))[0]


def kernel_call(body, place, operands, out_shapes, flops=0):
    out_bytes = sum(s.size * s.dtype.itemsize for s in out_shapes)
    in_bytes = sum(o.size * o.dtype.itemsize for o in operands)
    whole = pl.BlockSpec(memory_space=pltpu.VMEM)
    return pl.pallas_call(
        body,
        out_shape=out_shapes,
        in_specs=[pl.BlockSpec(memory_space=pltpu.SMEM)] + [whole] * len(operands),
        out_specs=[whole] * len(out_shapes),
        compiler_params=pltpu.CompilerParams(vmem_limit_bytes=24 * 1024 * 1024),
        cost_estimate=pl.CostEstimate(
            flops=flops, bytes_accessed=in_bytes + out_bytes, transcendentals=0
        ),
    )(place, *operands)


def block_of(index, size):
    return pl.ds(pl.multiple_of(index * size, size), size)


def split_link(place, link, keep, give):
    size = keep.shape[1] // 2
    for half in range(2):
        keep[:, half * size : (half + 1) * size] = link[:, block_of(place[half], size)]
        give[:, half * size : (half + 1) * size] = link[:, block_of(place[2 + half], size)]


def assemble_link(place, *refs):
    *pieces, out = refs
    size = pieces[0].shape[0] // 2
    for step in range(SIDE):
        for half in range(2):
            out[block_of(half * SIDE + (place[0] ^ step), size), :] = pieces[step][
                half * size : (half + 1) * size, :
            ]


def inner_kernel(place, *refs):
    *pieces, out = refs
    inverse, coupling = pieces[:SIDE], pieces[SIDE:]
    size = inverse[0].shape[0]
    for j in range(SIDE):
        for k in range(SIDE):
            out[block_of(place[0] ^ j, size), block_of(place[1] ^ k, size)] = lax.dot_general(
                inverse[j][...],
                coupling[k][...],
                (((1,), (1,)), ((), ())),
                preferred_element_type=f32,
            ).astype(bf16)


def folded_kernel(place, *refs):
    pieces, outs = refs[: 2 * SIDE], refs[2 * SIDE :]
    coupling, inner = pieces[:SIDE], pieces[SIDE:]
    size = inner[0].shape[0]
    for j in range(SIDE):
        total = jnp.zeros(outs[j].shape, f32)
        for k in range(SIDE):
            total = total + jnp.dot(
                coupling[j][:, block_of(place[1] ^ k, size)],
                inner[k][...],
                preferred_element_type=f32,
            )
        outs[j][...] = total.astype(bf16)


def schur_kernel(place, *refs):
    separator, *pieces, schur, narrow = refs
    size = schur.shape[0]
    for step in range(SIDE):
        for row in range(SIDE):
            columns = block_of(row * SIDE + (place[0] ^ step), size)
            value = separator[:, columns] - pieces[step][:, row * size : (row + 1) * size].astype(f32)
            schur[:, columns] = value
            narrow[:, columns] = value.astype(bf16)


def shards(interior_inverse, coupling, separator, link, source, weights):
    inverse_rows, coupling_rows, separator_rows = interior_inverse[0], coupling[0], separator[0]
    link_rows, source_rows, weight_row = link[0], source[0], weights[0]
    rows, nodes = link_rows.shape
    keys = source_rows.shape[0]
    share = keys // SIDE
    line = SIDE * rows
    half = 2 * line
    shape = jax.ShapeDtypeStruct
    p = lax.axis_index("tm").astype(jnp.int32)
    b = lax.axis_index("blk").astype(jnp.int32)
    y, x = b >> 2, b & 3
    even = (p & 1) == 0
    pair = y >> 1
    ring = ((y + 1) >> 1) & 1
    out_place = jnp.where(even, y & 1, pair)
    in_place = jnp.where(even, pair, y & 1)
    in_low = jnp.where(even, ring, 2 * pair)
    in_high = jnp.where(even, 3 - ring, 2 * pair + 1)
    away_low = jnp.where(even, 1 - ring, 2 - 2 * pair)
    away_high = jnp.where(even, 2 + ring, 3 - 2 * pair)
    place = jnp.stack([x, y])

    def ordered(pieces):
        stacked = jnp.stack(pieces)
        return [
            lax.dynamic_index_in_dim(stacked, x ^ k, 0, keepdims=False) for k in range(SIDE)
        ]

    def spread_x(array):
        return [array] + [along_x(array, step) for step in (1, 2, 3)]

    def exchange_x(chunk):
        return [chunk(0)] + [along_x(chunk(step), step) for step in (1, 2, 3)]

    keep, give = kernel_call(
        split_link,
        jnp.stack([in_low, in_high, away_low, away_high]),
        [link_rows],
        [shape((rows, half), bf16)] * 2,
    )
    got = permuted(give, lambda p, y, x: (p, partner(p, y), x))
    started = weight_row[None, :] * source_rows

    def source_chunk(step):
        part = lax.dynamic_slice(started, ((x ^ step) * share, 0), (share, rows))
        return jnp.concatenate([part, jnp.broadcast_to(weight_row[None, :], (8, rows))], axis=0)

    line_values = jnp.concatenate(ordered(exchange_x(source_chunk)), axis=1)
    line_weights = line_values[share : share + 1]
    away_weights = permuted(line_weights, lambda p, y, x: (p, partner(p, y), x))
    two = jnp.where(
        out_place == 0, jnp.concatenate([keep, got]), jnp.concatenate([got, keep])
    )
    (block,) = kernel_call(
        assemble_link, place, spread_x(two), [shape((half, half), bf16)]
    )
    weight_half = jnp.where(
        out_place == 0,
        jnp.concatenate([line_weights, away_weights], axis=1),
        jnp.concatenate([away_weights, line_weights], axis=1),
    )
    zeros = jnp.zeros((share, line), f32)
    own = jnp.where(
        out_place == 0,
        jnp.concatenate([line_values[:share], zeros], axis=1),
        jnp.concatenate([zeros, line_values[:share]], axis=1),
    )

    coupling_in = [coupling_rows] + [along_y(coupling_rows, step) for step in (1, 2, 3)]
    inverse_out = spread_x(tie(inverse_rows, block))

    message = own.astype(bf16)
    final = message
    for turn in range(1, PARTITIONS):
        far, near = turn_messages(message, turn - 1)
        previous = (far.astype(f32) + near.astype(f32)).astype(bf16)
        if turn == 6:
            inverse_out, coupling_in = tie((inverse_out, coupling_in), message)
            (inner,) = kernel_call(
                inner_kernel,
                place,
                inverse_out + coupling_in,
                [shape((line, line), bf16)],
                flops=2 * line * line * nodes,
            )
            inner_all = [inner] + [along_y(inner, step) for step in (1, 2, 3)]
            coupling_out = spread_x(tie(coupling_rows, inner))
            previous = tie(previous, inner)
        if turn == 12:
            coupling_out, inner_all = tie((coupling_out, inner_all), message)
            folded = kernel_call(
                folded_kernel,
                place,
                coupling_out + inner_all,
                [shape((rows, line), bf16)] * SIDE,
                flops=2 * line * line * nodes,
            )
            back_rows = exchange_x(lambda step: folded[step])
            previous = tie(previous, folded)
        if turn == 14:
            back_rows = tie(back_rows, message)
            schur_rows, narrow = kernel_call(
                schur_kernel,
                place,
                [separator_rows] + back_rows,
                [shape((rows, nodes), f32), shape((rows, nodes), bf16)],
            )
            previous = tie(previous, schur_rows, narrow)
        product = lax.dot_general(
            previous, block, (((1,), (1,)), ((), ())), preferred_element_type=f32
        )
        message = (own - weight_half * product).astype(bf16)
        final = jnp.where(p == turn, message, final)

    total = final.astype(f32) + permuted(
        final, lambda p, y, x: (p, partner(p, y), x)
    ).astype(f32)
    rounded = total.astype(bf16)

    back = jnp.dot(rounded, block, preferred_element_type=f32).astype(bf16)
    mine = lax.dynamic_slice(back, (0, in_place * line), (share, line))
    theirs = lax.dynamic_slice(back, (0, (1 - in_place) * line), (share, line))
    later = range(1, PARTITIONS)
    following_line = permuted(
        theirs, lambda p, y, x: (p - 1, other(p, y), x), later
    ).astype(f32) + permuted(mine, lambda p, y, x: (p - 1, y, x), later).astype(f32)

    def own_shard(line_array):
        pieces = exchange_x(
            lambda step: lax.dynamic_slice(line_array, (0, (x ^ step) * rows), (share, rows))
        )
        return jnp.concatenate(ordered(pieces), axis=0)

    rest = permuted(rounded, lambda p, y, x: (p, other(p, y), x))
    m0, m1, r0, r1 = rounded[:, :line], rounded[:, line:], rest[:, :line], rest[:, line:]
    lines = jnp.where(
        even,
        jnp.where(
            pair == 0,
            jnp.concatenate([m0, m1, r0, r1], axis=1),
            jnp.concatenate([r0, r1, m0, m1], axis=1),
        ),
        jnp.where(
            ring == 0,
            jnp.concatenate([m0, r0, r1, m1], axis=1),
            jnp.concatenate([r0, m0, m1, r1], axis=1),
        ),
    )
    terms = lax.dot_general(
        jnp.concatenate(spread_x(lines)),
        narrow,
        (((1,), (1,)), ((), ())),
        preferred_element_type=f32,
    ).reshape(SIDE, share, rows)
    own_terms = jnp.concatenate(ordered([terms[step] for step in range(SIDE)]), axis=0)
    sweep = own_shard(lax.dynamic_slice(total, (0, out_place * line), (share, line)))
    following = own_shard(following_line)
    residual = sweep / weight_row[None, :] - own_terms - following
    return schur_rows[None], sweep[None], residual[None]


def solution(mesh):
    in_specs = (
        P("tm", "blk", None),
        P("tm", "blk", None),
        P("tm", "blk", None),
        P("tm", "blk", None),
        P("tm", None, "blk"),
        P("tm", "blk"),
    )
    out_specs = (P("tm", "blk", None), P("tm", None, "blk"), P("tm", None, "blk"))
    return jax.shard_map(shards, mesh=mesh, in_specs=in_specs, out_specs=out_specs, check_vma=False)
```

```python
import jax
import jax.numpy as jnp
from jax import lax
from jax.experimental import pallas as pl
from jax.experimental.pallas import tpu as pltpu
from jax.sharding import PartitionSpec as P

AXES = ("tm", "blk")
SIDE = 4
PLANE = SIDE * SIDE
PARTITIONS = 16
f32, bf16 = jnp.float32, jnp.bfloat16


def partner(p, y):
    return y ^ 1 if p % 2 == 0 else y ^ 3


def other(p, y):
    return y ^ 3 if p % 2 == 0 else y ^ 1


def permuted(value, rule, partitions=range(PARTITIONS)):
    pairs = []
    for p in partitions:
        for b in range(PLANE):
            target, y, x = rule(p, *divmod(b, SIDE))
            pairs.append((p * PLANE + b, target * PLANE + y * SIDE + x))
    return lax.ppermute(value, AXES, pairs)


def along_x(value, step):
    return permuted(value, lambda p, y, x: (p, y, x ^ step))


def along_y(value, step):
    return permuted(value, lambda p, y, x: (p, y ^ step, x))


def turn_messages(message, last):
    if last % 2 == 0:
        far = permuted(message, lambda p, y, x: (p ^ 1, y ^ 1, x))
        near = permuted(message, lambda p, y, x: (p ^ 1, y, x))
    else:
        far = permuted(message, lambda p, y, x: (p + 1, partner(p, y), x), [last])
        near = permuted(message, lambda p, y, x: (p + 1, y, x), [last])
    return far, near


def tie(values, *others):
    return lax.optimization_barrier((values, others))[0]


def kernel_call(body, place, operands, out_shapes, flops=0):
    out_bytes = sum(s.size * s.dtype.itemsize for s in out_shapes)
    in_bytes = sum(o.size * o.dtype.itemsize for o in operands)
    whole = pl.BlockSpec(memory_space=pltpu.VMEM)
    return pl.pallas_call(
        body,
        out_shape=out_shapes,
        in_specs=[pl.BlockSpec(memory_space=pltpu.SMEM)] + [whole] * len(operands),
        out_specs=[whole] * len(out_shapes),
        compiler_params=pltpu.CompilerParams(vmem_limit_bytes=24 * 1024 * 1024),
        cost_estimate=pl.CostEstimate(
            flops=flops, bytes_accessed=in_bytes + out_bytes, transcendentals=0
        ),
    )(place, *operands)


def block_of(index, size):
    return pl.ds(pl.multiple_of(index * size, size), size)


def split_link(place, link, keep, give):
    size = keep.shape[1] // 2
    for half in range(2):
        keep[:, half * size : (half + 1) * size] = link[:, block_of(place[half], size)]
        give[:, half * size : (half + 1) * size] = link[:, block_of(place[2 + half], size)]


def assemble_link(place, *refs):
    *pieces, out = refs
    size = pieces[0].shape[0] // 2
    for step in range(SIDE):
        for half in range(2):
            out[block_of(half * SIDE + (place[0] ^ step), size), :] = pieces[step][
                half * size : (half + 1) * size, :
            ]


def schur_kernel(place, *refs):
    separator, *pieces, schur, narrow = refs
    size = schur.shape[0]
    for step in range(SIDE):
        for k in range(SIDE):
            columns = block_of(k * place[1] + (place[0] ^ step) * place[2], size)
            value = separator[:, columns] - pieces[step][:, k * size : (k + 1) * size].astype(f32)
            schur[:, columns] = value
            narrow[:, columns] = value.astype(bf16)


def finish_kernel(place, narrow, weight, *refs):
    *pieces, sweep, residual = refs
    rows, nodes = narrow.shape
    share = pieces[0].shape[0]
    iterate = jnp.concatenate([piece[:, :nodes] for piece in pieces], axis=0)
    terms = lax.dot_general(
        iterate, narrow[...], (((1,), (1,)), ((), ())), preferred_element_type=f32
    )
    for step in range(SIDE):
        extra = [
            pieces[step][:, nodes + k * rows : nodes + (k + 1) * rows].astype(f32) for k in range(3)
        ]
        value = extra[1] + extra[2]
        target = block_of(place[0] ^ step, share)
        sweep[target, :] = value
        residual[target, :] = (
            value / weight[...] - terms[step * share : (step + 1) * share] - extra[0]
        )


def gather_groups(along_reduce):
    groups = []
    for p in range(PARTITIONS):
        for k in range(SIDE):
            if (p % 2 == 0) == along_reduce:
                groups.append([p * PLANE + k * SIDE + x for x in range(SIDE)])
            else:
                groups.append([p * PLANE + y * SIDE + k for y in range(SIDE)])
    return groups


def gathered(array, along_reduce):
    return lax.all_gather(
        array, AXES, axis=0, tiled=True, axis_index_groups=gather_groups(along_reduce)
    )


def along_reduce(value, step):
    return permuted(
        value, lambda p, y, x: (p, y, x ^ step) if p % 2 == 0 else (p, y ^ step, x)
    )


def shards(interior_inverse, coupling, separator, link, source, weights):
    inverse_rows, coupling_rows, separator_rows = interior_inverse[0], coupling[0], separator[0]
    link_rows, source_rows, weight_row = link[0], source[0], weights[0]
    rows, nodes = link_rows.shape
    keys = source_rows.shape[0]
    share = keys // SIDE
    line = SIDE * rows
    half = 2 * line
    shape = jax.ShapeDtypeStruct
    p = lax.axis_index("tm").astype(jnp.int32)
    b = lax.axis_index("blk").astype(jnp.int32)
    y, x = b >> 2, b & 3
    even = (p & 1) == 0
    r = jnp.where(even, x, y)
    pair = y >> 1
    ring = ((y + 1) >> 1) & 1
    out_place = jnp.where(even, y & 1, pair)
    in_place = jnp.where(even, pair, y & 1)
    in_low = jnp.where(even, ring, 2 * pair)
    in_high = jnp.where(even, 3 - ring, 2 * pair + 1)
    away_low = jnp.where(even, 1 - ring, 2 - 2 * pair)
    away_high = jnp.where(even, 2 + ring, 3 - 2 * pair)
    place = jnp.stack([x, y])

    coupling_in = gathered(coupling_rows, False)
    inverse_out = gathered(inverse_rows, True)
    turned = jnp.where(
        even,
        coupling_rows,
        coupling_rows.reshape(rows, SIDE, SIDE, rows).transpose(0, 2, 1, 3).reshape(rows, nodes),
    )
    coupling_out = gathered(turned, True)

    def ordered(pieces):
        stacked = jnp.stack(pieces)
        return [
            lax.dynamic_index_in_dim(stacked, x ^ k, 0, keepdims=False) for k in range(SIDE)
        ]

    def spread_x(array):
        return [array] + [along_x(array, step) for step in (1, 2, 3)]

    def exchange_x(chunk):
        return [chunk(0)] + [along_x(chunk(step), step) for step in (1, 2, 3)]

    keep, give = kernel_call(
        split_link,
        jnp.stack([in_low, in_high, away_low, away_high]),
        [link_rows],
        [shape((rows, half), bf16)] * 2,
    )
    got = permuted(give, lambda p, y, x: (p, partner(p, y), x))
    two = jnp.where(
        out_place == 0, jnp.concatenate([keep, got]), jnp.concatenate([got, keep])
    )
    pieces = spread_x(two)
    source_rows, weight_row = tie((source_rows, weight_row), two)
    started = weight_row[None, :] * source_rows

    def source_chunk(step):
        part = lax.dynamic_slice(started, ((x ^ step) * share, 0), (share, rows))
        return jnp.concatenate([part, jnp.broadcast_to(weight_row[None, :], (8, rows))], axis=0)

    line_values = jnp.concatenate(ordered(exchange_x(source_chunk)), axis=1)
    line_weights = line_values[share : share + 1]
    away_weights = permuted(line_weights, lambda p, y, x: (p, partner(p, y), x))
    (block,) = kernel_call(assemble_link, place, pieces, [shape((half, half), bf16)])
    weight_half = jnp.where(
        out_place == 0,
        jnp.concatenate([line_weights, away_weights], axis=1),
        jnp.concatenate([away_weights, line_weights], axis=1),
    )
    zeros = jnp.zeros((share, line), f32)
    own = jnp.where(
        out_place == 0,
        jnp.concatenate([line_values[:share], zeros], axis=1),
        jnp.concatenate([zeros, line_values[:share]], axis=1),
    )

    message = own.astype(bf16)
    final = message
    for turn in range(1, PARTITIONS):
        far, near = turn_messages(message, turn - 1)
        previous = (far.astype(f32) + near.astype(f32)).astype(bf16)
        if turn == 8:
            inverse_out, coupling_in = tie((inverse_out, coupling_in), message)
            inner = lax.dot_general(
                inverse_out, coupling_in, (((1,), (1,)), ((), ())), preferred_element_type=f32
            ).astype(bf16)
            inner_all = gathered(inner, False)
            previous = tie(previous, inner)
        product = lax.dot_general(
            previous, block, (((1,), (1,)), ((), ())), preferred_element_type=f32
        )
        message = (own - weight_half * product).astype(bf16)
        final = jnp.where(p == turn, message, final)

    total = final.astype(f32) + permuted(
        final, lambda p, y, x: (p, partner(p, y), x)
    ).astype(f32)
    rounded = total.astype(bf16)

    back = jnp.dot(rounded, block, preferred_element_type=f32).astype(bf16)
    mine = lax.dynamic_slice(back, (0, in_place * line), (share, line))
    theirs = lax.dynamic_slice(back, (0, (1 - in_place) * line), (share, line))
    later = range(1, PARTITIONS)
    following = permuted(
        theirs, lambda p, y, x: (p - 1, other(p, y), x), later
    ).astype(f32) + permuted(mine, lambda p, y, x: (p - 1, y, x), later).astype(f32)
    following = following.astype(bf16)

    rest = permuted(rounded, lambda p, y, x: (p, other(p, y), x))
    m0, m1, r0, r1 = rounded[:, :line], rounded[:, line:], rest[:, :line], rest[:, line:]
    lines = jnp.where(
        even,
        jnp.where(
            pair == 0,
            jnp.concatenate([m0, m1, r0, r1], axis=1),
            jnp.concatenate([r0, r1, m0, m1], axis=1),
        ),
        jnp.where(
            ring == 0,
            jnp.concatenate([m0, r0, r1, m1], axis=1),
            jnp.concatenate([r0, m0, m1, r1], axis=1),
        ),
    )
    sweep_line = lax.dynamic_slice(total, (0, out_place * line), (share, line))
    sweep_high = sweep_line.astype(bf16)
    sweep_low = (sweep_line - sweep_high.astype(f32)).astype(bf16)

    def last_chunk(step):
        start = (0, (x ^ step) * rows)
        extra = [
            lax.dynamic_slice(array, start, (share, rows))
            for array in (following, sweep_high, sweep_low)
        ]
        return jnp.concatenate([lines] + extra, axis=1)

    last = exchange_x(last_chunk)

    coupling_out, inner_all = tie((coupling_out, inner_all), lines)
    folded = jnp.dot(coupling_out, inner_all, preferred_element_type=f32).astype(bf16)

    def folded_chunk(step):
        return lax.dynamic_slice(folded, ((r ^ step) * rows, 0), (rows, line))

    back_rows = [folded_chunk(0)] + [along_reduce(folded_chunk(s), s) for s in (1, 2, 3)]
    schur_rows, narrow = kernel_call(
        schur_kernel,
        jnp.stack([r, jnp.where(even, SIDE, 1), jnp.where(even, 1, SIDE)]),
        [separator_rows] + back_rows,
        [shape((rows, nodes), f32), shape((rows, nodes), bf16)],
    )
    sweep, residual = kernel_call(
        finish_kernel,
        place,
        [narrow, weight_row[None, :]] + last,
        [shape((keys, rows), f32)] * 2,
        flops=2 * keys * rows * nodes,
    )
    return schur_rows[None], sweep[None], residual[None]


def solution(mesh):
    in_specs = (
        P("tm", "blk", None),
        P("tm", "blk", None),
        P("tm", "blk", None),
        P("tm", "blk", None),
        P("tm", None, "blk"),
        P("tm", "blk"),
    )
    out_specs = (P("tm", "blk", None), P("tm", None, "blk"), P("tm", None, "blk"))
    return jax.shard_map(shards, mesh=mesh, in_specs=in_specs, out_specs=out_specs, check_vma=False)
```

```python
import jax
import jax.numpy as jnp
from jax import lax
from jax.experimental import pallas as pl
from jax.experimental.pallas import tpu as pltpu
from jax.sharding import PartitionSpec as P

AXES = ("tm", "blk")
SIDE = 4
PLANE = SIDE * SIDE
PARTITIONS = 16
f32, bf16 = jnp.float32, jnp.bfloat16


def partner(p, y):
    return y ^ 1 if p % 2 == 0 else y ^ 3


def other(p, y):
    return y ^ 3 if p % 2 == 0 else y ^ 1


def permuted(value, rule, partitions=range(PARTITIONS)):
    pairs = []
    for p in partitions:
        for b in range(PLANE):
            target, y, x = rule(p, *divmod(b, SIDE))
            pairs.append((p * PLANE + b, target * PLANE + y * SIDE + x))
    return lax.ppermute(value, AXES, pairs)


def along_x(value, step):
    return permuted(value, lambda p, y, x: (p, y, x ^ step))


def along_y(value, step):
    return permuted(value, lambda p, y, x: (p, y ^ step, x))


def turn_messages(message, last):
    if last % 2 == 0:
        far = permuted(message, lambda p, y, x: (p ^ 1, y ^ 1, x))
        near = permuted(message, lambda p, y, x: (p ^ 1, y, x))
    else:
        far = permuted(message, lambda p, y, x: (p + 1, partner(p, y), x), [last])
        near = permuted(message, lambda p, y, x: (p + 1, y, x), [last])
    return far, near


def tie(values, *others):
    return lax.optimization_barrier((values, others))[0]


def kernel_call(body, place, operands, out_shapes, flops=0, scratch=()):
    out_bytes = sum(s.size * s.dtype.itemsize for s in out_shapes)
    in_bytes = sum(o.size * o.dtype.itemsize for o in operands)
    whole = pl.BlockSpec(memory_space=pltpu.VMEM)
    return pl.pallas_call(
        body,
        out_shape=out_shapes,
        in_specs=[pl.BlockSpec(memory_space=pltpu.SMEM)] + [whole] * len(operands),
        out_specs=[whole] * len(out_shapes),
        scratch_shapes=scratch,
        compiler_params=pltpu.CompilerParams(vmem_limit_bytes=24 * 1024 * 1024),
        cost_estimate=pl.CostEstimate(
            flops=flops, bytes_accessed=in_bytes + out_bytes, transcendentals=0
        ),
    )(place, *operands)


def block_of(index, size):
    return pl.ds(pl.multiple_of(index * size, size), size)


def split_link(place, link, keep, give):
    size = keep.shape[1] // 2
    for half in range(2):
        keep[:, half * size : (half + 1) * size] = link[:, block_of(place[half], size)]
        give[:, half * size : (half + 1) * size] = link[:, block_of(place[2 + half], size)]


def assemble_link(place, *refs):
    *pieces, out = refs
    size = pieces[0].shape[0] // 2
    for step in range(SIDE):
        for half in range(2):
            out[block_of(half * SIDE + (place[0] ^ step), size), :] = pieces[step][
                half * size : (half + 1) * size, :
            ]


def schur_kernel(place, *refs):
    separator, *pieces, schur, narrow = refs
    size = schur.shape[0]
    for step in range(SIDE):
        for k in range(SIDE):
            columns = block_of(k * place[1] + (place[0] ^ step) * place[2], size)
            value = separator[:, columns] - pieces[step][:, k * size : (k + 1) * size].astype(f32)
            schur[:, columns] = value
            narrow[:, columns] = value.astype(bf16)


def finish_kernel(place, narrow, weight, *refs):
    *pieces, sweep, residual = refs
    rows, nodes = narrow.shape
    share = pieces[0].shape[0]
    iterate = jnp.concatenate([piece[:, :nodes] for piece in pieces], axis=0)
    terms = lax.dot_general(
        iterate, narrow[...], (((1,), (1,)), ((), ())), preferred_element_type=f32
    )
    for step in range(SIDE):
        extra = [
            pieces[step][:, nodes + k * rows : nodes + (k + 1) * rows].astype(f32) for k in range(3)
        ]
        value = extra[1] + extra[2]
        target = block_of(place[0] ^ step, share)
        sweep[target, :] = value
        residual[target, :] = (
            value / weight[...] - terms[step * share : (step + 1) * share] - extra[0]
        )


def inner_kernel(place, first, second, out):
    def multiply(left, right):
        out[...] = lax.dot_general(
            left[...], right[...], (((1,), (1,)), ((), ())), preferred_element_type=f32
        ).astype(bf16)

    pl.when(place[0] == 1)(lambda: multiply(second, first))
    pl.when(place[0] == 0)(lambda: multiply(first, second))


def folded_kernel(place, coupling, *refs):
    early, late, inner, outs, turned = refs[:3], refs[3:6], refs[6], refs[7:11], refs[11]
    size = coupling.shape[0]
    for j, step in enumerate((0, 1, 3, 2)):
        for k in range(SIDE * SIDE):
            columns = block_of((k // SIDE) * place[0] + (k % SIDE) * place[1], size)
            if step == 0:
                value = coupling[:, columns]
            else:
                value = early[j - 1][:, columns] + late[j - 1][:, columns]
            turned[:, k * size : (k + 1) * size] = value
        outs[step][...] = jnp.dot(
            turned[...], inner[...], preferred_element_type=f32
        ).astype(bf16)


def over_axis(array, axis):
    if axis == "x":
        groups = [[k * SIDE + i for i in range(SIDE)] for k in range(SIDE)]
    else:
        groups = [[i * SIDE + k for i in range(SIDE)] for k in range(SIDE)]
    return lax.all_gather(array, "blk", axis=0, tiled=True, axis_index_groups=groups)


def over_other(array):
    groups = []
    for p in range(PARTITIONS):
        for k in range(SIDE):
            if p % 2 == 0:
                groups.append([p * PLANE + i * SIDE + k for i in range(SIDE)])
            else:
                groups.append([p * PLANE + k * SIDE + i for i in range(SIDE)])
    return lax.all_gather(array, AXES, axis=0, tiled=True, axis_index_groups=groups)


def along_reduce(value, step, partitions=range(PARTITIONS)):
    return permuted(
        value, lambda p, y, x: (p, y, x ^ step) if p % 2 == 0 else (p, y ^ step, x), partitions
    )


def shards(interior_inverse, coupling, separator, link, source, weights):
    inverse_rows, coupling_rows, separator_rows = interior_inverse[0], coupling[0], separator[0]
    link_rows, source_rows, weight_row = link[0], source[0], weights[0]
    rows, nodes = link_rows.shape
    keys = source_rows.shape[0]
    share = keys // SIDE
    line = SIDE * rows
    half = 2 * line
    shape = jax.ShapeDtypeStruct
    p = lax.axis_index("tm").astype(jnp.int32)
    b = lax.axis_index("blk").astype(jnp.int32)
    y, x = b >> 2, b & 3
    even = (p & 1) == 0
    r = jnp.where(even, x, y)
    pair = y >> 1
    ring = ((y + 1) >> 1) & 1
    out_place = jnp.where(even, y & 1, pair)
    in_place = jnp.where(even, pair, y & 1)
    in_low = jnp.where(even, ring, 2 * pair)
    in_high = jnp.where(even, 3 - ring, 2 * pair + 1)
    away_low = jnp.where(even, 1 - ring, 2 - 2 * pair)
    away_high = jnp.where(even, 2 + ring, 3 - 2 * pair)
    place = jnp.stack([x, y])

    first = over_axis(jnp.where(even, coupling_rows, inverse_rows), "y")
    second = over_axis(jnp.where(even, inverse_rows, coupling_rows), "x")
    early, late = range(PARTITIONS // 2, PARTITIONS), range(PARTITIONS // 2)

    def ordered(pieces):
        stacked = jnp.stack(pieces)
        return [
            lax.dynamic_index_in_dim(stacked, x ^ k, 0, keepdims=False) for k in range(SIDE)
        ]

    def spread_x(array):
        return [array] + [along_x(array, step) for step in (1, 2, 3)]

    def exchange_x(chunk):
        return [chunk(0)] + [along_x(chunk(step), step) for step in (1, 2, 3)]

    keep, give = kernel_call(
        split_link,
        jnp.stack([in_low, in_high, away_low, away_high]),
        [link_rows],
        [shape((rows, half), bf16)] * 2,
    )
    got = permuted(give, lambda p, y, x: (p, partner(p, y), x))
    two = jnp.where(
        out_place == 0, jnp.concatenate([keep, got]), jnp.concatenate([got, keep])
    )
    pieces = [two] + [
        permuted(two, lambda p, y, x: (p, y, x ^ step), range(1, PARTITIONS)) for step in (1, 2, 3)
    ]
    early_rows = tie(coupling_rows, two)
    early_pieces = [along_reduce(early_rows, 1, early), along_reduce(early_rows, 3, early)]
    source_rows, weight_row = tie((source_rows, weight_row), two)
    started = weight_row[None, :] * source_rows

    def source_chunk(step):
        part = lax.dynamic_slice(started, ((x ^ step) * share, 0), (share, rows))
        return jnp.concatenate([part, jnp.broadcast_to(weight_row[None, :], (8, rows))], axis=0)

    line_values = jnp.concatenate(ordered(exchange_x(source_chunk)), axis=1)
    line_weights = line_values[share : share + 1]
    away_weights = permuted(line_weights, lambda p, y, x: (p, partner(p, y), x))
    (block,) = kernel_call(assemble_link, place, pieces, [shape((half, half), bf16)])
    weight_half = jnp.where(
        out_place == 0,
        jnp.concatenate([line_weights, away_weights], axis=1),
        jnp.concatenate([away_weights, line_weights], axis=1),
    )
    zeros = jnp.zeros((share, line), f32)
    own = jnp.where(
        out_place == 0,
        jnp.concatenate([line_values[:share], zeros], axis=1),
        jnp.concatenate([zeros, line_values[:share]], axis=1),
    )

    message = own.astype(bf16)
    final = message
    for turn in range(1, PARTITIONS):
        far, near = turn_messages(message, turn - 1)
        previous = (far.astype(f32) + near.astype(f32)).astype(bf16)
        if turn == 3:
            early_pieces.append(along_reduce(early_pieces[0], 3, early))
            previous = tie(previous, early_pieces[:2])
        if turn == 7:
            previous = tie(previous, early_pieces[2])
        if turn == 9:
            late_rows = tie(coupling_rows, message)
            late_pieces = [along_reduce(late_rows, 1, late), along_reduce(late_rows, 3, late)]
        if turn == 12:
            late_pieces.append(along_reduce(late_pieces[0], 3, late))
            previous = tie(previous, late_pieces[:2])
        if turn == 10:
            first, second = tie((first, second), message)
            (inner,) = kernel_call(
                inner_kernel,
                jnp.stack([even.astype(jnp.int32)]),
                [first, second],
                [shape((line, line), bf16)],
                flops=2 * line * line * nodes,
            )
            inner_all = over_other(inner)
            previous = tie(previous, inner)
        product = lax.dot_general(
            previous, block, (((1,), (1,)), ((), ())), preferred_element_type=f32
        )
        message = (own - weight_half * product).astype(bf16)
        final = jnp.where(p == turn, message, final)

    total = final.astype(f32) + permuted(
        final, lambda p, y, x: (p, partner(p, y), x)
    ).astype(f32)
    rounded = total.astype(bf16)

    back = jnp.dot(rounded, block, preferred_element_type=f32).astype(bf16)
    mine = lax.dynamic_slice(back, (0, in_place * line), (share, line))
    theirs = lax.dynamic_slice(back, (0, (1 - in_place) * line), (share, line))
    later = range(1, PARTITIONS)
    following = permuted(
        theirs, lambda p, y, x: (p - 1, other(p, y), x), later
    ).astype(f32) + permuted(mine, lambda p, y, x: (p - 1, y, x), later).astype(f32)
    following = following.astype(bf16)

    rest = permuted(rounded, lambda p, y, x: (p, other(p, y), x))
    m0, m1, r0, r1 = rounded[:, :line], rounded[:, line:], rest[:, :line], rest[:, line:]
    lines = jnp.where(
        even,
        jnp.where(
            pair == 0,
            jnp.concatenate([m0, m1, r0, r1], axis=1),
            jnp.concatenate([r0, r1, m0, m1], axis=1),
        ),
        jnp.where(
            ring == 0,
            jnp.concatenate([m0, r0, r1, m1], axis=1),
            jnp.concatenate([r0, m0, m1, r1], axis=1),
        ),
    )
    sweep_line = lax.dynamic_slice(total, (0, out_place * line), (share, line))
    sweep_high = sweep_line.astype(bf16)
    sweep_low = (sweep_line - sweep_high.astype(f32)).astype(bf16)

    def last_chunk(step):
        start = (0, (x ^ step) * rows)
        extra = [
            lax.dynamic_slice(array, start, (share, rows))
            for array in (following, sweep_high, sweep_low)
        ]
        return jnp.concatenate([lines] + extra, axis=1)

    last = exchange_x(last_chunk)

    inner_all = tie(inner_all, rounded)
    strides = [jnp.where(even, SIDE, 1), jnp.where(even, 1, SIDE)]
    folded = kernel_call(
        folded_kernel,
        jnp.stack(strides),
        [coupling_rows] + early_pieces + late_pieces + [inner_all],
        [shape((rows, line), bf16)] * SIDE,
        flops=2 * line * line * nodes,
        scratch=[pltpu.VMEM((rows, nodes), bf16)],
    )
    back_rows = [folded[0]] + [along_reduce(folded[step], step) for step in (1, 2, 3)]
    schur_rows, narrow = kernel_call(
        schur_kernel,
        jnp.stack([r] + strides),
        [separator_rows] + back_rows,
        [shape((rows, nodes), f32), shape((rows, nodes), bf16)],
    )
    sweep, residual = kernel_call(
        finish_kernel,
        place,
        [narrow, weight_row[None, :]] + last,
        [shape((keys, rows), f32)] * 2,
        flops=2 * keys * rows * nodes,
    )
    return schur_rows[None], sweep[None], residual[None]


def solution(mesh):
    in_specs = (
        P("tm", "blk", None),
        P("tm", "blk", None),
        P("tm", "blk", None),
        P("tm", "blk", None),
        P("tm", None, "blk"),
        P("tm", "blk"),
    )
    out_specs = (P("tm", "blk", None), P("tm", None, "blk"), P("tm", None, "blk"))
    return jax.shard_map(shards, mesh=mesh, in_specs=in_specs, out_specs=out_specs, check_vma=False)
```

```python
import jax
import jax.numpy as jnp
from jax import lax
from jax.experimental import pallas as pl
from jax.experimental.pallas import tpu as pltpu
from jax.sharding import PartitionSpec as P

AXES = ("tm", "blk")
SIDE = 4
PLANE = SIDE * SIDE
PARTITIONS = 16
f32, bf16 = jnp.float32, jnp.bfloat16


def partner(p, y):
    return y ^ 1 if p % 2 == 0 else y ^ 3


def other(p, y):
    return y ^ 3 if p % 2 == 0 else y ^ 1


def permuted(value, rule, partitions=range(PARTITIONS)):
    pairs = []
    for p in partitions:
        for b in range(PLANE):
            target, y, x = rule(p, *divmod(b, SIDE))
            pairs.append((p * PLANE + b, target * PLANE + y * SIDE + x))
    return lax.ppermute(value, AXES, pairs)


def along_x(value, step):
    return permuted(value, lambda p, y, x: (p, y, x ^ step))


def along_y(value, step):
    return permuted(value, lambda p, y, x: (p, y ^ step, x))


def turn_messages(message, last):
    if last % 2 == 0:
        far = permuted(message, lambda p, y, x: (p ^ 1, y ^ 1, x))
        near = permuted(message, lambda p, y, x: (p ^ 1, y, x))
    else:
        far = permuted(message, lambda p, y, x: (p + 1, partner(p, y), x), [last])
        near = permuted(message, lambda p, y, x: (p + 1, y, x), [last])
    return far, near


def tie(values, *others):
    return lax.optimization_barrier((values, others))[0]


def kernel_call(body, place, operands, out_shapes, flops=0):
    out_bytes = sum(s.size * s.dtype.itemsize for s in out_shapes)
    in_bytes = sum(o.size * o.dtype.itemsize for o in operands)
    whole = pl.BlockSpec(memory_space=pltpu.VMEM)
    return pl.pallas_call(
        body,
        out_shape=out_shapes,
        in_specs=[pl.BlockSpec(memory_space=pltpu.SMEM)] + [whole] * len(operands),
        out_specs=[whole] * len(out_shapes),
        compiler_params=pltpu.CompilerParams(vmem_limit_bytes=24 * 1024 * 1024),
        cost_estimate=pl.CostEstimate(
            flops=flops, bytes_accessed=in_bytes + out_bytes, transcendentals=0
        ),
    )(place, *operands)


def block_of(index, size):
    return pl.ds(pl.multiple_of(index * size, size), size)


def split_link(place, link, keep, give):
    size = keep.shape[1] // 2
    for half in range(2):
        keep[:, half * size : (half + 1) * size] = link[:, block_of(place[half], size)]
        give[:, half * size : (half + 1) * size] = link[:, block_of(place[2 + half], size)]


def assemble_link(place, *refs):
    *pieces, out = refs
    size = pieces[0].shape[0] // 2
    for step in range(SIDE):
        for half in range(2):
            out[block_of(half * SIDE + (place[0] ^ step), size), :] = pieces[step][
                half * size : (half + 1) * size, :
            ]


def schur_kernel(place, *refs):
    separator, *pieces, schur, narrow = refs
    size = schur.shape[0]
    for step in range(SIDE):
        for k in range(SIDE):
            columns = block_of(k * place[1] + (place[0] ^ step) * place[2], size)
            value = separator[:, columns] - pieces[step][:, k * size : (k + 1) * size].astype(f32)
            schur[:, columns] = value
            narrow[:, columns] = value.astype(bf16)


def finish_kernel(place, narrow, weight, *refs):
    *pieces, sweep, residual = refs
    rows, nodes = narrow.shape
    share = pieces[0].shape[0]
    iterate = jnp.concatenate([piece[:, :nodes] for piece in pieces], axis=0)
    terms = lax.dot_general(
        iterate, narrow[...], (((1,), (1,)), ((), ())), preferred_element_type=f32
    )
    for step in range(SIDE):
        extra = [
            pieces[step][:, nodes + k * rows : nodes + (k + 1) * rows].astype(f32) for k in range(3)
        ]
        value = extra[1] + extra[2]
        target = block_of(place[0] ^ step, share)
        sweep[target, :] = value
        residual[target, :] = (
            value / weight[...] - terms[step * share : (step + 1) * share] - extra[0]
        )


def inner_kernel(place, second, right, *refs):
    *left, out = refs
    size, cut = left[0].shape

    def dot(a, b):
        return lax.dot_general(a, b, (((1,), (1,)), ((), ())), preferred_element_type=f32)

    for step in range(SIDE):
        target = block_of(place[1] ^ step, size)

        def by_rows(step=step, target=target):
            value = dot(left[step][...], second[:, :cut]) + dot(right[target, :], second[:, cut:])
            out[target, :] = value.astype(bf16)

        def by_columns(step=step, target=target):
            value = dot(second[:, :cut], left[step][...]) + dot(second[:, cut:], right[target, :])
            out[:, target] = value.astype(bf16)

        pl.when(place[0] == 1)(by_columns)
        pl.when(place[0] == 0)(by_rows)


def over_axis(array, axis):
    if axis == "x":
        groups = [[k * SIDE + i for i in range(SIDE)] for k in range(SIDE)]
    else:
        groups = [[i * SIDE + k for i in range(SIDE)] for k in range(SIDE)]
    return lax.all_gather(array, "blk", axis=0, tiled=True, axis_index_groups=groups)


def over_parity(array, reduce_axis):
    groups = []
    for p in range(PARTITIONS):
        for k in range(SIDE):
            if (p % 2 == 0) == reduce_axis:
                groups.append([p * PLANE + k * SIDE + i for i in range(SIDE)])
            else:
                groups.append([p * PLANE + i * SIDE + k for i in range(SIDE)])
    return lax.all_gather(array, AXES, axis=0, tiled=True, axis_index_groups=groups)


def along_reduce(value, step):
    return permuted(
        value, lambda p, y, x: (p, y, x ^ step) if p % 2 == 0 else (p, y ^ step, x)
    )


def shards(interior_inverse, coupling, separator, link, source, weights):
    inverse_rows, coupling_rows, separator_rows = interior_inverse[0], coupling[0], separator[0]
    link_rows, source_rows, weight_row = link[0], source[0], weights[0]
    rows, nodes = link_rows.shape
    keys = source_rows.shape[0]
    share = keys // SIDE
    line = SIDE * rows
    half = 2 * line
    shape = jax.ShapeDtypeStruct
    p = lax.axis_index("tm").astype(jnp.int32)
    b = lax.axis_index("blk").astype(jnp.int32)
    y, x = b >> 2, b & 3
    even = (p & 1) == 0
    r = jnp.where(even, x, y)
    pair = y >> 1
    ring = ((y + 1) >> 1) & 1
    out_place = jnp.where(even, y & 1, pair)
    in_place = jnp.where(even, pair, y & 1)
    in_low = jnp.where(even, ring, 2 * pair)
    in_high = jnp.where(even, 3 - ring, 2 * pair + 1)
    away_low = jnp.where(even, 1 - ring, 2 - 2 * pair)
    away_high = jnp.where(even, 2 + ring, 3 - 2 * pair)
    place = jnp.stack([x, y])

    first = jnp.where(even, coupling_rows, inverse_rows)
    second = jnp.where(even, inverse_rows, coupling_rows)
    first_right = over_axis(first[:, nodes // 2 :], "y")

    def ordered(pieces):
        stacked = jnp.stack(pieces)
        return [
            lax.dynamic_index_in_dim(stacked, x ^ k, 0, keepdims=False) for k in range(SIDE)
        ]

    def spread_x(array):
        return [array] + [along_x(array, step) for step in (1, 2, 3)]

    def exchange_x(chunk):
        return [chunk(0)] + [along_x(chunk(step), step) for step in (1, 2, 3)]

    keep, give = kernel_call(
        split_link,
        jnp.stack([in_low, in_high, away_low, away_high]),
        [link_rows],
        [shape((rows, half), bf16)] * 2,
    )
    got = permuted(give, lambda p, y, x: (p, partner(p, y), x))
    two = jnp.where(
        out_place == 0, jnp.concatenate([keep, got]), jnp.concatenate([got, keep])
    )
    pieces = spread_x(two)
    left, second, coupling_rows = tie((first[:, : nodes // 2], second, coupling_rows), two)
    second = over_axis(second, "x")
    first_left = [left] + [along_y(left, step) for step in (1, 2, 3)]
    turned = jnp.where(
        even,
        coupling_rows,
        coupling_rows.reshape(rows, SIDE, SIDE, rows).transpose(0, 2, 1, 3).reshape(rows, nodes),
    )
    coupling_out = over_parity(turned, True)
    pieces = tie(pieces, first_left, turned)
    source_rows, weight_row = tie((source_rows, weight_row), two)
    started = weight_row[None, :] * source_rows

    def source_chunk(step):
        part = lax.dynamic_slice(started, ((x ^ step) * share, 0), (share, rows))
        return jnp.concatenate([part, jnp.broadcast_to(weight_row[None, :], (8, rows))], axis=0)

    line_values = jnp.concatenate(ordered(exchange_x(source_chunk)), axis=1)
    line_weights = line_values[share : share + 1]
    away_weights = permuted(line_weights, lambda p, y, x: (p, partner(p, y), x))
    (block,) = kernel_call(assemble_link, place, pieces, [shape((half, half), bf16)])
    weight_half = jnp.where(
        out_place == 0,
        jnp.concatenate([line_weights, away_weights], axis=1),
        jnp.concatenate([away_weights, line_weights], axis=1),
    )
    zeros = jnp.zeros((share, line), f32)
    own = jnp.where(
        out_place == 0,
        jnp.concatenate([line_values[:share], zeros], axis=1),
        jnp.concatenate([zeros, line_values[:share]], axis=1),
    )

    message = own.astype(bf16)
    final = message
    for turn in range(1, PARTITIONS):
        far, near = turn_messages(message, turn - 1)
        previous = (far.astype(f32) + near.astype(f32)).astype(bf16)
        if turn == 12:
            second, first_right = tie((second, first_right), message)
            (inner,) = kernel_call(
                inner_kernel,
                jnp.stack([even.astype(jnp.int32), y]),
                [second, first_right] + first_left,
                [shape((line, line), bf16)],
                flops=2 * line * line * nodes,
            )
            inner_all = over_parity(inner, False)
            previous = tie(previous, inner)
        product = lax.dot_general(
            previous, block, (((1,), (1,)), ((), ())), preferred_element_type=f32
        )
        message = (own - weight_half * product).astype(bf16)
        final = jnp.where(p == turn, message, final)

    total = final.astype(f32) + permuted(
        final, lambda p, y, x: (p, partner(p, y), x)
    ).astype(f32)
    rounded = total.astype(bf16)

    back = jnp.dot(rounded, block, preferred_element_type=f32).astype(bf16)
    mine = lax.dynamic_slice(back, (0, in_place * line), (share, line))
    theirs = lax.dynamic_slice(back, (0, (1 - in_place) * line), (share, line))
    later = range(1, PARTITIONS)
    following = permuted(
        theirs, lambda p, y, x: (p - 1, other(p, y), x), later
    ).astype(f32) + permuted(mine, lambda p, y, x: (p - 1, y, x), later).astype(f32)
    following = following.astype(bf16)

    rest = permuted(rounded, lambda p, y, x: (p, other(p, y), x))
    m0, m1, r0, r1 = rounded[:, :line], rounded[:, line:], rest[:, :line], rest[:, line:]
    lines = jnp.where(
        even,
        jnp.where(
            pair == 0,
            jnp.concatenate([m0, m1, r0, r1], axis=1),
            jnp.concatenate([r0, r1, m0, m1], axis=1),
        ),
        jnp.where(
            ring == 0,
            jnp.concatenate([m0, r0, r1, m1], axis=1),
            jnp.concatenate([r0, m0, m1, r1], axis=1),
        ),
    )
    sweep_line = lax.dynamic_slice(total, (0, out_place * line), (share, line))
    sweep_high = sweep_line.astype(bf16)
    sweep_low = (sweep_line - sweep_high.astype(f32)).astype(bf16)

    def last_chunk(step):
        start = (0, (x ^ step) * rows)
        extra = [
            lax.dynamic_slice(array, start, (share, rows))
            for array in (following, sweep_high, sweep_low)
        ]
        return jnp.concatenate([lines] + extra, axis=1)

    last = exchange_x(last_chunk)

    coupling_out, inner_all = tie((coupling_out, inner_all), rounded)
    folded = jnp.dot(coupling_out, inner_all, preferred_element_type=f32).astype(bf16)

    def folded_chunk(step):
        return lax.dynamic_slice(folded, ((r ^ step) * rows, 0), (rows, line))

    back_rows = [folded_chunk(0)] + [along_reduce(folded_chunk(s), s) for s in (1, 2, 3)]
    schur_rows, narrow = kernel_call(
        schur_kernel,
        jnp.stack([r, jnp.where(even, SIDE, 1), jnp.where(even, 1, SIDE)]),
        [separator_rows] + back_rows,
        [shape((rows, nodes), f32), shape((rows, nodes), bf16)],
    )
    sweep, residual = kernel_call(
        finish_kernel,
        place,
        [narrow, weight_row[None, :]] + last,
        [shape((keys, rows), f32)] * 2,
        flops=2 * keys * rows * nodes,
    )
    return schur_rows[None], sweep[None], residual[None]


def solution(mesh):
    in_specs = (
        P("tm", "blk", None),
        P("tm", "blk", None),
        P("tm", "blk", None),
        P("tm", "blk", None),
        P("tm", None, "blk"),
        P("tm", "blk"),
    )
    out_specs = (P("tm", "blk", None), P("tm", None, "blk"), P("tm", None, "blk"))
    return jax.shard_map(shards, mesh=mesh, in_specs=in_specs, out_specs=out_specs, check_vma=False)
```

```python
import jax
import jax.numpy as jnp
from jax import lax
from jax.experimental import pallas as pl
from jax.experimental.pallas import tpu as pltpu
from jax.sharding import PartitionSpec as P

AXES = ("tm", "blk")
SIDE = 4
PLANE = SIDE * SIDE
PARTITIONS = 16
f32, bf16 = jnp.float32, jnp.bfloat16


def partner(p, y):
    return y ^ 1 if p % 2 == 0 else y ^ 3


def other(p, y):
    return y ^ 3 if p % 2 == 0 else y ^ 1


def permuted(value, rule, partitions=range(PARTITIONS)):
    pairs = []
    for p in partitions:
        for b in range(PLANE):
            target, y, x = rule(p, *divmod(b, SIDE))
            pairs.append((p * PLANE + b, target * PLANE + y * SIDE + x))
    return lax.ppermute(value, AXES, pairs)


def along_x(value, step):
    return permuted(value, lambda p, y, x: (p, y, x ^ step))


def along_y(value, step):
    return permuted(value, lambda p, y, x: (p, y ^ step, x))


def turn_messages(message, last):
    if last % 2 == 0:
        far = permuted(message, lambda p, y, x: (p ^ 1, y ^ 1, x))
        near = permuted(message, lambda p, y, x: (p ^ 1, y, x))
    else:
        far = permuted(message, lambda p, y, x: (p + 1, partner(p, y), x), [last])
        near = permuted(message, lambda p, y, x: (p + 1, y, x), [last])
    return far, near


def tie(values, *others):
    return lax.optimization_barrier((values, others))[0]


def kernel_call(body, place, operands, out_shapes, flops=0, space=pltpu.VMEM, scratch=()):
    out_bytes = sum(s.size * s.dtype.itemsize for s in out_shapes)
    in_bytes = sum(o.size * o.dtype.itemsize for o in operands)
    whole = pl.BlockSpec(memory_space=space)
    return pl.pallas_call(
        body,
        out_shape=out_shapes,
        in_specs=[pl.BlockSpec(memory_space=pltpu.SMEM)] + [whole] * len(operands),
        out_specs=[whole] * len(out_shapes),
        scratch_shapes=scratch,
        compiler_params=pltpu.CompilerParams(vmem_limit_bytes=24 * 1024 * 1024),
        cost_estimate=pl.CostEstimate(
            flops=flops, bytes_accessed=in_bytes + out_bytes, transcendentals=0
        ),
    )(place, *operands)


def block_of(index, size):
    return pl.ds(pl.multiple_of(index * size, size), size)


def split_link(place, link, weight, keep, give):
    rows, size = keep.shape[0], keep.shape[1] // 2
    for half in range(2):
        keep[:, half * size : (half + 1) * size] = link[:, block_of(place[half], size)]
        give[:rows, half * size : (half + 1) * size] = link[:, block_of(place[2 + half], size)]
    high = weight[...].astype(bf16)
    rest = weight[...] - high.astype(f32)
    middle = rest.astype(bf16)
    low = (rest - middle.astype(f32)).astype(bf16)
    width = weight.shape[1]
    row = lax.broadcasted_iota(jnp.int32, (16, width), 0)
    parts = jnp.where(
        row == 0,
        high.astype(f32),
        jnp.where(row == 1, middle.astype(f32), jnp.where(row == 2, low.astype(f32), 0.0)),
    )
    give[rows:, :] = jnp.zeros((16, 2 * size), bf16)
    give[rows:, :width] = parts.astype(bf16)


def assemble_link(place, *refs):
    pieces, out, sems = refs[:SIDE], refs[SIDE], refs[SIDE + 1]
    size = pieces[0].shape[0] // 2
    copies = []
    for step in range(SIDE):
        for half in range(2):
            copies.append(
                pltpu.make_async_copy(
                    pieces[step].at[half * size : (half + 1) * size, :],
                    out.at[block_of(half * SIDE + (place[0] ^ step), size), :],
                    sems.at[2 * step + half],
                )
            )
    for copy in copies:
        copy.start()
    for copy in copies:
        copy.wait()


def schur_kernel(place, *refs):
    separator, *pieces, schur, narrow = refs
    size = schur.shape[0]
    for step in range(SIDE):
        for k in range(SIDE):
            columns = block_of(k * place[1] + (place[0] ^ step) * place[2], size)
            value = separator[:, columns] - pieces[step][:, k * size : (k + 1) * size].astype(f32)
            schur[:, columns] = value
            narrow[:, columns] = value.astype(bf16)


def finish_kernel(place, narrow, weight, *refs):
    *pieces, sweep, residual = refs
    rows, nodes = narrow.shape
    share = pieces[0].shape[0]
    iterate = jnp.concatenate([piece[:, :nodes] for piece in pieces], axis=0)
    terms = lax.dot_general(
        iterate, narrow[...], (((1,), (1,)), ((), ())), preferred_element_type=f32
    )
    for step in range(SIDE):
        extra = [
            pieces[step][:, nodes + k * rows : nodes + (k + 1) * rows].astype(f32) for k in range(3)
        ]
        value = extra[1] + extra[2]
        target = block_of(place[0] ^ step, share)
        sweep[target, :] = value
        residual[target, :] = (
            value / weight[...] - terms[step * share : (step + 1) * share] - extra[0]
        )


def gather_groups(along_reduce):
    groups = []
    for p in range(PARTITIONS):
        for k in range(SIDE):
            if (p % 2 == 0) == along_reduce:
                groups.append([p * PLANE + k * SIDE + x for x in range(SIDE)])
            else:
                groups.append([p * PLANE + y * SIDE + k for y in range(SIDE)])
    return groups


def gathered(array, along_reduce):
    return lax.all_gather(
        array, AXES, axis=0, tiled=True, axis_index_groups=gather_groups(along_reduce)
    )


def along_reduce(value, step):
    return permuted(
        value, lambda p, y, x: (p, y, x ^ step) if p % 2 == 0 else (p, y ^ step, x)
    )


def shards(interior_inverse, coupling, separator, link, source, weights):
    inverse_rows, coupling_rows, separator_rows = interior_inverse[0], coupling[0], separator[0]
    link_rows, source_rows, weight_row = link[0], source[0], weights[0]
    rows, nodes = link_rows.shape
    keys = source_rows.shape[0]
    share = keys // SIDE
    line = SIDE * rows
    half = 2 * line
    shape = jax.ShapeDtypeStruct
    p = lax.axis_index("tm").astype(jnp.int32)
    b = lax.axis_index("blk").astype(jnp.int32)
    y, x = b >> 2, b & 3
    even = (p & 1) == 0
    r = jnp.where(even, x, y)
    pair = y >> 1
    ring = ((y + 1) >> 1) & 1
    out_place = jnp.where(even, y & 1, pair)
    in_place = jnp.where(even, pair, y & 1)
    in_low = jnp.where(even, ring, 2 * pair)
    in_high = jnp.where(even, 3 - ring, 2 * pair + 1)
    away_low = jnp.where(even, 1 - ring, 2 - 2 * pair)
    away_high = jnp.where(even, 2 + ring, 3 - 2 * pair)
    place = jnp.stack([x, y])

    coupling_in = gathered(coupling_rows, False)

    def ordered(pieces):
        stacked = jnp.stack(pieces)
        return [
            lax.dynamic_index_in_dim(stacked, x ^ k, 0, keepdims=False) for k in range(SIDE)
        ]

    def spread_x(array):
        return [array] + [along_x(array, step) for step in (1, 2, 3)]

    def exchange_x(chunk):
        return [chunk(0)] + [along_x(chunk(step), step) for step in (1, 2, 3)]

    keep, give = kernel_call(
        split_link,
        jnp.stack([in_low, in_high, away_low, away_high]),
        [link_rows, weight_row[None, :]],
        [shape((rows, half), bf16), shape((rows + 16, half), bf16)],
    )
    got = permuted(give, lambda p, y, x: (p, partner(p, y), x))
    away_weight = got[rows : rows + 3, :rows].astype(f32).sum(axis=0, keepdims=True)
    got = got[:rows]
    two = jnp.where(
        out_place == 0, jnp.concatenate([keep, got]), jnp.concatenate([got, keep])
    )
    pieces = spread_x(two)
    source_rows, away_weight, coupling_late = tie(
        (source_rows, away_weight, coupling_rows), pieces[1]
    )
    started = weight_row[None, :] * source_rows
    both_weights = jnp.concatenate(
        [weight_row[None, :], away_weight, jnp.zeros((6, rows), f32)], axis=0
    )

    def source_chunk(step):
        part = lax.dynamic_slice(started, ((x ^ step) * share, 0), (share, rows))
        return jnp.concatenate([part, both_weights], axis=0)

    line_values = jnp.concatenate(ordered(exchange_x(source_chunk)), axis=1)
    line_weights, away_weights = line_values[share : share + 1], line_values[share + 1 : share + 2]
    turned = jnp.where(
        even,
        coupling_late,
        coupling_late.reshape(rows, SIDE, SIDE, rows).transpose(0, 2, 1, 3).reshape(rows, nodes),
    )
    outer = gathered(jnp.concatenate([inverse_rows, turned]), True).reshape(SIDE, 2, rows, nodes)
    pieces = tie(pieces, line_values, turned)
    (block,) = kernel_call(
        assemble_link,
        place,
        pieces,
        [shape((half, half), bf16)],
        space=pl.ANY,
        scratch=[pltpu.SemaphoreType.DMA((2 * SIDE,))],
    )
    weight_half = jnp.where(
        out_place == 0,
        jnp.concatenate([line_weights, away_weights], axis=1),
        jnp.concatenate([away_weights, line_weights], axis=1),
    )
    zeros = jnp.zeros((share, line), f32)
    own = jnp.where(
        out_place == 0,
        jnp.concatenate([line_values[:share], zeros], axis=1),
        jnp.concatenate([zeros, line_values[:share]], axis=1),
    )

    message = own.astype(bf16)
    final = message
    for turn in range(1, PARTITIONS):
        far, near = turn_messages(message, turn - 1)
        previous = (far.astype(f32) + near.astype(f32)).astype(bf16)
        if turn == 10:
            outer, coupling_in = tie((outer, coupling_in), message)
            inner = lax.dot_general(
                outer[:, 0].reshape(line, nodes),
                coupling_in,
                (((1,), (1,)), ((), ())),
                preferred_element_type=f32,
            ).astype(bf16)
            inner_all = gathered(inner, False)
            previous = tie(previous, inner)
        product = lax.dot_general(
            previous, block, (((1,), (1,)), ((), ())), preferred_element_type=f32
        )
        message = (own - weight_half * product).astype(bf16)
        final = jnp.where(p == turn, message, final)

    total = final.astype(f32) + permuted(
        final, lambda p, y, x: (p, partner(p, y), x)
    ).astype(f32)
    rounded = total.astype(bf16)

    back = jnp.dot(rounded, block, preferred_element_type=f32).astype(bf16)
    mine = lax.dynamic_slice(back, (0, in_place * line), (share, line))
    theirs = lax.dynamic_slice(back, (0, (1 - in_place) * line), (share, line))
    later = range(1, PARTITIONS)
    following = permuted(
        theirs, lambda p, y, x: (p - 1, other(p, y), x), later
    ).astype(f32) + permuted(mine, lambda p, y, x: (p - 1, y, x), later).astype(f32)
    following = following.astype(bf16)

    rest = permuted(rounded, lambda p, y, x: (p, other(p, y), x))
    m0, m1, r0, r1 = rounded[:, :line], rounded[:, line:], rest[:, :line], rest[:, line:]
    lines = jnp.where(
        even,
        jnp.where(
            pair == 0,
            jnp.concatenate([m0, m1, r0, r1], axis=1),
            jnp.concatenate([r0, r1, m0, m1], axis=1),
        ),
        jnp.where(
            ring == 0,
            jnp.concatenate([m0, r0, r1, m1], axis=1),
            jnp.concatenate([r0, m0, m1, r1], axis=1),
        ),
    )
    sweep_line = lax.dynamic_slice(total, (0, out_place * line), (share, line))
    sweep_high = sweep_line.astype(bf16)
    sweep_low = (sweep_line - sweep_high.astype(f32)).astype(bf16)

    def last_chunk(step):
        start = (0, (x ^ step) * rows)
        extra = [
            lax.dynamic_slice(array, start, (share, rows))
            for array in (following, sweep_high, sweep_low)
        ]
        return jnp.concatenate([lines] + extra, axis=1)

    last = exchange_x(last_chunk)

    inner_all = tie(inner_all, rounded)
    folded = jnp.dot(
        outer[:, 1].reshape(line, nodes), inner_all, preferred_element_type=f32
    ).astype(bf16)

    def folded_chunk(step):
        return lax.dynamic_slice(folded, ((r ^ step) * rows, 0), (rows, line))

    back_rows = [folded_chunk(0)] + [along_reduce(folded_chunk(s), s) for s in (1, 2, 3)]
    schur_rows, narrow = kernel_call(
        schur_kernel,
        jnp.stack([r, jnp.where(even, SIDE, 1), jnp.where(even, 1, SIDE)]),
        [separator_rows] + back_rows,
        [shape((rows, nodes), f32), shape((rows, nodes), bf16)],
    )
    sweep, residual = kernel_call(
        finish_kernel,
        place,
        [narrow, weight_row[None, :]] + last,
        [shape((keys, rows), f32)] * 2,
        flops=2 * keys * rows * nodes,
    )
    return schur_rows[None], sweep[None], residual[None]


def solution(mesh):
    in_specs = (
        P("tm", "blk", None),
        P("tm", "blk", None),
        P("tm", "blk", None),
        P("tm", "blk", None),
        P("tm", None, "blk"),
        P("tm", "blk"),
    )
    out_specs = (P("tm", "blk", None), P("tm", None, "blk"), P("tm", None, "blk"))
    return jax.shard_map(shards, mesh=mesh, in_specs=in_specs, out_specs=out_specs, check_vma=False)
```

```python
import jax
import jax.numpy as jnp
from jax import lax
from jax.experimental import pallas as pl
from jax.experimental.pallas import tpu as pltpu
from jax.sharding import PartitionSpec as P

AXES = ("tm", "blk")
SIDE = 4
PLANE = SIDE * SIDE
PARTITIONS = 16
f32, bf16 = jnp.float32, jnp.bfloat16


def partner(p, y):
    return y ^ 1 if p % 2 == 0 else y ^ 3


def other(p, y):
    return y ^ 3 if p % 2 == 0 else y ^ 1


def permuted(value, rule, partitions=range(PARTITIONS)):
    pairs = []
    for p in partitions:
        for b in range(PLANE):
            target, y, x = rule(p, *divmod(b, SIDE))
            pairs.append((p * PLANE + b, target * PLANE + y * SIDE + x))
    return lax.ppermute(value, AXES, pairs)


def along_x(value, step):
    return permuted(value, lambda p, y, x: (p, y, x ^ step))


def along_y(value, step):
    return permuted(value, lambda p, y, x: (p, y ^ step, x))


def turn_messages(message, last):
    if last % 2 == 0:
        far = permuted(message, lambda p, y, x: (p ^ 1, y ^ 1, x))
        near = permuted(message, lambda p, y, x: (p ^ 1, y, x))
    else:
        far = permuted(message, lambda p, y, x: (p + 1, partner(p, y), x), [last])
        near = permuted(message, lambda p, y, x: (p + 1, y, x), [last])
    return far, near


def tie(values, *others):
    return lax.optimization_barrier((values, others))[0]


def kernel_call(body, place, operands, out_shapes, flops=0):
    out_bytes = sum(s.size * s.dtype.itemsize for s in out_shapes)
    in_bytes = sum(o.size * o.dtype.itemsize for o in operands)
    whole = pl.BlockSpec(memory_space=pltpu.VMEM)
    return pl.pallas_call(
        body,
        out_shape=out_shapes,
        in_specs=[pl.BlockSpec(memory_space=pltpu.SMEM)] + [whole] * len(operands),
        out_specs=[whole] * len(out_shapes),
        compiler_params=pltpu.CompilerParams(vmem_limit_bytes=24 * 1024 * 1024),
        cost_estimate=pl.CostEstimate(
            flops=flops, bytes_accessed=in_bytes + out_bytes, transcendentals=0
        ),
    )(place, *operands)


def block_of(index, size):
    return pl.ds(pl.multiple_of(index * size, size), size)


def split_link(place, link, keep, give):
    size = keep.shape[1] // 2
    for half in range(2):
        keep[:, half * size : (half + 1) * size] = link[:, block_of(place[half], size)]
        give[:, half * size : (half + 1) * size] = link[:, block_of(place[2 + half], size)]


def assemble_link(place, *refs):
    *pieces, out = refs
    size = pieces[0].shape[0] // 2
    for step in range(SIDE):
        for half in range(2):
            out[block_of(half * SIDE + (place[0] ^ step), size), :] = pieces[step][
                half * size : (half + 1) * size, :
            ]


def schur_kernel(place, *refs):
    separator, *pieces, schur, narrow = refs
    size = schur.shape[0]
    for step in range(SIDE):
        for k in range(SIDE):
            columns = block_of(k * place[1] + (place[0] ^ step) * place[2], size)
            value = separator[:, columns] - pieces[step][:, k * size : (k + 1) * size].astype(f32)
            schur[:, columns] = value
            narrow[:, columns] = value.astype(bf16)


def finish_kernel(place, narrow, weight, *refs):
    *pieces, sweep, residual = refs
    rows, nodes = narrow.shape
    share = pieces[0].shape[0]
    iterate = jnp.concatenate([piece[:, :nodes] for piece in pieces], axis=0)
    terms = lax.dot_general(
        iterate, narrow[...], (((1,), (1,)), ((), ())), preferred_element_type=f32
    )
    for step in range(SIDE):
        extra = [
            pieces[step][:, nodes + k * rows : nodes + (k + 1) * rows].astype(f32) for k in range(3)
        ]
        value = extra[1] + extra[2]
        target = block_of(place[0] ^ step, share)
        sweep[target, :] = value
        residual[target, :] = (
            value / weight[...] - terms[step * share : (step + 1) * share] - extra[0]
        )


def gather_groups(along_reduce):
    groups = []
    for p in range(PARTITIONS):
        for k in range(SIDE):
            if (p % 2 == 0) == along_reduce:
                groups.append([p * PLANE + k * SIDE + x for x in range(SIDE)])
            else:
                groups.append([p * PLANE + y * SIDE + k for y in range(SIDE)])
    return groups


def gathered(array, along_reduce):
    return lax.all_gather(
        array, AXES, axis=0, tiled=True, axis_index_groups=gather_groups(along_reduce)
    )


def along_reduce(value, step):
    return permuted(
        value, lambda p, y, x: (p, y, x ^ step) if p % 2 == 0 else (p, y ^ step, x)
    )


def shards(interior_inverse, coupling, separator, link, source, weights):
    inverse_rows, coupling_rows, separator_rows = interior_inverse[0], coupling[0], separator[0]
    link_rows, source_rows, weight_row = link[0], source[0], weights[0]
    rows, nodes = link_rows.shape
    keys = source_rows.shape[0]
    share = keys // SIDE
    line = SIDE * rows
    half = 2 * line
    shape = jax.ShapeDtypeStruct
    p = lax.axis_index("tm").astype(jnp.int32)
    b = lax.axis_index("blk").astype(jnp.int32)
    y, x = b >> 2, b & 3
    even = (p & 1) == 0
    r = jnp.where(even, x, y)
    pair = y >> 1
    ring = ((y + 1) >> 1) & 1
    out_place = jnp.where(even, y & 1, pair)
    in_place = jnp.where(even, pair, y & 1)
    in_low = jnp.where(even, ring, 2 * pair)
    in_high = jnp.where(even, 3 - ring, 2 * pair + 1)
    away_low = jnp.where(even, 1 - ring, 2 - 2 * pair)
    away_high = jnp.where(even, 2 + ring, 3 - 2 * pair)
    place = jnp.stack([x, y])

    coupling_in = gathered(coupling_rows, False)
    turned = jnp.where(
        even,
        coupling_rows,
        coupling_rows.reshape(rows, SIDE, SIDE, rows).transpose(0, 2, 1, 3).reshape(rows, nodes),
    )
    outer = gathered(jnp.concatenate([inverse_rows, turned], axis=1), True)

    def ordered(pieces):
        stacked = jnp.stack(pieces)
        return [
            lax.dynamic_index_in_dim(stacked, x ^ k, 0, keepdims=False) for k in range(SIDE)
        ]

    def spread_x(array):
        return [array] + [along_x(array, step) for step in (1, 2, 3)]

    def exchange_x(chunk):
        return [chunk(0)] + [along_x(chunk(step), step) for step in (1, 2, 3)]

    keep, give = kernel_call(
        split_link,
        jnp.stack([in_low, in_high, away_low, away_high]),
        [link_rows],
        [shape((rows, half), bf16)] * 2,
    )
    got = permuted(give, lambda p, y, x: (p, partner(p, y), x))
    started = weight_row[None, :] * source_rows

    def source_chunk(step):
        part = lax.dynamic_slice(started, ((x ^ step) * share, 0), (share, rows))
        return jnp.concatenate([part, jnp.broadcast_to(weight_row[None, :], (8, rows))], axis=0)

    line_values = jnp.concatenate(ordered(exchange_x(source_chunk)), axis=1)
    keep, got, line_values = tie((keep, got, line_values), turned)
    line_weights = line_values[share : share + 1]
    two = jnp.where(
        out_place == 0, jnp.concatenate([keep, got]), jnp.concatenate([got, keep])
    )
    pieces = spread_x(two)
    away_weights = permuted(line_weights, lambda p, y, x: (p, partner(p, y), x))
    (block,) = kernel_call(assemble_link, place, pieces, [shape((half, half), bf16)])
    weight_half = jnp.where(
        out_place == 0,
        jnp.concatenate([line_weights, away_weights], axis=1),
        jnp.concatenate([away_weights, line_weights], axis=1),
    )
    zeros = jnp.zeros((share, line), f32)
    own = jnp.where(
        out_place == 0,
        jnp.concatenate([line_values[:share], zeros], axis=1),
        jnp.concatenate([zeros, line_values[:share]], axis=1),
    )

    message = own.astype(bf16)
    final = message
    for turn in range(1, PARTITIONS):
        far, near = turn_messages(message, turn - 1)
        previous = (far.astype(f32) + near.astype(f32)).astype(bf16)
        if turn == 10:
            outer, coupling_in = tie((outer, coupling_in), message)
            inner = lax.dot_general(
                outer[:, :nodes], coupling_in, (((1,), (1,)), ((), ())), preferred_element_type=f32
            ).astype(bf16)
            inner_all = gathered(inner, False)
            previous = tie(previous, inner)
        product = lax.dot_general(
            previous, block, (((1,), (1,)), ((), ())), preferred_element_type=f32
        )
        message = (own - weight_half * product).astype(bf16)
        final = jnp.where(p == turn, message, final)

    total = final.astype(f32) + permuted(
        final, lambda p, y, x: (p, partner(p, y), x)
    ).astype(f32)
    rounded = total.astype(bf16)

    back = jnp.dot(rounded, block, preferred_element_type=f32).astype(bf16)
    mine = lax.dynamic_slice(back, (0, in_place * line), (share, line))
    theirs = lax.dynamic_slice(back, (0, (1 - in_place) * line), (share, line))
    later = range(1, PARTITIONS)
    following = permuted(
        theirs, lambda p, y, x: (p - 1, other(p, y), x), later
    ).astype(f32) + permuted(mine, lambda p, y, x: (p - 1, y, x), later).astype(f32)
    following = following.astype(bf16)

    rest = permuted(rounded, lambda p, y, x: (p, other(p, y), x))
    m0, m1, r0, r1 = rounded[:, :line], rounded[:, line:], rest[:, :line], rest[:, line:]
    lines = jnp.where(
        even,
        jnp.where(
            pair == 0,
            jnp.concatenate([m0, m1, r0, r1], axis=1),
            jnp.concatenate([r0, r1, m0, m1], axis=1),
        ),
        jnp.where(
            ring == 0,
            jnp.concatenate([m0, r0, r1, m1], axis=1),
            jnp.concatenate([r0, m0, m1, r1], axis=1),
        ),
    )
    sweep_line = lax.dynamic_slice(total, (0, out_place * line), (share, line))
    sweep_high = sweep_line.astype(bf16)
    sweep_low = (sweep_line - sweep_high.astype(f32)).astype(bf16)

    def last_chunk(step):
        start = (0, (x ^ step) * rows)
        extra = [
            lax.dynamic_slice(array, start, (share, rows))
            for array in (following, sweep_high, sweep_low)
        ]
        return jnp.concatenate([lines] + extra, axis=1)

    last = exchange_x(last_chunk)

    inner_all = tie(inner_all, rounded)
    folded = jnp.dot(outer[:, nodes:], inner_all, preferred_element_type=f32).astype(bf16)

    def folded_chunk(step):
        return lax.dynamic_slice(folded, ((r ^ step) * rows, 0), (rows, line))

    back_rows = [folded_chunk(0)] + [along_reduce(folded_chunk(s), s) for s in (1, 2, 3)]
    schur_rows, narrow = kernel_call(
        schur_kernel,
        jnp.stack([r, jnp.where(even, SIDE, 1), jnp.where(even, 1, SIDE)]),
        [separator_rows] + back_rows,
        [shape((rows, nodes), f32), shape((rows, nodes), bf16)],
    )
    sweep, residual = kernel_call(
        finish_kernel,
        place,
        [narrow, weight_row[None, :]] + last,
        [shape((keys, rows), f32)] * 2,
        flops=2 * keys * rows * nodes,
    )
    return schur_rows[None], sweep[None], residual[None]


def solution(mesh):
    in_specs = (
        P("tm", "blk", None),
        P("tm", "blk", None),
        P("tm", "blk", None),
        P("tm", "blk", None),
        P("tm", None, "blk"),
        P("tm", "blk"),
    )
    out_specs = (P("tm", "blk", None), P("tm", None, "blk"), P("tm", None, "blk"))
    return jax.shard_map(shards, mesh=mesh, in_specs=in_specs, out_specs=out_specs, check_vma=False)
```

```python
import jax
import jax.numpy as jnp
from jax import lax
from jax.experimental import pallas as pl
from jax.experimental.pallas import tpu as pltpu
from jax.sharding import PartitionSpec as P

AXES = ("tm", "blk")
SIDE = 4
PLANE = SIDE * SIDE
PARTITIONS = 16
f32, bf16 = jnp.float32, jnp.bfloat16


def partner(p, y):
    return y ^ 1 if p % 2 == 0 else y ^ 3


def other(p, y):
    return y ^ 3 if p % 2 == 0 else y ^ 1


def permuted(value, rule, partitions=range(PARTITIONS)):
    pairs = []
    for p in partitions:
        for b in range(PLANE):
            target, y, x = rule(p, *divmod(b, SIDE))
            pairs.append((p * PLANE + b, target * PLANE + y * SIDE + x))
    return lax.ppermute(value, AXES, pairs)


def along_x(value, step):
    return permuted(value, lambda p, y, x: (p, y, x ^ step))


def along_y(value, step):
    return permuted(value, lambda p, y, x: (p, y ^ step, x))


def turn_messages(message, last):
    if last % 2 == 0:
        far = permuted(message, lambda p, y, x: (p ^ 1, y ^ 1, x))
        near = permuted(message, lambda p, y, x: (p ^ 1, y, x))
    else:
        far = permuted(message, lambda p, y, x: (p + 1, partner(p, y), x), [last])
        near = permuted(message, lambda p, y, x: (p + 1, y, x), [last])
    return far, near


def tie(values, *others):
    return lax.optimization_barrier((values, others))[0]


def kernel_call(body, place, operands, out_shapes, flops=0):
    out_bytes = sum(s.size * s.dtype.itemsize for s in out_shapes)
    in_bytes = sum(o.size * o.dtype.itemsize for o in operands)
    whole = pl.BlockSpec(memory_space=pltpu.VMEM)
    return pl.pallas_call(
        body,
        out_shape=out_shapes,
        in_specs=[pl.BlockSpec(memory_space=pltpu.SMEM)] + [whole] * len(operands),
        out_specs=[whole] * len(out_shapes),
        compiler_params=pltpu.CompilerParams(vmem_limit_bytes=24 * 1024 * 1024),
        cost_estimate=pl.CostEstimate(
            flops=flops, bytes_accessed=in_bytes + out_bytes, transcendentals=0
        ),
    )(place, *operands)


def block_of(index, size):
    return pl.ds(pl.multiple_of(index * size, size), size)


def split_link(place, link, keep, give):
    size = keep.shape[1] // 2
    for half in range(2):
        keep[:, half * size : (half + 1) * size] = link[:, block_of(place[half], size)]
        give[:, half * size : (half + 1) * size] = link[:, block_of(place[2 + half], size)]


def assemble_link(place, *refs):
    *pieces, out = refs
    size = pieces[0].shape[0] // 2
    for step in range(SIDE):
        for half in range(2):
            out[block_of(half * SIDE + (place[0] ^ step), size), :] = pieces[step][
                half * size : (half + 1) * size, :
            ]


def outer_kernel(place, inverse, coupling, out):
    nodes = inverse.shape[1]
    size = nodes // PLANE
    out[:, :nodes] = inverse[...]
    for k in range(PLANE):
        source = (k % SIDE) * SIDE + k // SIDE
        out[:, nodes + k * size : nodes + (k + 1) * size] = coupling[
            :, source * size : (source + 1) * size
        ]


def schur_kernel(place, *refs):
    separator, *pieces, schur, narrow = refs
    for step in range(SIDE):
        columns = block_of(place[1] ^ step, pieces[step].shape[1])
        value = separator[:, columns] - pieces[step][...].astype(f32)
        schur[:, columns] = value
        narrow[:, columns] = value.astype(bf16)


def finish_kernel(place, narrow, weight, *refs):
    *pieces, sweep, residual = refs
    rows, nodes = narrow.shape
    share = pieces[0].shape[0]
    iterate = jnp.concatenate([piece[:, :nodes] for piece in pieces], axis=0)
    terms = lax.dot_general(
        iterate, narrow[...], (((1,), (1,)), ((), ())), preferred_element_type=f32
    )
    for step in range(SIDE):
        extra = [
            pieces[step][:, nodes + k * rows : nodes + (k + 1) * rows].astype(f32) for k in range(3)
        ]
        value = extra[1] + extra[2]
        target = block_of(place[0] ^ step, share)
        sweep[target, :] = value
        residual[target, :] = (
            value / weight[...] - terms[step * share : (step + 1) * share] - extra[0]
        )


def over_axis(array, axis):
    if axis == "x":
        groups = [[k * SIDE + i for i in range(SIDE)] for k in range(SIDE)]
    else:
        groups = [[i * SIDE + k for i in range(SIDE)] for k in range(SIDE)]
    return lax.all_gather(array, "blk", axis=0, tiled=True, axis_index_groups=groups)


def shards(interior_inverse, coupling, separator, link, source, weights):
    inverse_rows, coupling_rows, separator_rows = interior_inverse[0], coupling[0], separator[0]
    link_rows, source_rows, weight_row = link[0], source[0], weights[0]
    rows, nodes = link_rows.shape
    keys = source_rows.shape[0]
    share = keys // SIDE
    line = SIDE * rows
    half = 2 * line
    shape = jax.ShapeDtypeStruct
    p = lax.axis_index("tm").astype(jnp.int32)
    b = lax.axis_index("blk").astype(jnp.int32)
    y, x = b >> 2, b & 3
    even = (p & 1) == 0
    pair = y >> 1
    ring = ((y + 1) >> 1) & 1
    out_place = jnp.where(even, y & 1, pair)
    in_place = jnp.where(even, pair, y & 1)
    in_low = jnp.where(even, ring, 2 * pair)
    in_high = jnp.where(even, 3 - ring, 2 * pair + 1)
    away_low = jnp.where(even, 1 - ring, 2 - 2 * pair)
    away_high = jnp.where(even, 2 + ring, 3 - 2 * pair)
    place = jnp.stack([x, y])

    (outer,) = kernel_call(
        outer_kernel, place, [inverse_rows, coupling_rows], [shape((rows, 2 * nodes), bf16)]
    )
    link_rows = tie(link_rows, outer)
    outer = over_axis(outer, "y")

    def ordered(pieces):
        stacked = jnp.stack(pieces)
        return [
            lax.dynamic_index_in_dim(stacked, x ^ k, 0, keepdims=False) for k in range(SIDE)
        ]

    def spread_x(array):
        return [array] + [along_x(array, step) for step in (1, 2, 3)]

    def exchange_x(chunk):
        return [chunk(0)] + [along_x(chunk(step), step) for step in (1, 2, 3)]

    keep, give = kernel_call(
        split_link,
        jnp.stack([in_low, in_high, away_low, away_high]),
        [link_rows],
        [shape((rows, half), bf16)] * 2,
    )
    got = permuted(give, lambda p, y, x: (p, partner(p, y), x))
    started = weight_row[None, :] * source_rows

    def source_chunk(step):
        part = lax.dynamic_slice(started, ((x ^ step) * share, 0), (share, rows))
        return jnp.concatenate([part, jnp.broadcast_to(weight_row[None, :], (8, rows))], axis=0)

    line_values = jnp.concatenate(ordered(exchange_x(source_chunk)), axis=1)
    keep, got, line_values = tie((keep, got, line_values))
    line_weights = line_values[share : share + 1]
    two = jnp.where(
        out_place == 0, jnp.concatenate([keep, got]), jnp.concatenate([got, keep])
    )
    pieces = spread_x(two)
    coupling_in = over_axis(tie(coupling_rows, pieces[1]), "x")
    away_weights = permuted(line_weights, lambda p, y, x: (p, partner(p, y), x))
    (block,) = kernel_call(assemble_link, place, pieces, [shape((half, half), bf16)])
    weight_half = jnp.where(
        out_place == 0,
        jnp.concatenate([line_weights, away_weights], axis=1),
        jnp.concatenate([away_weights, line_weights], axis=1),
    )
    zeros = jnp.zeros((share, line), f32)
    own = jnp.where(
        out_place == 0,
        jnp.concatenate([line_values[:share], zeros], axis=1),
        jnp.concatenate([zeros, line_values[:share]], axis=1),
    )

    message = own.astype(bf16)
    final = message
    for turn in range(1, PARTITIONS):
        far, near = turn_messages(message, turn - 1)
        previous = (far.astype(f32) + near.astype(f32)).astype(bf16)
        if turn == 10:
            outer, coupling_in = tie((outer, coupling_in), message)
            inner = lax.dot_general(
                outer[:, :nodes], coupling_in, (((1,), (1,)), ((), ())), preferred_element_type=f32
            ).astype(bf16)
            inner_all = over_axis(inner, "x")
            previous = tie(previous, inner)
        product = lax.dot_general(
            previous, block, (((1,), (1,)), ((), ())), preferred_element_type=f32
        )
        message = (own - weight_half * product).astype(bf16)
        final = jnp.where(p == turn, message, final)

    total = final.astype(f32) + permuted(
        final, lambda p, y, x: (p, partner(p, y), x)
    ).astype(f32)
    rounded = total.astype(bf16)

    back = jnp.dot(rounded, block, preferred_element_type=f32).astype(bf16)
    mine = lax.dynamic_slice(back, (0, in_place * line), (share, line))
    theirs = lax.dynamic_slice(back, (0, (1 - in_place) * line), (share, line))
    later = range(1, PARTITIONS)
    following = permuted(
        theirs, lambda p, y, x: (p - 1, other(p, y), x), later
    ).astype(f32) + permuted(mine, lambda p, y, x: (p - 1, y, x), later).astype(f32)
    following = following.astype(bf16)

    rest = permuted(rounded, lambda p, y, x: (p, other(p, y), x))
    m0, m1, r0, r1 = rounded[:, :line], rounded[:, line:], rest[:, :line], rest[:, line:]
    lines = jnp.where(
        even,
        jnp.where(
            pair == 0,
            jnp.concatenate([m0, m1, r0, r1], axis=1),
            jnp.concatenate([r0, r1, m0, m1], axis=1),
        ),
        jnp.where(
            ring == 0,
            jnp.concatenate([m0, r0, r1, m1], axis=1),
            jnp.concatenate([r0, m0, m1, r1], axis=1),
        ),
    )
    sweep_line = lax.dynamic_slice(total, (0, out_place * line), (share, line))
    sweep_high = sweep_line.astype(bf16)
    sweep_low = (sweep_line - sweep_high.astype(f32)).astype(bf16)

    def last_chunk(step):
        start = (0, (x ^ step) * rows)
        extra = [
            lax.dynamic_slice(array, start, (share, rows))
            for array in (following, sweep_high, sweep_low)
        ]
        return jnp.concatenate([lines] + extra, axis=1)

    last = exchange_x(last_chunk)

    inner_all = tie(inner_all, rounded)
    folded = jnp.dot(outer[:, nodes:], inner_all, preferred_element_type=f32).astype(bf16)

    def folded_chunk(step):
        return lax.dynamic_slice(folded, ((y ^ step) * rows, 0), (rows, line))

    back_rows = [folded_chunk(0)] + [along_y(folded_chunk(step), step) for step in (1, 2, 3)]
    schur_rows, narrow = kernel_call(
        schur_kernel,
        place,
        [separator_rows] + back_rows,
        [shape((rows, nodes), f32), shape((rows, nodes), bf16)],
    )
    sweep, residual = kernel_call(
        finish_kernel,
        place,
        [narrow, weight_row[None, :]] + last,
        [shape((keys, rows), f32)] * 2,
        flops=2 * keys * rows * nodes,
    )
    return schur_rows[None], sweep[None], residual[None]


def solution(mesh):
    in_specs = (
        P("tm", "blk", None),
        P("tm", "blk", None),
        P("tm", "blk", None),
        P("tm", "blk", None),
        P("tm", None, "blk"),
        P("tm", "blk"),
    )
    out_specs = (P("tm", "blk", None), P("tm", None, "blk"), P("tm", None, "blk"))
    return jax.shard_map(shards, mesh=mesh, in_specs=in_specs, out_specs=out_specs, check_vma=False)
```

```python
import jax
import jax.numpy as jnp
from jax import lax
from jax.experimental import pallas as pl
from jax.experimental.pallas import tpu as pltpu
from jax.sharding import PartitionSpec as P

AXES = ("tm", "blk")
SIDE = 4
PLANE = SIDE * SIDE
PARTITIONS = 16
f32, bf16 = jnp.float32, jnp.bfloat16


def partner(p, y):
    return y ^ 1 if p % 2 == 0 else y ^ 3


def other(p, y):
    return y ^ 3 if p % 2 == 0 else y ^ 1


def permuted(value, rule, partitions=range(PARTITIONS)):
    pairs = []
    for p in partitions:
        for b in range(PLANE):
            target, y, x = rule(p, *divmod(b, SIDE))
            pairs.append((p * PLANE + b, target * PLANE + y * SIDE + x))
    return lax.ppermute(value, AXES, pairs)


def along_x(value, step):
    return permuted(value, lambda p, y, x: (p, y, x ^ step))


def along_y(value, step):
    return permuted(value, lambda p, y, x: (p, y ^ step, x))


def turn_messages(message, last):
    if last % 2 == 0:
        far = permuted(message, lambda p, y, x: (p ^ 1, y ^ 1, x))
        near = permuted(message, lambda p, y, x: (p ^ 1, y, x))
    else:
        far = permuted(message, lambda p, y, x: (p + 1, partner(p, y), x), [last])
        near = permuted(message, lambda p, y, x: (p + 1, y, x), [last])
    return far, near


def tie(values, *others):
    return lax.optimization_barrier((values, others))[0]


def kernel_call(body, place, operands, out_shapes, flops=0):
    out_bytes = sum(s.size * s.dtype.itemsize for s in out_shapes)
    in_bytes = sum(o.size * o.dtype.itemsize for o in operands)
    whole = pl.BlockSpec(memory_space=pltpu.VMEM)
    return pl.pallas_call(
        body,
        out_shape=out_shapes,
        in_specs=[pl.BlockSpec(memory_space=pltpu.SMEM)] + [whole] * len(operands),
        out_specs=[whole] * len(out_shapes),
        compiler_params=pltpu.CompilerParams(vmem_limit_bytes=24 * 1024 * 1024),
        cost_estimate=pl.CostEstimate(
            flops=flops, bytes_accessed=in_bytes + out_bytes, transcendentals=0
        ),
    )(place, *operands)


def block_of(index, size):
    return pl.ds(pl.multiple_of(index * size, size), size)


def split_link(place, link, keep, give):
    size = keep.shape[1] // 2
    for half in range(2):
        keep[:, half * size : (half + 1) * size] = link[:, block_of(place[half], size)]
        give[:, half * size : (half + 1) * size] = link[:, block_of(place[2 + half], size)]


def assemble_link(place, *refs):
    *pieces, out = refs
    size = pieces[0].shape[0] // 2
    for step in range(SIDE):
        for half in range(2):
            out[block_of(half * SIDE + (place[0] ^ step), size), :] = pieces[step][
                half * size : (half + 1) * size, :
            ]


def schur_kernel(place, *refs):
    separator, *pieces, schur, narrow = refs
    size = schur.shape[0]
    for step in range(SIDE):
        for k in range(SIDE):
            columns = block_of(k * SIDE + (place[0] ^ step), size)
            value = separator[:, columns] - pieces[step][:, k * size : (k + 1) * size].astype(f32)
            schur[:, columns] = value
            narrow[:, columns] = value.astype(bf16)


def finish_kernel(place, narrow, weight, *refs):
    *pieces, sweep, residual = refs
    rows, nodes = narrow.shape
    share = pieces[0].shape[0]
    iterate = jnp.concatenate([piece[:, :nodes] for piece in pieces], axis=0)
    terms = lax.dot_general(
        iterate, narrow[...], (((1,), (1,)), ((), ())), preferred_element_type=f32
    )
    for step in range(SIDE):
        extra = [
            pieces[step][:, nodes + k * rows : nodes + (k + 1) * rows].astype(f32) for k in range(3)
        ]
        value = extra[1] + extra[2]
        target = block_of(place[0] ^ step, share)
        sweep[target, :] = value
        residual[target, :] = (
            value / weight[...] - terms[step * share : (step + 1) * share] - extra[0]
        )


def over_axis(array, axis):
    if axis == "x":
        groups = [[k * SIDE + i for i in range(SIDE)] for k in range(SIDE)]
    else:
        groups = [[i * SIDE + k for i in range(SIDE)] for k in range(SIDE)]
    return lax.all_gather(array, "blk", axis=0, tiled=True, axis_index_groups=groups)


def shards(interior_inverse, coupling, separator, link, source, weights):
    inverse_rows, coupling_rows, separator_rows = interior_inverse[0], coupling[0], separator[0]
    link_rows, source_rows, weight_row = link[0], source[0], weights[0]
    rows, nodes = link_rows.shape
    keys = source_rows.shape[0]
    share = keys // SIDE
    line = SIDE * rows
    half = 2 * line
    shape = jax.ShapeDtypeStruct
    p = lax.axis_index("tm").astype(jnp.int32)
    b = lax.axis_index("blk").astype(jnp.int32)
    y, x = b >> 2, b & 3
    even = (p & 1) == 0
    pair = y >> 1
    ring = ((y + 1) >> 1) & 1
    out_place = jnp.where(even, y & 1, pair)
    in_place = jnp.where(even, pair, y & 1)
    in_low = jnp.where(even, ring, 2 * pair)
    in_high = jnp.where(even, 3 - ring, 2 * pair + 1)
    away_low = jnp.where(even, 1 - ring, 2 - 2 * pair)
    away_high = jnp.where(even, 2 + ring, 3 - 2 * pair)
    place = jnp.stack([x, y])

    coupling_in = over_axis(coupling_rows, "y")
    outer = over_axis(jnp.concatenate([inverse_rows, coupling_rows], axis=1), "x")

    def ordered(pieces):
        stacked = jnp.stack(pieces)
        return [
            lax.dynamic_index_in_dim(stacked, x ^ k, 0, keepdims=False) for k in range(SIDE)
        ]

    def spread_x(array):
        return [array] + [along_x(array, step) for step in (1, 2, 3)]

    def exchange_x(chunk):
        return [chunk(0)] + [along_x(chunk(step), step) for step in (1, 2, 3)]

    keep, give = kernel_call(
        split_link,
        jnp.stack([in_low, in_high, away_low, away_high]),
        [link_rows],
        [shape((rows, half), bf16)] * 2,
    )
    got = permuted(give, lambda p, y, x: (p, partner(p, y), x))
    started = weight_row[None, :] * source_rows

    def source_chunk(step):
        part = lax.dynamic_slice(started, ((x ^ step) * share, 0), (share, rows))
        return jnp.concatenate([part, jnp.broadcast_to(weight_row[None, :], (8, rows))], axis=0)

    line_values = jnp.concatenate(ordered(exchange_x(source_chunk)), axis=1)
    keep, got, line_values = tie((keep, got, line_values))
    line_weights = line_values[share : share + 1]
    two = jnp.where(
        out_place == 0, jnp.concatenate([keep, got]), jnp.concatenate([got, keep])
    )
    pieces = spread_x(two)
    away_weights = permuted(line_weights, lambda p, y, x: (p, partner(p, y), x))
    (block,) = kernel_call(assemble_link, place, pieces, [shape((half, half), bf16)])
    weight_half = jnp.where(
        out_place == 0,
        jnp.concatenate([line_weights, away_weights], axis=1),
        jnp.concatenate([away_weights, line_weights], axis=1),
    )
    zeros = jnp.zeros((share, line), f32)
    own = jnp.where(
        out_place == 0,
        jnp.concatenate([line_values[:share], zeros], axis=1),
        jnp.concatenate([zeros, line_values[:share]], axis=1),
    )

    message = own.astype(bf16)
    final = message
    for turn in range(1, PARTITIONS):
        far, near = turn_messages(message, turn - 1)
        previous = (far.astype(f32) + near.astype(f32)).astype(bf16)
        if turn == 10:
            outer, coupling_in = tie((outer, coupling_in), message)
            inner = lax.dot_general(
                outer[:, :nodes], coupling_in, (((1,), (1,)), ((), ())), preferred_element_type=f32
            ).astype(bf16)
            inner_all = over_axis(inner, "y")
            previous = tie(previous, inner)
        product = lax.dot_general(
            previous, block, (((1,), (1,)), ((), ())), preferred_element_type=f32
        )
        message = (own - weight_half * product).astype(bf16)
        final = jnp.where(p == turn, message, final)

    total = final.astype(f32) + permuted(
        final, lambda p, y, x: (p, partner(p, y), x)
    ).astype(f32)
    rounded = total.astype(bf16)

    back = jnp.dot(rounded, block, preferred_element_type=f32).astype(bf16)
    mine = lax.dynamic_slice(back, (0, in_place * line), (share, line))
    theirs = lax.dynamic_slice(back, (0, (1 - in_place) * line), (share, line))
    later = range(1, PARTITIONS)
    following = permuted(
        theirs, lambda p, y, x: (p - 1, other(p, y), x), later
    ).astype(f32) + permuted(mine, lambda p, y, x: (p - 1, y, x), later).astype(f32)
    following = following.astype(bf16)

    rest = permuted(rounded, lambda p, y, x: (p, other(p, y), x))
    m0, m1, r0, r1 = rounded[:, :line], rounded[:, line:], rest[:, :line], rest[:, line:]
    lines = jnp.where(
        even,
        jnp.where(
            pair == 0,
            jnp.concatenate([m0, m1, r0, r1], axis=1),
            jnp.concatenate([r0, r1, m0, m1], axis=1),
        ),
        jnp.where(
            ring == 0,
            jnp.concatenate([m0, r0, r1, m1], axis=1),
            jnp.concatenate([r0, m0, m1, r1], axis=1),
        ),
    )
    sweep_line = lax.dynamic_slice(total, (0, out_place * line), (share, line))
    sweep_high = sweep_line.astype(bf16)
    sweep_low = (sweep_line - sweep_high.astype(f32)).astype(bf16)

    def last_chunk(step):
        start = (0, (x ^ step) * rows)
        extra = [
            lax.dynamic_slice(array, start, (share, rows))
            for array in (following, sweep_high, sweep_low)
        ]
        return jnp.concatenate([lines] + extra, axis=1)

    last = exchange_x(last_chunk)

    inner_all = tie(inner_all, rounded)
    folded = jnp.dot(outer[:, nodes:], inner_all, preferred_element_type=f32).astype(bf16)

    def folded_chunk(step):
        return lax.dynamic_slice(folded, ((x ^ step) * rows, 0), (rows, line))

    back_rows = exchange_x(folded_chunk)
    schur_rows, narrow = kernel_call(
        schur_kernel,
        place,
        [separator_rows] + back_rows,
        [shape((rows, nodes), f32), shape((rows, nodes), bf16)],
    )
    sweep, residual = kernel_call(
        finish_kernel,
        place,
        [narrow, weight_row[None, :]] + last,
        [shape((keys, rows), f32)] * 2,
        flops=2 * keys * rows * nodes,
    )
    return schur_rows[None], sweep[None], residual[None]


def solution(mesh):
    in_specs = (
        P("tm", "blk", None),
        P("tm", "blk", None),
        P("tm", "blk", None),
        P("tm", "blk", None),
        P("tm", None, "blk"),
        P("tm", "blk"),
    )
    out_specs = (P("tm", "blk", None), P("tm", None, "blk"), P("tm", None, "blk"))
    return jax.shard_map(shards, mesh=mesh, in_specs=in_specs, out_specs=out_specs, check_vma=False)
```

```python
import jax
import jax.numpy as jnp
from jax import lax
from jax.experimental import pallas as pl
from jax.experimental.pallas import tpu as pltpu
from jax.sharding import PartitionSpec as P

AXES = ("tm", "blk")
SIDE = 4
PLANE = SIDE * SIDE
PARTITIONS = 16
f32, bf16 = jnp.float32, jnp.bfloat16


def partner(p, y):
    return y ^ 1 if p % 2 == 0 else y ^ 3


def other(p, y):
    return y ^ 3 if p % 2 == 0 else y ^ 1


def permuted(value, rule, partitions=range(PARTITIONS)):
    pairs = []
    for p in partitions:
        for b in range(PLANE):
            target, y, x = rule(p, *divmod(b, SIDE))
            pairs.append((p * PLANE + b, target * PLANE + y * SIDE + x))
    return lax.ppermute(value, AXES, pairs)


def along_x(value, step):
    return permuted(value, lambda p, y, x: (p, y, x ^ step))


def along_y(value, step):
    return permuted(value, lambda p, y, x: (p, y ^ step, x))


def turn_messages(message, last):
    if last % 2 == 0:
        far = permuted(message, lambda p, y, x: (p ^ 1, y ^ 1, x))
        near = permuted(message, lambda p, y, x: (p ^ 1, y, x))
    else:
        far = permuted(message, lambda p, y, x: (p + 1, partner(p, y), x), [last])
        near = permuted(message, lambda p, y, x: (p + 1, y, x), [last])
    return far, near


def tie(values, *others):
    return lax.optimization_barrier((values, others))[0]


def kernel_call(body, place, operands, out_shapes, flops=0):
    out_bytes = sum(s.size * s.dtype.itemsize for s in out_shapes)
    in_bytes = sum(o.size * o.dtype.itemsize for o in operands)
    whole = pl.BlockSpec(memory_space=pltpu.VMEM)
    return pl.pallas_call(
        body,
        out_shape=out_shapes,
        in_specs=[pl.BlockSpec(memory_space=pltpu.SMEM)] + [whole] * len(operands),
        out_specs=[whole] * len(out_shapes),
        compiler_params=pltpu.CompilerParams(vmem_limit_bytes=24 * 1024 * 1024),
        cost_estimate=pl.CostEstimate(
            flops=flops, bytes_accessed=in_bytes + out_bytes, transcendentals=0
        ),
    )(place, *operands)


def block_of(index, size):
    return pl.ds(pl.multiple_of(index * size, size), size)


def split_link(place, link, keep, give):
    size = keep.shape[1] // 2
    for half in range(2):
        keep[:, half * size : (half + 1) * size] = link[:, block_of(place[half], size)]
        give[:, half * size : (half + 1) * size] = link[:, block_of(place[2 + half], size)]


def assemble_link(place, *refs):
    *pieces, out = refs
    size = pieces[0].shape[0] // 2
    for step in range(SIDE):
        for half in range(2):
            out[block_of(half * SIDE + (place[0] ^ step), size), :] = pieces[step][
                half * size : (half + 1) * size, :
            ]


def inner_kernel(place, first, second, out):
    def multiply(left, right):
        out[...] = lax.dot_general(
            left[...], right[...], (((1,), (1,)), ((), ())), preferred_element_type=f32
        ).astype(bf16)

    pl.when(place[0] == 1)(lambda: multiply(second, first))
    pl.when(place[0] == 0)(lambda: multiply(first, second))


def schur_kernel(place, *refs):
    separator, *pieces, schur, narrow = refs
    size = schur.shape[0]
    for step in range(SIDE):
        for k in range(SIDE):
            columns = block_of(k * place[1] + (place[0] ^ step) * place[2], size)
            value = separator[:, columns] - pieces[step][:, k * size : (k + 1) * size].astype(f32)
            schur[:, columns] = value
            narrow[:, columns] = value.astype(bf16)


def finish_kernel(place, narrow, weight, *refs):
    *pieces, sweep, residual = refs
    rows, nodes = narrow.shape
    share = pieces[0].shape[0]
    iterate = jnp.concatenate([piece[:, :nodes] for piece in pieces], axis=0)
    terms = lax.dot_general(
        iterate, narrow[...], (((1,), (1,)), ((), ())), preferred_element_type=f32
    )
    for step in range(SIDE):
        extra = [
            pieces[step][:, nodes + k * rows : nodes + (k + 1) * rows].astype(f32) for k in range(3)
        ]
        value = extra[1] + extra[2]
        target = block_of(place[0] ^ step, share)
        sweep[target, :] = value
        residual[target, :] = (
            value / weight[...] - terms[step * share : (step + 1) * share] - extra[0]
        )


def over_axis(array, axis):
    if axis == "x":
        groups = [[k * SIDE + i for i in range(SIDE)] for k in range(SIDE)]
    else:
        groups = [[i * SIDE + k for i in range(SIDE)] for k in range(SIDE)]
    return lax.all_gather(array, "blk", axis=0, tiled=True, axis_index_groups=groups)


def over_other(array):
    groups = []
    for p in range(PARTITIONS):
        for k in range(SIDE):
            if p % 2 == 0:
                groups.append([p * PLANE + i * SIDE + k for i in range(SIDE)])
            else:
                groups.append([p * PLANE + k * SIDE + i for i in range(SIDE)])
    return lax.all_gather(array, AXES, axis=0, tiled=True, axis_index_groups=groups)


def along_reduce(value, step):
    return permuted(
        value, lambda p, y, x: (p, y, x ^ step) if p % 2 == 0 else (p, y ^ step, x)
    )


def shards(interior_inverse, coupling, separator, link, source, weights):
    inverse_rows, coupling_rows, separator_rows = interior_inverse[0], coupling[0], separator[0]
    link_rows, source_rows, weight_row = link[0], source[0], weights[0]
    rows, nodes = link_rows.shape
    keys = source_rows.shape[0]
    share = keys // SIDE
    line = SIDE * rows
    half = 2 * line
    shape = jax.ShapeDtypeStruct
    p = lax.axis_index("tm").astype(jnp.int32)
    b = lax.axis_index("blk").astype(jnp.int32)
    y, x = b >> 2, b & 3
    even = (p & 1) == 0
    r = jnp.where(even, x, y)
    pair = y >> 1
    ring = ((y + 1) >> 1) & 1
    out_place = jnp.where(even, y & 1, pair)
    in_place = jnp.where(even, pair, y & 1)
    in_low = jnp.where(even, ring, 2 * pair)
    in_high = jnp.where(even, 3 - ring, 2 * pair + 1)
    away_low = jnp.where(even, 1 - ring, 2 - 2 * pair)
    away_high = jnp.where(even, 2 + ring, 3 - 2 * pair)
    place = jnp.stack([x, y])

    first = over_axis(jnp.where(even, coupling_rows, inverse_rows), "y")
    second = over_axis(jnp.where(even, inverse_rows, coupling_rows), "x")

    def ordered(pieces):
        stacked = jnp.stack(pieces)
        return [
            lax.dynamic_index_in_dim(stacked, x ^ k, 0, keepdims=False) for k in range(SIDE)
        ]

    def spread_x(array):
        return [array] + [along_x(array, step) for step in (1, 2, 3)]

    def exchange_x(chunk):
        return [chunk(0)] + [along_x(chunk(step), step) for step in (1, 2, 3)]

    keep, give = kernel_call(
        split_link,
        jnp.stack([in_low, in_high, away_low, away_high]),
        [link_rows],
        [shape((rows, half), bf16)] * 2,
    )
    got = permuted(give, lambda p, y, x: (p, partner(p, y), x))
    started = weight_row[None, :] * source_rows

    def source_chunk(step):
        part = lax.dynamic_slice(started, ((x ^ step) * share, 0), (share, rows))
        return jnp.concatenate([part, jnp.broadcast_to(weight_row[None, :], (8, rows))], axis=0)

    line_values = jnp.concatenate(ordered(exchange_x(source_chunk)), axis=1)
    keep, got, line_values = tie((keep, got, line_values))
    line_weights = line_values[share : share + 1]
    two = jnp.where(
        out_place == 0, jnp.concatenate([keep, got]), jnp.concatenate([got, keep])
    )
    pieces = spread_x(two)
    coupling_late = tie(coupling_rows, two)
    turned = jnp.where(
        even,
        coupling_late,
        coupling_late.reshape(rows, SIDE, SIDE, rows).transpose(0, 2, 1, 3).reshape(rows, nodes),
    )
    away_weights = permuted(line_weights, lambda p, y, x: (p, partner(p, y), x))
    (block,) = kernel_call(assemble_link, place, pieces, [shape((half, half), bf16)])
    weight_half = jnp.where(
        out_place == 0,
        jnp.concatenate([line_weights, away_weights], axis=1),
        jnp.concatenate([away_weights, line_weights], axis=1),
    )
    zeros = jnp.zeros((share, line), f32)
    own = jnp.where(
        out_place == 0,
        jnp.concatenate([line_values[:share], zeros], axis=1),
        jnp.concatenate([zeros, line_values[:share]], axis=1),
    )

    own = tie(own, turned)

    message = own.astype(bf16)
    final = message
    for turn in range(1, PARTITIONS):
        far, near = turn_messages(message, turn - 1)
        previous = (far.astype(f32) + near.astype(f32)).astype(bf16)
        if turn == 8:
            first, second = tie((first, second), message)
            (inner,) = kernel_call(
                inner_kernel,
                jnp.stack([even.astype(jnp.int32)]),
                [first, second],
                [shape((line, line), bf16)],
                flops=2 * line * line * nodes,
            )
            inner_all = over_other(inner)
            previous = tie(previous, inner)
        if turn == 12:
            turned = tie(turned, message)
            coupling_out = [turned] + [along_reduce(turned, step) for step in (1, 2, 3)]
        if turn == 14:
            previous = tie(previous, coupling_out)
        if turn == 15:
            previous = tie(previous, inner_all)
        product = lax.dot_general(
            previous, block, (((1,), (1,)), ((), ())), preferred_element_type=f32
        )
        message = (own - weight_half * product).astype(bf16)
        final = jnp.where(p == turn, message, final)

    total = final.astype(f32) + permuted(
        final, lambda p, y, x: (p, partner(p, y), x)
    ).astype(f32)
    folded = jnp.dot(
        jnp.concatenate(coupling_out), inner_all, preferred_element_type=f32
    ).astype(bf16)
    back_rows = [folded[:rows]] + [
        along_reduce(folded[step * rows : (step + 1) * rows], step) for step in (1, 2, 3)
    ]
    rounded = tie(total.astype(bf16), folded)

    back = jnp.dot(rounded, block, preferred_element_type=f32).astype(bf16)
    mine = lax.dynamic_slice(back, (0, in_place * line), (share, line))
    theirs = lax.dynamic_slice(back, (0, (1 - in_place) * line), (share, line))
    later = range(1, PARTITIONS)
    following = permuted(
        theirs, lambda p, y, x: (p - 1, other(p, y), x), later
    ).astype(f32) + permuted(mine, lambda p, y, x: (p - 1, y, x), later).astype(f32)
    following = following.astype(bf16)

    rest = permuted(rounded, lambda p, y, x: (p, other(p, y), x))
    m0, m1, r0, r1 = rounded[:, :line], rounded[:, line:], rest[:, :line], rest[:, line:]
    lines = jnp.where(
        even,
        jnp.where(
            pair == 0,
            jnp.concatenate([m0, m1, r0, r1], axis=1),
            jnp.concatenate([r0, r1, m0, m1], axis=1),
        ),
        jnp.where(
            ring == 0,
            jnp.concatenate([m0, r0, r1, m1], axis=1),
            jnp.concatenate([r0, m0, m1, r1], axis=1),
        ),
    )
    sweep_line = lax.dynamic_slice(total, (0, out_place * line), (share, line))
    sweep_high = sweep_line.astype(bf16)
    sweep_low = (sweep_line - sweep_high.astype(f32)).astype(bf16)

    def last_chunk(step):
        start = (0, (x ^ step) * rows)
        extra = [
            lax.dynamic_slice(array, start, (share, rows))
            for array in (following, sweep_high, sweep_low)
        ]
        return jnp.concatenate([lines] + extra, axis=1)

    lines = tie(lines, back_rows)
    last = exchange_x(last_chunk)

    schur_rows, narrow = kernel_call(
        schur_kernel,
        jnp.stack([r, jnp.where(even, SIDE, 1), jnp.where(even, 1, SIDE)]),
        [separator_rows] + back_rows,
        [shape((rows, nodes), f32), shape((rows, nodes), bf16)],
    )
    sweep, residual = kernel_call(
        finish_kernel,
        place,
        [narrow, weight_row[None, :]] + last,
        [shape((keys, rows), f32)] * 2,
        flops=2 * keys * rows * nodes,
    )
    return schur_rows[None], sweep[None], residual[None]


def solution(mesh):
    in_specs = (
        P("tm", "blk", None),
        P("tm", "blk", None),
        P("tm", "blk", None),
        P("tm", "blk", None),
        P("tm", None, "blk"),
        P("tm", "blk"),
    )
    out_specs = (P("tm", "blk", None), P("tm", None, "blk"), P("tm", None, "blk"))
    return jax.shard_map(shards, mesh=mesh, in_specs=in_specs, out_specs=out_specs, check_vma=False)
```

```python
import jax
import jax.numpy as jnp
from jax import lax
from jax.experimental import pallas as pl
from jax.experimental.pallas import tpu as pltpu
from jax.sharding import PartitionSpec as P

AXES = ("tm", "blk")
SIDE = 4
PLANE = SIDE * SIDE
PARTITIONS = 16
f32, bf16 = jnp.float32, jnp.bfloat16


def partner(p, y):
    return y ^ 1 if p % 2 == 0 else y ^ 3


def other(p, y):
    return y ^ 3 if p % 2 == 0 else y ^ 1


def permuted(value, rule, partitions=range(PARTITIONS)):
    pairs = []
    for p in partitions:
        for b in range(PLANE):
            target, y, x = rule(p, *divmod(b, SIDE))
            pairs.append((p * PLANE + b, target * PLANE + y * SIDE + x))
    return lax.ppermute(value, AXES, pairs)


def along_x(value, step):
    return permuted(value, lambda p, y, x: (p, y, x ^ step))


def along_y(value, step):
    return permuted(value, lambda p, y, x: (p, y ^ step, x))


def turn_messages(message, last):
    if last % 2 == 0:
        far = permuted(message, lambda p, y, x: (p ^ 1, y ^ 1, x))
        near = permuted(message, lambda p, y, x: (p ^ 1, y, x))
    else:
        far = permuted(message, lambda p, y, x: (p + 1, partner(p, y), x), [last])
        near = permuted(message, lambda p, y, x: (p + 1, y, x), [last])
    return far, near


def tie(values, *others):
    return lax.optimization_barrier((values, others))[0]


def kernel_call(body, place, operands, out_shapes, flops=0, space=pltpu.VMEM, scratch=()):
    out_bytes = sum(s.size * s.dtype.itemsize for s in out_shapes)
    in_bytes = sum(o.size * o.dtype.itemsize for o in operands)
    whole = pl.BlockSpec(memory_space=pltpu.VMEM)
    return pl.pallas_call(
        body,
        out_shape=out_shapes,
        in_specs=[pl.BlockSpec(memory_space=pltpu.SMEM)]
        + [pl.BlockSpec(memory_space=space)] * len(operands),
        out_specs=[whole] * len(out_shapes),
        scratch_shapes=scratch,
        compiler_params=pltpu.CompilerParams(vmem_limit_bytes=24 * 1024 * 1024),
        cost_estimate=pl.CostEstimate(
            flops=flops, bytes_accessed=in_bytes + out_bytes, transcendentals=0
        ),
    )(place, *operands)


def block_of(index, size):
    return pl.ds(pl.multiple_of(index * size, size), size)


def split_link(place, link, keep, give):
    size = keep.shape[1] // 2
    for half in range(2):
        keep[:, half * size : (half + 1) * size] = link[:, block_of(place[half], size)]
        give[:, half * size : (half + 1) * size] = link[:, block_of(place[2 + half], size)]


def assemble_link(place, *refs):
    pieces, out, sems = refs[:SIDE], refs[SIDE], refs[SIDE + 1]
    size = pieces[0].shape[0] // 2
    copies = []
    for step in range(SIDE):
        for half in range(2):
            copies.append(
                pltpu.make_async_copy(
                    pieces[step].at[half * size : (half + 1) * size, :],
                    out.at[block_of(half * SIDE + (place[0] ^ step), size), :],
                    sems.at[2 * step + half],
                )
            )
    for copy in copies:
        copy.start()
    for copy in copies:
        copy.wait()


def inner_kernel(place, first, second, out):
    def multiply(left, right):
        out[...] = lax.dot_general(
            left[...], right[...], (((1,), (1,)), ((), ())), preferred_element_type=f32
        ).astype(bf16)

    pl.when(place[0] == 1)(lambda: multiply(second, first))
    pl.when(place[0] == 0)(lambda: multiply(first, second))


def schur_kernel(place, *refs):
    separator, *pieces, schur, narrow = refs
    size = schur.shape[0]
    for step in range(SIDE):
        for k in range(SIDE):
            columns = block_of(k * place[1] + (place[0] ^ step) * place[2], size)
            value = separator[:, columns] - pieces[step][:, k * size : (k + 1) * size].astype(f32)
            schur[:, columns] = value
            narrow[:, columns] = value.astype(bf16)


def finish_kernel(place, narrow, weight, *refs):
    *pieces, sweep, residual = refs
    rows, nodes = narrow.shape
    share = pieces[0].shape[0]
    iterate = jnp.concatenate([piece[:, :nodes] for piece in pieces], axis=0)
    terms = lax.dot_general(
        iterate, narrow[...], (((1,), (1,)), ((), ())), preferred_element_type=f32
    )
    for step in range(SIDE):
        extra = [
            pieces[step][:, nodes + k * rows : nodes + (k + 1) * rows].astype(f32) for k in range(3)
        ]
        value = extra[1] + extra[2]
        target = block_of(place[0] ^ step, share)
        sweep[target, :] = value
        residual[target, :] = (
            value / weight[...] - terms[step * share : (step + 1) * share] - extra[0]
        )


def over_axis(array, axis):
    if axis == "x":
        groups = [[k * SIDE + i for i in range(SIDE)] for k in range(SIDE)]
    else:
        groups = [[i * SIDE + k for i in range(SIDE)] for k in range(SIDE)]
    return lax.all_gather(array, "blk", axis=0, tiled=True, axis_index_groups=groups)


def over_other(array):
    groups = []
    for p in range(PARTITIONS):
        for k in range(SIDE):
            if p % 2 == 0:
                groups.append([p * PLANE + i * SIDE + k for i in range(SIDE)])
            else:
                groups.append([p * PLANE + k * SIDE + i for i in range(SIDE)])
    return lax.all_gather(array, AXES, axis=0, tiled=True, axis_index_groups=groups)


def along_reduce(value, step):
    return permuted(
        value, lambda p, y, x: (p, y, x ^ step) if p % 2 == 0 else (p, y ^ step, x)
    )


def shards(interior_inverse, coupling, separator, link, source, weights):
    inverse_rows, coupling_rows, separator_rows = interior_inverse[0], coupling[0], separator[0]
    link_rows, source_rows, weight_row = link[0], source[0], weights[0]
    rows, nodes = link_rows.shape
    keys = source_rows.shape[0]
    share = keys // SIDE
    line = SIDE * rows
    half = 2 * line
    shape = jax.ShapeDtypeStruct
    p = lax.axis_index("tm").astype(jnp.int32)
    b = lax.axis_index("blk").astype(jnp.int32)
    y, x = b >> 2, b & 3
    even = (p & 1) == 0
    r = jnp.where(even, x, y)
    pair = y >> 1
    ring = ((y + 1) >> 1) & 1
    out_place = jnp.where(even, y & 1, pair)
    in_place = jnp.where(even, pair, y & 1)
    in_low = jnp.where(even, ring, 2 * pair)
    in_high = jnp.where(even, 3 - ring, 2 * pair + 1)
    away_low = jnp.where(even, 1 - ring, 2 - 2 * pair)
    away_high = jnp.where(even, 2 + ring, 3 - 2 * pair)
    place = jnp.stack([x, y])

    first = over_axis(jnp.where(even, coupling_rows, inverse_rows), "y")
    second = over_axis(jnp.where(even, inverse_rows, coupling_rows), "x")

    def ordered(pieces):
        stacked = jnp.stack(pieces)
        return [
            lax.dynamic_index_in_dim(stacked, x ^ k, 0, keepdims=False) for k in range(SIDE)
        ]

    def spread_x(array):
        return [array] + [along_x(array, step) for step in (1, 2, 3)]

    def exchange_x(chunk):
        return [chunk(0)] + [along_x(chunk(step), step) for step in (1, 2, 3)]

    keep, give = kernel_call(
        split_link,
        jnp.stack([in_low, in_high, away_low, away_high]),
        [link_rows],
        [shape((rows, half), bf16)] * 2,
    )
    got = permuted(give, lambda p, y, x: (p, partner(p, y), x))
    started = weight_row[None, :] * source_rows

    def source_chunk(step):
        part = lax.dynamic_slice(started, ((x ^ step) * share, 0), (share, rows))
        return jnp.concatenate([part, jnp.broadcast_to(weight_row[None, :], (8, rows))], axis=0)

    line_values = jnp.concatenate(ordered(exchange_x(source_chunk)), axis=1)
    keep, got, line_values = tie((keep, got, line_values))
    line_weights = line_values[share : share + 1]
    two = jnp.where(
        out_place == 0, jnp.concatenate([keep, got]), jnp.concatenate([got, keep])
    )
    pieces = spread_x(two)
    coupling_late = tie(coupling_rows, two)
    turned = jnp.where(
        even,
        coupling_late,
        coupling_late.reshape(rows, SIDE, SIDE, rows).transpose(0, 2, 1, 3).reshape(rows, nodes),
    )
    away_weights = permuted(line_weights, lambda p, y, x: (p, partner(p, y), x))
    (block,) = kernel_call(
        assemble_link,
        place,
        pieces,
        [shape((half, half), bf16)],
        space=pltpu.HBM,
        scratch=[pltpu.SemaphoreType.DMA((2 * SIDE,))],
    )
    weight_half = jnp.where(
        out_place == 0,
        jnp.concatenate([line_weights, away_weights], axis=1),
        jnp.concatenate([away_weights, line_weights], axis=1),
    )
    zeros = jnp.zeros((share, line), f32)
    own = jnp.where(
        out_place == 0,
        jnp.concatenate([line_values[:share], zeros], axis=1),
        jnp.concatenate([zeros, line_values[:share]], axis=1),
    )

    own = tie(own, turned)

    message = own.astype(bf16)
    final = message
    for turn in range(1, PARTITIONS):
        far, near = turn_messages(message, turn - 1)
        previous = (far.astype(f32) + near.astype(f32)).astype(bf16)
        if turn == 8:
            first, second = tie((first, second), message)
            (inner,) = kernel_call(
                inner_kernel,
                jnp.stack([even.astype(jnp.int32)]),
                [first, second],
                [shape((line, line), bf16)],
                flops=2 * line * line * nodes,
            )
            inner_all = over_other(inner)
            own = tie(own, inner)
        if turn == 10:
            turned = tie(turned, message)
            coupling_out = [turned] + [along_reduce(turned, step) for step in (1, 2, 3)]
        if turn == 12:
            own = tie(own, coupling_out)
        if turn == 15:
            own = tie(own, inner_all)
        product = lax.dot_general(
            previous, block, (((1,), (1,)), ((), ())), preferred_element_type=f32
        )
        message = (own - weight_half * product).astype(bf16)
        final = jnp.where(p == turn, message, final)

    total = final.astype(f32) + permuted(
        final, lambda p, y, x: (p, partner(p, y), x)
    ).astype(f32)
    folded = jnp.dot(
        jnp.concatenate(coupling_out), inner_all, preferred_element_type=f32
    ).astype(bf16)
    back_rows = [folded[:rows]] + [
        along_reduce(folded[step * rows : (step + 1) * rows], step) for step in (1, 2, 3)
    ]
    rounded = tie(total.astype(bf16), folded)

    back = jnp.dot(rounded, block, preferred_element_type=f32).astype(bf16)
    mine = lax.dynamic_slice(back, (0, in_place * line), (share, line))
    theirs = lax.dynamic_slice(back, (0, (1 - in_place) * line), (share, line))
    later = range(1, PARTITIONS)
    following = permuted(
        theirs, lambda p, y, x: (p - 1, other(p, y), x), later
    ).astype(f32) + permuted(mine, lambda p, y, x: (p - 1, y, x), later).astype(f32)
    following = following.astype(bf16)

    rest = permuted(rounded, lambda p, y, x: (p, other(p, y), x))
    m0, m1, r0, r1 = rounded[:, :line], rounded[:, line:], rest[:, :line], rest[:, line:]
    lines = jnp.where(
        even,
        jnp.where(
            pair == 0,
            jnp.concatenate([m0, m1, r0, r1], axis=1),
            jnp.concatenate([r0, r1, m0, m1], axis=1),
        ),
        jnp.where(
            ring == 0,
            jnp.concatenate([m0, r0, r1, m1], axis=1),
            jnp.concatenate([r0, m0, m1, r1], axis=1),
        ),
    )
    sweep_line = lax.dynamic_slice(total, (0, out_place * line), (share, line))
    sweep_high = sweep_line.astype(bf16)
    sweep_low = (sweep_line - sweep_high.astype(f32)).astype(bf16)

    def last_chunk(step):
        start = (0, (x ^ step) * rows)
        extra = [
            lax.dynamic_slice(array, start, (share, rows))
            for array in (following, sweep_high, sweep_low)
        ]
        return jnp.concatenate([lines] + extra, axis=1)

    lines = tie(lines, back_rows)
    last = exchange_x(last_chunk)

    schur_rows, narrow = kernel_call(
        schur_kernel,
        jnp.stack([r, jnp.where(even, SIDE, 1), jnp.where(even, 1, SIDE)]),
        [separator_rows] + back_rows,
        [shape((rows, nodes), f32), shape((rows, nodes), bf16)],
    )
    sweep, residual = kernel_call(
        finish_kernel,
        place,
        [narrow, weight_row[None, :]] + last,
        [shape((keys, rows), f32)] * 2,
        flops=2 * keys * rows * nodes,
    )
    return schur_rows[None], sweep[None], residual[None]


def solution(mesh):
    in_specs = (
        P("tm", "blk", None),
        P("tm", "blk", None),
        P("tm", "blk", None),
        P("tm", "blk", None),
        P("tm", None, "blk"),
        P("tm", "blk"),
    )
    out_specs = (P("tm", "blk", None), P("tm", None, "blk"), P("tm", None, "blk"))
    return jax.shard_map(shards, mesh=mesh, in_specs=in_specs, out_specs=out_specs, check_vma=False)
```

```python
import jax
import jax.numpy as jnp
from jax import lax
from jax.experimental import pallas as pl
from jax.experimental.pallas import tpu as pltpu
from jax.sharding import PartitionSpec as P

AXES = ("tm", "blk")
SIDE = 4
PLANE = SIDE * SIDE
PARTITIONS = 16
f32, bf16 = jnp.float32, jnp.bfloat16


def partner(p, y):
    return y ^ 1 if p % 2 == 0 else y ^ 3


def other(p, y):
    return y ^ 3 if p % 2 == 0 else y ^ 1


def permuted(value, rule, partitions=range(PARTITIONS)):
    pairs = []
    for p in partitions:
        for b in range(PLANE):
            target, y, x = rule(p, *divmod(b, SIDE))
            pairs.append((p * PLANE + b, target * PLANE + y * SIDE + x))
    return lax.ppermute(value, AXES, pairs)


def along_x(value, step):
    return permuted(value, lambda p, y, x: (p, y, x ^ step))


def along_y(value, step):
    return permuted(value, lambda p, y, x: (p, y ^ step, x))


def turn_messages(message, last):
    if last % 2 == 0:
        far = permuted(message, lambda p, y, x: (p ^ 1, y ^ 1, x))
        near = permuted(message, lambda p, y, x: (p ^ 1, y, x))
    else:
        far = permuted(message, lambda p, y, x: (p + 1, partner(p, y), x), [last])
        near = permuted(message, lambda p, y, x: (p + 1, y, x), [last])
    return far, near


def tie(values, *others):
    return lax.optimization_barrier((values, others))[0]


def kernel_call(body, place, operands, out_shapes, flops=0, space=pltpu.VMEM, scratch=()):
    out_bytes = sum(s.size * s.dtype.itemsize for s in out_shapes)
    in_bytes = sum(o.size * o.dtype.itemsize for o in operands)
    whole = pl.BlockSpec(memory_space=pltpu.VMEM)
    return pl.pallas_call(
        body,
        out_shape=out_shapes,
        in_specs=[pl.BlockSpec(memory_space=pltpu.SMEM)]
        + [pl.BlockSpec(memory_space=space)] * len(operands),
        out_specs=[whole] * len(out_shapes),
        scratch_shapes=scratch,
        compiler_params=pltpu.CompilerParams(vmem_limit_bytes=24 * 1024 * 1024),
        cost_estimate=pl.CostEstimate(
            flops=flops, bytes_accessed=in_bytes + out_bytes, transcendentals=0
        ),
    )(place, *operands)


def block_of(index, size):
    return pl.ds(pl.multiple_of(index * size, size), size)


def split_link(place, link, keep, give):
    size = keep.shape[1] // 2
    for half in range(2):
        keep[:, half * size : (half + 1) * size] = link[:, block_of(place[half], size)]
        give[:, half * size : (half + 1) * size] = link[:, block_of(place[2 + half], size)]


def assemble_link(place, *refs):
    pieces, out, sems = refs[:SIDE], refs[SIDE], refs[SIDE + 1]
    size = pieces[0].shape[0] // 2
    copies = []
    for step in range(SIDE):
        for half in range(2):
            copies.append(
                pltpu.make_async_copy(
                    pieces[step].at[half * size : (half + 1) * size, :],
                    out.at[block_of(half * SIDE + (place[0] ^ step), size), :],
                    sems.at[2 * step + half],
                )
            )
    for copy in copies:
        copy.start()
    for copy in copies:
        copy.wait()


def inner_kernel(place, first, second, out, left, right, sems):
    size = left.shape[0] // SIDE

    def multiply(rows_from, whole):
        copies = [pltpu.make_async_copy(whole, right, sems.at[SIDE])]
        for k in range(SIDE):
            rows = slice(k * size, (k + 1) * size)
            copies.append(
                pltpu.make_async_copy(rows_from.at[rows, :], left.at[rows, :], sems.at[k])
            )
        for copy in copies:
            copy.start()
        copies[0].wait()
        for k in range(SIDE):
            copies[k + 1].wait()
            rows = slice(k * size, (k + 1) * size)
            out[rows, :] = lax.dot_general(
                left[rows, :], right[...], (((1,), (1,)), ((), ())), preferred_element_type=f32
            ).astype(bf16)

    pl.when(place[0] == 1)(lambda: multiply(second, first))
    pl.when(place[0] == 0)(lambda: multiply(first, second))


def schur_kernel(place, *refs):
    separator, *pieces, schur, narrow = refs
    size = schur.shape[0]
    for step in range(SIDE):
        for k in range(SIDE):
            columns = block_of(k * place[1] + (place[0] ^ step) * place[2], size)
            value = separator[:, columns] - pieces[step][:, k * size : (k + 1) * size].astype(f32)
            schur[:, columns] = value
            narrow[:, columns] = value.astype(bf16)


def finish_kernel(place, narrow, weight, *refs):
    *pieces, sweep, residual = refs
    rows, nodes = narrow.shape
    share = pieces[0].shape[0]
    iterate = jnp.concatenate([piece[:, :nodes] for piece in pieces], axis=0)
    terms = lax.dot_general(
        iterate, narrow[...], (((1,), (1,)), ((), ())), preferred_element_type=f32
    )
    for step in range(SIDE):
        extra = [
            pieces[step][:, nodes + k * rows : nodes + (k + 1) * rows].astype(f32) for k in range(3)
        ]
        value = extra[1] + extra[2]
        target = block_of(place[0] ^ step, share)
        sweep[target, :] = value
        residual[target, :] = (
            value / weight[...] - terms[step * share : (step + 1) * share] - extra[0]
        )


def over_axis(array, axis):
    if axis == "x":
        groups = [[k * SIDE + i for i in range(SIDE)] for k in range(SIDE)]
    else:
        groups = [[i * SIDE + k for i in range(SIDE)] for k in range(SIDE)]
    return lax.all_gather(array, "blk", axis=0, tiled=True, axis_index_groups=groups)


def over_other(array):
    groups = []
    for p in range(PARTITIONS):
        for k in range(SIDE):
            if p % 2 == 0:
                groups.append([p * PLANE + i * SIDE + k for i in range(SIDE)])
            else:
                groups.append([p * PLANE + k * SIDE + i for i in range(SIDE)])
    return lax.all_gather(array, AXES, axis=0, tiled=True, axis_index_groups=groups)


def along_reduce(value, step):
    return permuted(
        value, lambda p, y, x: (p, y, x ^ step) if p % 2 == 0 else (p, y ^ step, x)
    )


def shards(interior_inverse, coupling, separator, link, source, weights):
    inverse_rows, coupling_rows, separator_rows = interior_inverse[0], coupling[0], separator[0]
    link_rows, source_rows, weight_row = link[0], source[0], weights[0]
    rows, nodes = link_rows.shape
    keys = source_rows.shape[0]
    share = keys // SIDE
    line = SIDE * rows
    half = 2 * line
    shape = jax.ShapeDtypeStruct
    p = lax.axis_index("tm").astype(jnp.int32)
    b = lax.axis_index("blk").astype(jnp.int32)
    y, x = b >> 2, b & 3
    even = (p & 1) == 0
    r = jnp.where(even, x, y)
    pair = y >> 1
    ring = ((y + 1) >> 1) & 1
    out_place = jnp.where(even, y & 1, pair)
    in_place = jnp.where(even, pair, y & 1)
    in_low = jnp.where(even, ring, 2 * pair)
    in_high = jnp.where(even, 3 - ring, 2 * pair + 1)
    away_low = jnp.where(even, 1 - ring, 2 - 2 * pair)
    away_high = jnp.where(even, 2 + ring, 3 - 2 * pair)
    place = jnp.stack([x, y])

    first = over_axis(jnp.where(even, coupling_rows, inverse_rows), "y")
    second = over_axis(jnp.where(even, inverse_rows, coupling_rows), "x")

    def ordered(pieces):
        stacked = jnp.stack(pieces)
        return [
            lax.dynamic_index_in_dim(stacked, x ^ k, 0, keepdims=False) for k in range(SIDE)
        ]

    def spread_x(array):
        return [array] + [along_x(array, step) for step in (1, 2, 3)]

    def exchange_x(chunk):
        return [chunk(0)] + [along_x(chunk(step), step) for step in (1, 2, 3)]

    keep, give = kernel_call(
        split_link,
        jnp.stack([in_low, in_high, away_low, away_high]),
        [link_rows],
        [shape((rows, half), bf16)] * 2,
    )
    got = permuted(give, lambda p, y, x: (p, partner(p, y), x))
    started = weight_row[None, :] * source_rows

    def source_chunk(step):
        part = lax.dynamic_slice(started, ((x ^ step) * share, 0), (share, rows))
        return jnp.concatenate([part, jnp.broadcast_to(weight_row[None, :], (8, rows))], axis=0)

    line_values = jnp.concatenate(ordered(exchange_x(source_chunk)), axis=1)
    keep, got, line_values = tie((keep, got, line_values))
    line_weights = line_values[share : share + 1]
    two = jnp.where(
        out_place == 0, jnp.concatenate([keep, got]), jnp.concatenate([got, keep])
    )
    pieces = spread_x(two)
    coupling_late = tie(coupling_rows, two)
    turned = jnp.where(
        even,
        coupling_late,
        coupling_late.reshape(rows, SIDE, SIDE, rows).transpose(0, 2, 1, 3).reshape(rows, nodes),
    )
    away_weights = permuted(line_weights, lambda p, y, x: (p, partner(p, y), x))
    (block,) = kernel_call(
        assemble_link,
        place,
        pieces,
        [shape((half, half), bf16)],
        space=pl.ANY,
        scratch=[pltpu.SemaphoreType.DMA((2 * SIDE,))],
    )
    weight_half = jnp.where(
        out_place == 0,
        jnp.concatenate([line_weights, away_weights], axis=1),
        jnp.concatenate([away_weights, line_weights], axis=1),
    )
    zeros = jnp.zeros((share, line), f32)
    own = jnp.where(
        out_place == 0,
        jnp.concatenate([line_values[:share], zeros], axis=1),
        jnp.concatenate([zeros, line_values[:share]], axis=1),
    )

    coupling_out = [turned] + [along_reduce(turned, step) for step in (1, 2, 3)]
    own = tie(own, coupling_out)

    message = own.astype(bf16)
    final = message
    for turn in range(1, PARTITIONS):
        far, near = turn_messages(message, turn - 1)
        previous = (far.astype(f32) + near.astype(f32)).astype(bf16)
        if turn == 8:
            first, second = tie((first, second), message)
            (inner,) = kernel_call(
                inner_kernel,
                jnp.stack([even.astype(jnp.int32)]),
                [first, second],
                [shape((line, line), bf16)],
                flops=2 * line * line * nodes,
                space=pltpu.HBM,
                scratch=[
                    pltpu.VMEM((line, nodes), bf16),
                    pltpu.VMEM((line, nodes), bf16),
                    pltpu.SemaphoreType.DMA((SIDE + 1,)),
                ],
            )
            inner_all = over_other(inner)
            own = tie(own, inner)
        if turn == 15:
            own = tie(own, inner_all)
        product = lax.dot_general(
            previous, block, (((1,), (1,)), ((), ())), preferred_element_type=f32
        )
        message = (own - weight_half * product).astype(bf16)
        final = jnp.where(p == turn, message, final)

    total = final.astype(f32) + permuted(
        final, lambda p, y, x: (p, partner(p, y), x)
    ).astype(f32)
    folded = jnp.dot(
        jnp.concatenate(coupling_out), inner_all, preferred_element_type=f32
    ).astype(bf16)
    rounded = total.astype(bf16)

    rest = permuted(rounded, lambda p, y, x: (p, other(p, y), x))

    back = jnp.dot(rounded, block, preferred_element_type=f32).astype(bf16)
    folded, back = tie((folded, back))
    back_rows = [folded[:rows]] + [
        along_reduce(folded[step * rows : (step + 1) * rows], step) for step in (1, 2, 3)
    ]
    mine = lax.dynamic_slice(back, (0, in_place * line), (share, line))
    theirs = lax.dynamic_slice(back, (0, (1 - in_place) * line), (share, line))
    later = range(1, PARTITIONS)
    following = permuted(
        theirs, lambda p, y, x: (p - 1, other(p, y), x), later
    ).astype(f32) + permuted(mine, lambda p, y, x: (p - 1, y, x), later).astype(f32)
    following = following.astype(bf16)

    m0, m1, r0, r1 = rounded[:, :line], rounded[:, line:], rest[:, :line], rest[:, line:]
    lines = jnp.where(
        even,
        jnp.where(
            pair == 0,
            jnp.concatenate([m0, m1, r0, r1], axis=1),
            jnp.concatenate([r0, r1, m0, m1], axis=1),
        ),
        jnp.where(
            ring == 0,
            jnp.concatenate([m0, r0, r1, m1], axis=1),
            jnp.concatenate([r0, m0, m1, r1], axis=1),
        ),
    )
    sweep_line = lax.dynamic_slice(total, (0, out_place * line), (share, line))
    sweep_high = sweep_line.astype(bf16)
    sweep_low = (sweep_line - sweep_high.astype(f32)).astype(bf16)

    def last_chunk(step):
        start = (0, (x ^ step) * rows)
        extra = [
            lax.dynamic_slice(array, start, (share, rows))
            for array in (following, sweep_high, sweep_low)
        ]
        return jnp.concatenate([lines] + extra, axis=1)

    lines = tie(lines, back_rows)
    last = exchange_x(last_chunk)

    schur_rows, narrow = kernel_call(
        schur_kernel,
        jnp.stack([r, jnp.where(even, SIDE, 1), jnp.where(even, 1, SIDE)]),
        [separator_rows] + back_rows,
        [shape((rows, nodes), f32), shape((rows, nodes), bf16)],
    )
    sweep, residual = kernel_call(
        finish_kernel,
        place,
        [narrow, weight_row[None, :]] + last,
        [shape((keys, rows), f32)] * 2,
        flops=2 * keys * rows * nodes,
    )
    return schur_rows[None], sweep[None], residual[None]


def solution(mesh):
    in_specs = (
        P("tm", "blk", None),
        P("tm", "blk", None),
        P("tm", "blk", None),
        P("tm", "blk", None),
        P("tm", None, "blk"),
        P("tm", "blk"),
    )
    out_specs = (P("tm", "blk", None), P("tm", None, "blk"), P("tm", None, "blk"))
    return jax.shard_map(shards, mesh=mesh, in_specs=in_specs, out_specs=out_specs, check_vma=False)
```

```python
import jax
import jax.numpy as jnp
from jax import lax
from jax.experimental import pallas as pl
from jax.experimental.pallas import tpu as pltpu
from jax.sharding import PartitionSpec as P

AXES = ("tm", "blk")
SIDE = 4
PLANE = SIDE * SIDE
PARTITIONS = 16
f32, bf16 = jnp.float32, jnp.bfloat16


def partner(p, y):
    return y ^ 1 if p % 2 == 0 else y ^ 3


def other(p, y):
    return y ^ 3 if p % 2 == 0 else y ^ 1


def permuted(value, rule, partitions=range(PARTITIONS)):
    pairs = []
    for p in partitions:
        for b in range(PLANE):
            target, y, x = rule(p, *divmod(b, SIDE))
            pairs.append((p * PLANE + b, target * PLANE + y * SIDE + x))
    return lax.ppermute(value, AXES, pairs)


def along_x(value, step):
    return permuted(value, lambda p, y, x: (p, y, x ^ step))


def along_y(value, step):
    return permuted(value, lambda p, y, x: (p, y ^ step, x))


def turn_messages(message, last):
    if last % 2 == 0:
        far = permuted(message, lambda p, y, x: (p ^ 1, y ^ 1, x))
        near = permuted(message, lambda p, y, x: (p ^ 1, y, x))
    else:
        far = permuted(message, lambda p, y, x: (p + 1, partner(p, y), x), [last])
        near = permuted(message, lambda p, y, x: (p + 1, y, x), [last])
    return far, near


def tie(values, *others):
    return lax.optimization_barrier((values, others))[0]


def kernel_call(body, place, operands, out_shapes, flops=0):
    out_bytes = sum(s.size * s.dtype.itemsize for s in out_shapes)
    in_bytes = sum(o.size * o.dtype.itemsize for o in operands)
    whole = pl.BlockSpec(memory_space=pltpu.VMEM)
    return pl.pallas_call(
        body,
        out_shape=out_shapes,
        in_specs=[pl.BlockSpec(memory_space=pltpu.SMEM)] + [whole] * len(operands),
        out_specs=[whole] * len(out_shapes),
        compiler_params=pltpu.CompilerParams(vmem_limit_bytes=24 * 1024 * 1024),
        cost_estimate=pl.CostEstimate(
            flops=flops, bytes_accessed=in_bytes + out_bytes, transcendentals=0
        ),
    )(place, *operands)


def block_of(index, size):
    return pl.ds(pl.multiple_of(index * size, size), size)


def split_link(place, link, keep, give):
    size = keep.shape[1] // 2
    for half in range(2):
        keep[:, half * size : (half + 1) * size] = link[:, block_of(place[half], size)]
        give[:, half * size : (half + 1) * size] = link[:, block_of(place[2 + half], size)]


def assemble_link(place, *refs):
    *pieces, out = refs
    size = pieces[0].shape[0]
    for step in range(SIDE):
        for half in range(2):
            target = block_of(half * SIDE + (place[0] ^ step), size)
            out[target, :] = pieces[2 * step + half][...]


def schur_kernel(place, *refs):
    separator, *pieces, schur, narrow = refs
    size = schur.shape[0]
    for step in range(SIDE):
        for k in range(SIDE):
            columns = block_of(k * place[1] + (place[0] ^ step) * place[2], size)
            value = separator[:, columns] - pieces[step][:, k * size : (k + 1) * size].astype(f32)
            schur[:, columns] = value
            narrow[:, columns] = value.astype(bf16)


def finish_kernel(place, narrow, weight, *refs):
    *pieces, sweep, residual = refs
    rows, nodes = narrow.shape
    share = pieces[0].shape[0]
    iterate = jnp.concatenate([piece[:, :nodes] for piece in pieces], axis=0)
    terms = lax.dot_general(
        iterate, narrow[...], (((1,), (1,)), ((), ())), preferred_element_type=f32
    )
    for step in range(SIDE):
        extra = [
            pieces[step][:, nodes + k * rows : nodes + (k + 1) * rows].astype(f32) for k in range(3)
        ]
        value = extra[1] + extra[2]
        target = block_of(place[0] ^ step, share)
        sweep[target, :] = value
        residual[target, :] = (
            value / weight[...] - terms[step * share : (step + 1) * share] - extra[0]
        )


def gather_groups(along_reduce):
    groups = []
    for p in range(PARTITIONS):
        for k in range(SIDE):
            if (p % 2 == 0) == along_reduce:
                groups.append([p * PLANE + k * SIDE + x for x in range(SIDE)])
            else:
                groups.append([p * PLANE + y * SIDE + k for y in range(SIDE)])
    return groups


def gathered(array, along_reduce):
    return lax.all_gather(
        array, AXES, axis=0, tiled=True, axis_index_groups=gather_groups(along_reduce)
    )


def along_reduce(value, step):
    return permuted(
        value, lambda p, y, x: (p, y, x ^ step) if p % 2 == 0 else (p, y ^ step, x)
    )


def shards(interior_inverse, coupling, separator, link, source, weights):
    inverse_rows, coupling_rows, separator_rows = interior_inverse[0], coupling[0], separator[0]
    link_rows, source_rows, weight_row = link[0], source[0], weights[0]
    rows, nodes = link_rows.shape
    keys = source_rows.shape[0]
    share = keys // SIDE
    line = SIDE * rows
    half = 2 * line
    shape = jax.ShapeDtypeStruct
    p = lax.axis_index("tm").astype(jnp.int32)
    b = lax.axis_index("blk").astype(jnp.int32)
    y, x = b >> 2, b & 3
    even = (p & 1) == 0
    r = jnp.where(even, x, y)
    pair = y >> 1
    ring = ((y + 1) >> 1) & 1
    out_place = jnp.where(even, y & 1, pair)
    in_place = jnp.where(even, pair, y & 1)
    in_low = jnp.where(even, ring, 2 * pair)
    in_high = jnp.where(even, 3 - ring, 2 * pair + 1)
    away_low = jnp.where(even, 1 - ring, 2 - 2 * pair)
    away_high = jnp.where(even, 2 + ring, 3 - 2 * pair)
    place = jnp.stack([x, y])

    coupling_in = gathered(coupling_rows, False)
    turned = jnp.where(
        even,
        coupling_rows,
        coupling_rows.reshape(rows, SIDE, SIDE, rows).transpose(0, 2, 1, 3).reshape(rows, nodes),
    )
    outer = gathered(jnp.concatenate([inverse_rows, turned], axis=1), True)

    def ordered(pieces):
        stacked = jnp.stack(pieces)
        return [
            lax.dynamic_index_in_dim(stacked, x ^ k, 0, keepdims=False) for k in range(SIDE)
        ]

    def spread_x(array):
        return [array] + [along_x(array, step) for step in (1, 2, 3)]

    def exchange_x(chunk):
        return [chunk(0)] + [along_x(chunk(step), step) for step in (1, 2, 3)]

    keep, give = kernel_call(
        split_link,
        jnp.stack([in_low, in_high, away_low, away_high]),
        [link_rows],
        [shape((rows, half), bf16)] * 2,
    )
    got = permuted(give, lambda p, y, x: (p, partner(p, y), x))
    started = weight_row[None, :] * source_rows

    def source_chunk(step):
        part = lax.dynamic_slice(started, ((x ^ step) * share, 0), (share, rows))
        return jnp.concatenate([part, jnp.broadcast_to(weight_row[None, :], (8, rows))], axis=0)

    line_values = jnp.concatenate(ordered(exchange_x(source_chunk)), axis=1)
    keep, got, line_values = tie((keep, got, line_values), turned)
    line_weights = line_values[share : share + 1]
    two = jnp.where(
        out_place == 0, jnp.concatenate([keep, got]), jnp.concatenate([got, keep])
    )
    left, right = along_x(two, 1), along_x(two, 3)
    pieces = [
        two[:rows],
        two[rows:],
        left[:rows],
        left[rows:],
        along_x(left[:rows], 3),
        along_x(right[rows:], 1),
        right[:rows],
        right[rows:],
    ]
    away_weights = permuted(line_weights, lambda p, y, x: (p, partner(p, y), x))
    (block,) = kernel_call(assemble_link, place, pieces, [shape((half, half), bf16)])
    weight_half = jnp.where(
        out_place == 0,
        jnp.concatenate([line_weights, away_weights], axis=1),
        jnp.concatenate([away_weights, line_weights], axis=1),
    )
    zeros = jnp.zeros((share, line), f32)
    own = jnp.where(
        out_place == 0,
        jnp.concatenate([line_values[:share], zeros], axis=1),
        jnp.concatenate([zeros, line_values[:share]], axis=1),
    )

    message = own.astype(bf16)
    final = message
    for turn in range(1, PARTITIONS):
        far, near = turn_messages(message, turn - 1)
        previous = (far.astype(f32) + near.astype(f32)).astype(bf16)
        if turn == 10:
            outer, coupling_in = tie((outer, coupling_in), message)
            inner = lax.dot_general(
                outer[:, :nodes], coupling_in, (((1,), (1,)), ((), ())), preferred_element_type=f32
            ).astype(bf16)
            inner_all = gathered(inner, False)
            previous = tie(previous, inner)
        product = lax.dot_general(
            previous, block, (((1,), (1,)), ((), ())), preferred_element_type=f32
        )
        message = (own - weight_half * product).astype(bf16)
        final = jnp.where(p == turn, message, final)

    total = final.astype(f32) + permuted(
        final, lambda p, y, x: (p, partner(p, y), x)
    ).astype(f32)
    rounded = total.astype(bf16)

    back = jnp.dot(rounded, block, preferred_element_type=f32)
    mine = lax.dynamic_slice(back, (0, in_place * line), (share, line))
    theirs = lax.dynamic_slice(back, (0, (1 - in_place) * line), (share, line)).astype(bf16)
    rest = permuted(
        jnp.concatenate([rounded, theirs], axis=1), lambda p, y, x: (p, other(p, y), x)
    )
    following = permuted(
        (mine + rest[:, half:].astype(f32)).astype(bf16),
        lambda p, y, x: (p - 1, y, x),
        range(1, PARTITIONS),
    )

    m0, m1, r0, r1 = rounded[:, :line], rounded[:, line:], rest[:, :line], rest[:, line:half]
    lines = jnp.where(
        even,
        jnp.where(
            pair == 0,
            jnp.concatenate([m0, m1, r0, r1], axis=1),
            jnp.concatenate([r0, r1, m0, m1], axis=1),
        ),
        jnp.where(
            ring == 0,
            jnp.concatenate([m0, r0, r1, m1], axis=1),
            jnp.concatenate([r0, m0, m1, r1], axis=1),
        ),
    )
    inner_all = tie(inner_all, rounded)
    folded = jnp.dot(outer[:, nodes:], inner_all, preferred_element_type=f32).astype(bf16)

    lines = tie(lines, folded)
    sweep_line = lax.dynamic_slice(total, (0, out_place * line), (share, line))
    sweep_high = sweep_line.astype(bf16)
    sweep_low = (sweep_line - sweep_high.astype(f32)).astype(bf16)

    def last_chunk(step):
        start = (0, (x ^ step) * rows)
        extra = [
            lax.dynamic_slice(array, start, (share, rows))
            for array in (following, sweep_high, sweep_low)
        ]
        return jnp.concatenate([lines] + extra, axis=1)

    last = exchange_x(last_chunk)

    def folded_chunk(step):
        return lax.dynamic_slice(folded, ((r ^ step) * rows, 0), (rows, line))

    back_rows = [folded_chunk(0)] + [along_reduce(folded_chunk(s), s) for s in (1, 2, 3)]
    schur_rows, narrow = kernel_call(
        schur_kernel,
        jnp.stack([r, jnp.where(even, SIDE, 1), jnp.where(even, 1, SIDE)]),
        [separator_rows] + back_rows,
        [shape((rows, nodes), f32), shape((rows, nodes), bf16)],
    )
    sweep, residual = kernel_call(
        finish_kernel,
        place,
        [narrow, weight_row[None, :]] + last,
        [shape((keys, rows), f32)] * 2,
        flops=2 * keys * rows * nodes,
    )
    return schur_rows[None], sweep[None], residual[None]


def solution(mesh):
    in_specs = (
        P("tm", "blk", None),
        P("tm", "blk", None),
        P("tm", "blk", None),
        P("tm", "blk", None),
        P("tm", None, "blk"),
        P("tm", "blk"),
    )
    out_specs = (P("tm", "blk", None), P("tm", None, "blk"), P("tm", None, "blk"))
    return jax.shard_map(shards, mesh=mesh, in_specs=in_specs, out_specs=out_specs, check_vma=False)
```

```python
import jax
import jax.numpy as jnp
from jax import lax
from jax.experimental import pallas as pl
from jax.experimental.pallas import tpu as pltpu
from jax.sharding import PartitionSpec as P

AXES = ("tm", "blk")
SIDE = 4
PLANE = SIDE * SIDE
PARTITIONS = 16
f32, bf16 = jnp.float32, jnp.bfloat16


def partner(p, y):
    return y ^ 1 if p % 2 == 0 else y ^ 3


def other(p, y):
    return y ^ 3 if p % 2 == 0 else y ^ 1


def permuted(value, rule, partitions=range(PARTITIONS)):
    pairs = []
    for p in partitions:
        for b in range(PLANE):
            target, y, x = rule(p, *divmod(b, SIDE))
            pairs.append((p * PLANE + b, target * PLANE + y * SIDE + x))
    return lax.ppermute(value, AXES, pairs)


def along_x(value, step):
    return permuted(value, lambda p, y, x: (p, y, x ^ step))


def along_y(value, step):
    return permuted(value, lambda p, y, x: (p, y ^ step, x))


def turn_messages(message, last):
    if last % 2 == 0:
        far = permuted(message, lambda p, y, x: (p ^ 1, y ^ 1, x))
        near = permuted(message, lambda p, y, x: (p ^ 1, y, x))
    else:
        far = permuted(message, lambda p, y, x: (p + 1, partner(p, y), x), [last])
        near = permuted(message, lambda p, y, x: (p + 1, y, x), [last])
    return far, near


def tie(values, *others):
    return lax.optimization_barrier((values, others))[0]


def kernel_call(body, place, operands, out_shapes, flops=0):
    out_bytes = sum(s.size * s.dtype.itemsize for s in out_shapes)
    in_bytes = sum(o.size * o.dtype.itemsize for o in operands)
    whole = pl.BlockSpec(memory_space=pltpu.VMEM)
    return pl.pallas_call(
        body,
        out_shape=out_shapes,
        in_specs=[pl.BlockSpec(memory_space=pltpu.SMEM)] + [whole] * len(operands),
        out_specs=[whole] * len(out_shapes),
        compiler_params=pltpu.CompilerParams(vmem_limit_bytes=24 * 1024 * 1024),
        cost_estimate=pl.CostEstimate(
            flops=flops, bytes_accessed=in_bytes + out_bytes, transcendentals=0
        ),
    )(place, *operands)


def block_of(index, size):
    return pl.ds(pl.multiple_of(index * size, size), size)


def split_link(place, link, keep, give):
    size = keep.shape[1] // 2
    for half in range(2):
        keep[:, half * size : (half + 1) * size] = link[:, block_of(place[half], size)]
        give[:, half * size : (half + 1) * size] = link[:, block_of(place[2 + half], size)]


def assemble_link(place, *refs):
    *pieces, out = refs
    size = pieces[0].shape[0]
    for step in range(SIDE):
        for half in range(2):
            target = block_of(half * SIDE + (place[0] ^ step), size)
            out[target, :] = pieces[2 * step + half][...]


def schur_kernel(place, *refs):
    separator, *pieces, schur, narrow = refs
    size = schur.shape[0]
    for step in range(SIDE):
        for k in range(SIDE):
            columns = block_of(k * place[1] + (place[0] ^ step) * place[2], size)
            value = separator[:, columns] - pieces[step][:, k * size : (k + 1) * size].astype(f32)
            schur[:, columns] = value
            narrow[:, columns] = value.astype(bf16)


def finish_kernel(place, narrow, weight, *refs):
    *pieces, sweep, residual = refs
    rows, nodes = narrow.shape
    share = pieces[0].shape[0]
    iterate = jnp.concatenate([piece[:, :nodes] for piece in pieces], axis=0)
    terms = lax.dot_general(
        iterate, narrow[...], (((1,), (1,)), ((), ())), preferred_element_type=f32
    )
    for step in range(SIDE):
        extra = [
            pieces[step][:, nodes + k * rows : nodes + (k + 1) * rows].astype(f32) for k in range(3)
        ]
        value = extra[1] + extra[2]
        target = block_of(place[0] ^ step, share)
        sweep[target, :] = value
        residual[target, :] = (
            value / weight[...] - terms[step * share : (step + 1) * share] - extra[0]
        )


def gather_groups(along_reduce):
    groups = []
    for p in range(PARTITIONS):
        for k in range(SIDE):
            if (p % 2 == 0) == along_reduce:
                groups.append([p * PLANE + k * SIDE + x for x in range(SIDE)])
            else:
                groups.append([p * PLANE + y * SIDE + k for y in range(SIDE)])
    return groups


def gathered(array, along_reduce):
    return lax.all_gather(
        array, AXES, axis=0, tiled=True, axis_index_groups=gather_groups(along_reduce)
    )


def along_reduce(value, step):
    return permuted(
        value, lambda p, y, x: (p, y, x ^ step) if p % 2 == 0 else (p, y ^ step, x)
    )


def shards(interior_inverse, coupling, separator, link, source, weights):
    inverse_rows, coupling_rows, separator_rows = interior_inverse[0], coupling[0], separator[0]
    link_rows, source_rows, weight_row = link[0], source[0], weights[0]
    rows, nodes = link_rows.shape
    keys = source_rows.shape[0]
    share = keys // SIDE
    line = SIDE * rows
    half = 2 * line
    shape = jax.ShapeDtypeStruct
    p = lax.axis_index("tm").astype(jnp.int32)
    b = lax.axis_index("blk").astype(jnp.int32)
    y, x = b >> 2, b & 3
    even = (p & 1) == 0
    r = jnp.where(even, x, y)
    pair = y >> 1
    ring = ((y + 1) >> 1) & 1
    out_place = jnp.where(even, y & 1, pair)
    in_place = jnp.where(even, pair, y & 1)
    in_low = jnp.where(even, ring, 2 * pair)
    in_high = jnp.where(even, 3 - ring, 2 * pair + 1)
    away_low = jnp.where(even, 1 - ring, 2 - 2 * pair)
    away_high = jnp.where(even, 2 + ring, 3 - 2 * pair)
    place = jnp.stack([x, y])

    coupling_in = gathered(coupling_rows, False)

    def ordered(pieces):
        stacked = jnp.stack(pieces)
        return [
            lax.dynamic_index_in_dim(stacked, x ^ k, 0, keepdims=False) for k in range(SIDE)
        ]

    def spread_x(array):
        return [array] + [along_x(array, step) for step in (1, 2, 3)]

    def exchange_x(chunk):
        return [chunk(0)] + [along_x(chunk(step), step) for step in (1, 2, 3)]

    keep, give = kernel_call(
        split_link,
        jnp.stack([in_low, in_high, away_low, away_high]),
        [link_rows],
        [shape((rows, half), bf16)] * 2,
    )
    got = permuted(give, lambda p, y, x: (p, partner(p, y), x))
    started = weight_row[None, :] * source_rows

    def source_chunk(step):
        part = lax.dynamic_slice(started, ((x ^ step) * share, 0), (share, rows))
        return jnp.concatenate([part, jnp.broadcast_to(weight_row[None, :], (8, rows))], axis=0)

    line_values = jnp.concatenate(ordered(exchange_x(source_chunk)), axis=1)
    keep, got, line_values = tie((keep, got, line_values))
    line_weights = line_values[share : share + 1]
    two = jnp.where(
        out_place == 0, jnp.concatenate([keep, got]), jnp.concatenate([got, keep])
    )
    coupling_late = tie(coupling_rows, two)
    turned = jnp.where(
        even,
        coupling_late,
        coupling_late.reshape(rows, SIDE, SIDE, rows).transpose(0, 2, 1, 3).reshape(rows, nodes),
    )
    outer = gathered(jnp.concatenate([inverse_rows, turned], axis=1), True)
    left, right = along_x(two, 1), along_x(two, 3)
    pieces = [
        two[:rows],
        two[rows:],
        left[:rows],
        left[rows:],
        along_x(left[:rows], 3),
        along_x(right[rows:], 1),
        right[:rows],
        right[rows:],
    ]
    away_weights = permuted(line_weights, lambda p, y, x: (p, partner(p, y), x))
    (block,) = kernel_call(assemble_link, place, pieces, [shape((half, half), bf16)])
    weight_half = jnp.where(
        out_place == 0,
        jnp.concatenate([line_weights, away_weights], axis=1),
        jnp.concatenate([away_weights, line_weights], axis=1),
    )
    zeros = jnp.zeros((share, line), f32)
    own = jnp.where(
        out_place == 0,
        jnp.concatenate([line_values[:share], zeros], axis=1),
        jnp.concatenate([zeros, line_values[:share]], axis=1),
    )

    own = tie(own, turned)

    message = own.astype(bf16)
    final = message
    for turn in range(1, PARTITIONS):
        far, near = turn_messages(message, turn - 1)
        previous = (far.astype(f32) + near.astype(f32)).astype(bf16)
        if turn == 10:
            outer, coupling_in = tie((outer, coupling_in), message)
            inner = lax.dot_general(
                outer[:, :nodes], coupling_in, (((1,), (1,)), ((), ())), preferred_element_type=f32
            ).astype(bf16)
            inner_all = gathered(inner, False)
            own = tie(own, inner)
        product = lax.dot_general(
            previous, block, (((1,), (1,)), ((), ())), preferred_element_type=f32
        )
        message = (own - weight_half * product).astype(bf16)
        final = jnp.where(p == turn, message, final)

    total = final.astype(f32) + permuted(
        final, lambda p, y, x: (p, partner(p, y), x)
    ).astype(f32)
    rounded = total.astype(bf16)

    back = jnp.dot(rounded, block, preferred_element_type=f32)
    mine = lax.dynamic_slice(back, (0, in_place * line), (share, line))
    theirs = lax.dynamic_slice(back, (0, (1 - in_place) * line), (share, line)).astype(bf16)
    rest = permuted(
        jnp.concatenate([rounded, theirs], axis=1), lambda p, y, x: (p, other(p, y), x)
    )
    following = permuted(
        (mine + rest[:, half:].astype(f32)).astype(bf16),
        lambda p, y, x: (p - 1, y, x),
        range(1, PARTITIONS),
    )

    m0, m1, r0, r1 = rounded[:, :line], rounded[:, line:], rest[:, :line], rest[:, line:half]
    lines = jnp.where(
        even,
        jnp.where(
            pair == 0,
            jnp.concatenate([m0, m1, r0, r1], axis=1),
            jnp.concatenate([r0, r1, m0, m1], axis=1),
        ),
        jnp.where(
            ring == 0,
            jnp.concatenate([m0, r0, r1, m1], axis=1),
            jnp.concatenate([r0, m0, m1, r1], axis=1),
        ),
    )
    inner_all = tie(inner_all, rounded)
    folded = jnp.dot(outer[:, nodes:], inner_all, preferred_element_type=f32).astype(bf16)

    lines = tie(lines, folded)
    sweep_line = lax.dynamic_slice(total, (0, out_place * line), (share, line))
    sweep_high = sweep_line.astype(bf16)
    sweep_low = (sweep_line - sweep_high.astype(f32)).astype(bf16)

    def last_chunk(step):
        start = (0, (x ^ step) * rows)
        extra = [
            lax.dynamic_slice(array, start, (share, rows))
            for array in (following, sweep_high, sweep_low)
        ]
        return jnp.concatenate([lines] + extra, axis=1)

    last = exchange_x(last_chunk)

    def folded_chunk(step):
        return lax.dynamic_slice(folded, ((r ^ step) * rows, 0), (rows, line))

    back_rows = [folded_chunk(0)] + [along_reduce(folded_chunk(s), s) for s in (1, 2, 3)]
    schur_rows, narrow = kernel_call(
        schur_kernel,
        jnp.stack([r, jnp.where(even, SIDE, 1), jnp.where(even, 1, SIDE)]),
        [separator_rows] + back_rows,
        [shape((rows, nodes), f32), shape((rows, nodes), bf16)],
    )
    sweep, residual = kernel_call(
        finish_kernel,
        place,
        [narrow, weight_row[None, :]] + last,
        [shape((keys, rows), f32)] * 2,
        flops=2 * keys * rows * nodes,
    )
    return schur_rows[None], sweep[None], residual[None]


def solution(mesh):
    in_specs = (
        P("tm", "blk", None),
        P("tm", "blk", None),
        P("tm", "blk", None),
        P("tm", "blk", None),
        P("tm", None, "blk"),
        P("tm", "blk"),
    )
    out_specs = (P("tm", "blk", None), P("tm", None, "blk"), P("tm", None, "blk"))
    return jax.shard_map(shards, mesh=mesh, in_specs=in_specs, out_specs=out_specs, check_vma=False)
```

```python
import jax
import jax.numpy as jnp
from jax import lax
from jax.experimental import pallas as pl
from jax.experimental.pallas import tpu as pltpu
from jax.sharding import PartitionSpec as P

AXES = ("tm", "blk")
SIDE = 4
PLANE = SIDE * SIDE
PARTITIONS = 16
f32, bf16 = jnp.float32, jnp.bfloat16


def partner(p, y):
    return y ^ 1 if p % 2 == 0 else y ^ 3


def other(p, y):
    return y ^ 3 if p % 2 == 0 else y ^ 1


def permuted(value, rule, partitions=range(PARTITIONS)):
    pairs = []
    for p in partitions:
        for b in range(PLANE):
            target, y, x = rule(p, *divmod(b, SIDE))
            pairs.append((p * PLANE + b, target * PLANE + y * SIDE + x))
    return lax.ppermute(value, AXES, pairs)


def along_x(value, step):
    return permuted(value, lambda p, y, x: (p, y, x ^ step))


def along_y(value, step):
    return permuted(value, lambda p, y, x: (p, y ^ step, x))


def turn_messages(message, last):
    if last % 2 == 0:
        far = permuted(message, lambda p, y, x: (p ^ 1, y ^ 1, x))
        near = permuted(message, lambda p, y, x: (p ^ 1, y, x))
    else:
        far = permuted(message, lambda p, y, x: (p + 1, partner(p, y), x), [last])
        near = permuted(message, lambda p, y, x: (p + 1, y, x), [last])
    return far, near


def tie(values, *others):
    return lax.optimization_barrier((values, others))[0]


def kernel_call(body, place, operands, out_shapes, flops=0):
    out_bytes = sum(s.size * s.dtype.itemsize for s in out_shapes)
    in_bytes = sum(o.size * o.dtype.itemsize for o in operands)
    whole = pl.BlockSpec(memory_space=pltpu.VMEM)
    return pl.pallas_call(
        body,
        out_shape=out_shapes,
        in_specs=[pl.BlockSpec(memory_space=pltpu.SMEM)] + [whole] * len(operands),
        out_specs=[whole] * len(out_shapes),
        compiler_params=pltpu.CompilerParams(vmem_limit_bytes=24 * 1024 * 1024),
        cost_estimate=pl.CostEstimate(
            flops=flops, bytes_accessed=in_bytes + out_bytes, transcendentals=0
        ),
    )(place, *operands)


def block_of(index, size):
    return pl.ds(pl.multiple_of(index * size, size), size)


def split_link(place, link, keep, give):
    size = keep.shape[1] // 2
    for half in range(2):
        keep[:, half * size : (half + 1) * size] = link[:, block_of(place[half], size)]
        give[:, half * size : (half + 1) * size] = link[:, block_of(place[2 + half], size)]


def assemble_link(place, *refs):
    *pieces, out = refs
    size = pieces[0].shape[0]
    for step in range(SIDE):
        for half in range(2):
            target = block_of(half * SIDE + (place[0] ^ step), size)
            out[target, :] = pieces[2 * step + half][...]


def schur_kernel(place, *refs):
    separator, *pieces, schur, narrow = refs
    size = schur.shape[0]
    for step in range(SIDE):
        for k in range(SIDE):
            columns = block_of(k * place[1] + (place[0] ^ step) * place[2], size)
            value = separator[:, columns] - pieces[step][:, k * size : (k + 1) * size].astype(f32)
            schur[:, columns] = value
            narrow[:, columns] = value.astype(bf16)


def finish_kernel(place, narrow, weight, *refs):
    *pieces, sweep, residual = refs
    rows, nodes = narrow.shape
    share = pieces[0].shape[0]
    iterate = jnp.concatenate([piece[:, :nodes] for piece in pieces], axis=0)
    terms = lax.dot_general(
        iterate, narrow[...], (((1,), (1,)), ((), ())), preferred_element_type=f32
    )
    for step in range(SIDE):
        extra = [
            pieces[step][:, nodes + k * rows : nodes + (k + 1) * rows].astype(f32) for k in range(3)
        ]
        value = extra[1] + extra[2]
        target = block_of(place[0] ^ step, share)
        sweep[target, :] = value
        residual[target, :] = (
            value / weight[...] - terms[step * share : (step + 1) * share] - extra[0]
        )


def gather_groups(along_reduce):
    groups = []
    for p in range(PARTITIONS):
        for k in range(SIDE):
            if (p % 2 == 0) == along_reduce:
                groups.append([p * PLANE + k * SIDE + x for x in range(SIDE)])
            else:
                groups.append([p * PLANE + y * SIDE + k for y in range(SIDE)])
    return groups


def gathered(array, along_reduce):
    return lax.all_gather(
        array, AXES, axis=0, tiled=True, axis_index_groups=gather_groups(along_reduce)
    )


def along_reduce(value, step):
    return permuted(
        value, lambda p, y, x: (p, y, x ^ step) if p % 2 == 0 else (p, y ^ step, x)
    )


def shards(interior_inverse, coupling, separator, link, source, weights):
    inverse_rows, coupling_rows, separator_rows = interior_inverse[0], coupling[0], separator[0]
    link_rows, source_rows, weight_row = link[0], source[0], weights[0]
    rows, nodes = link_rows.shape
    keys = source_rows.shape[0]
    share = keys // SIDE
    line = SIDE * rows
    half = 2 * line
    shape = jax.ShapeDtypeStruct
    p = lax.axis_index("tm").astype(jnp.int32)
    b = lax.axis_index("blk").astype(jnp.int32)
    y, x = b >> 2, b & 3
    even = (p & 1) == 0
    r = jnp.where(even, x, y)
    pair = y >> 1
    ring = ((y + 1) >> 1) & 1
    out_place = jnp.where(even, y & 1, pair)
    in_place = jnp.where(even, pair, y & 1)
    in_low = jnp.where(even, ring, 2 * pair)
    in_high = jnp.where(even, 3 - ring, 2 * pair + 1)
    away_low = jnp.where(even, 1 - ring, 2 - 2 * pair)
    away_high = jnp.where(even, 2 + ring, 3 - 2 * pair)
    place = jnp.stack([x, y])

    coupling_in = gathered(coupling_rows, False)

    def ordered(pieces):
        stacked = jnp.stack(pieces)
        return [
            lax.dynamic_index_in_dim(stacked, x ^ k, 0, keepdims=False) for k in range(SIDE)
        ]

    def spread_x(array):
        return [array] + [along_x(array, step) for step in (1, 2, 3)]

    def exchange_x(chunk):
        return [chunk(0)] + [along_x(chunk(step), step) for step in (1, 2, 3)]

    keep, give = kernel_call(
        split_link,
        jnp.stack([in_low, in_high, away_low, away_high]),
        [link_rows],
        [shape((rows, half), bf16)] * 2,
    )
    got = permuted(give, lambda p, y, x: (p, partner(p, y), x))
    started = weight_row[None, :] * source_rows

    def source_chunk(step):
        part = lax.dynamic_slice(started, ((x ^ step) * share, 0), (share, rows))
        return jnp.concatenate([part, jnp.broadcast_to(weight_row[None, :], (8, rows))], axis=0)

    line_values = jnp.concatenate(ordered(exchange_x(source_chunk)), axis=1)
    keep, got, line_values = tie((keep, got, line_values))
    line_weights = line_values[share : share + 1]
    two = jnp.where(
        out_place == 0, jnp.concatenate([keep, got]), jnp.concatenate([got, keep])
    )
    coupling_late = tie(coupling_rows, two)
    turned = jnp.where(
        even,
        coupling_late,
        coupling_late.reshape(rows, SIDE, SIDE, rows).transpose(0, 2, 1, 3).reshape(rows, nodes),
    )
    outer = gathered(jnp.concatenate([inverse_rows, turned], axis=1), True)
    left, right = along_x(two, 1), along_x(two, 3)
    pieces = [
        two[:rows],
        two[rows:],
        left[:rows],
        left[rows:],
        along_x(left[:rows], 3),
        along_x(right[rows:], 1),
        right[:rows],
        right[rows:],
    ]
    away_weights = permuted(line_weights, lambda p, y, x: (p, partner(p, y), x))
    (block,) = kernel_call(assemble_link, place, pieces, [shape((half, half), bf16)])
    weight_half = jnp.where(
        out_place == 0,
        jnp.concatenate([line_weights, away_weights], axis=1),
        jnp.concatenate([away_weights, line_weights], axis=1),
    )
    zeros = jnp.zeros((share, line), f32)
    own = jnp.where(
        out_place == 0,
        jnp.concatenate([line_values[:share], zeros], axis=1),
        jnp.concatenate([zeros, line_values[:share]], axis=1),
    )

    own = tie(own, turned)

    message = own.astype(bf16)
    final = message
    for turn in range(1, PARTITIONS):
        far, near = turn_messages(message, turn - 1)
        previous = (far.astype(f32) + near.astype(f32)).astype(bf16)
        if turn == 10:
            outer, coupling_in = tie((outer, coupling_in), message)
            inner = lax.dot_general(
                outer[:, :nodes], coupling_in, (((1,), (1,)), ((), ())), preferred_element_type=f32
            ).astype(bf16)
            inner_all = gathered(inner, False)
            own = tie(own, inner)
        product = lax.dot_general(
            previous, block, (((1,), (1,)), ((), ())), preferred_element_type=f32
        )
        message = (own - weight_half * product).astype(bf16)
        final = jnp.where(p == turn, message, final)

    total = final.astype(f32) + permuted(
        final, lambda p, y, x: (p, partner(p, y), x)
    ).astype(f32)
    rounded = total.astype(bf16)

    back = jnp.dot(rounded, block, preferred_element_type=f32)
    mine = lax.dynamic_slice(back, (0, in_place * line), (share, line))
    theirs = lax.dynamic_slice(back, (0, (1 - in_place) * line), (share, line)).astype(bf16)
    rest = permuted(
        jnp.concatenate([rounded, theirs], axis=1), lambda p, y, x: (p, other(p, y), x)
    )
    inner_all = tie(inner_all, rounded)
    folded = jnp.dot(outer[:, nodes:], inner_all, preferred_element_type=f32).astype(bf16)

    rest = tie(rest, folded)
    following = permuted(
        (mine + rest[:, half:].astype(f32)).astype(bf16),
        lambda p, y, x: (p - 1, y, x),
        range(1, PARTITIONS),
    )

    m0, m1, r0, r1 = rounded[:, :line], rounded[:, line:], rest[:, :line], rest[:, line:half]
    lines = jnp.where(
        even,
        jnp.where(
            pair == 0,
            jnp.concatenate([m0, m1, r0, r1], axis=1),
            jnp.concatenate([r0, r1, m0, m1], axis=1),
        ),
        jnp.where(
            ring == 0,
            jnp.concatenate([m0, r0, r1, m1], axis=1),
            jnp.concatenate([r0, m0, m1, r1], axis=1),
        ),
    )
    sweep_line = lax.dynamic_slice(total, (0, out_place * line), (share, line))
    sweep_high = sweep_line.astype(bf16)
    sweep_low = (sweep_line - sweep_high.astype(f32)).astype(bf16)

    def last_chunk(step):
        start = (0, (x ^ step) * rows)
        extra = [
            lax.dynamic_slice(array, start, (share, rows))
            for array in (following, sweep_high, sweep_low)
        ]
        return jnp.concatenate([lines] + extra, axis=1)

    last = exchange_x(last_chunk)

    def folded_chunk(step):
        return lax.dynamic_slice(folded, ((r ^ step) * rows, 0), (rows, line))

    back_rows = [folded_chunk(0)] + [along_reduce(folded_chunk(s), s) for s in (1, 2, 3)]
    schur_rows, narrow = kernel_call(
        schur_kernel,
        jnp.stack([r, jnp.where(even, SIDE, 1), jnp.where(even, 1, SIDE)]),
        [separator_rows] + back_rows,
        [shape((rows, nodes), f32), shape((rows, nodes), bf16)],
    )
    sweep, residual = kernel_call(
        finish_kernel,
        place,
        [narrow, weight_row[None, :]] + last,
        [shape((keys, rows), f32)] * 2,
        flops=2 * keys * rows * nodes,
    )
    return schur_rows[None], sweep[None], residual[None]


def solution(mesh):
    in_specs = (
        P("tm", "blk", None),
        P("tm", "blk", None),
        P("tm", "blk", None),
        P("tm", "blk", None),
        P("tm", None, "blk"),
        P("tm", "blk"),
    )
    out_specs = (P("tm", "blk", None), P("tm", None, "blk"), P("tm", None, "blk"))
    return jax.shard_map(shards, mesh=mesh, in_specs=in_specs, out_specs=out_specs, check_vma=False)
```

```python
import jax
import jax.numpy as jnp
from jax import lax
from jax.experimental import pallas as pl
from jax.experimental.pallas import tpu as pltpu
from jax.sharding import PartitionSpec as P

AXES = ("tm", "blk")
SIDE = 4
PLANE = SIDE * SIDE
PARTITIONS = 16
f32, bf16 = jnp.float32, jnp.bfloat16


def partner(p, y):
    return y ^ 1 if p % 2 == 0 else y ^ 3


def other(p, y):
    return y ^ 3 if p % 2 == 0 else y ^ 1


def permuted(value, rule, partitions=range(PARTITIONS)):
    pairs = []
    for p in partitions:
        for b in range(PLANE):
            target, y, x = rule(p, *divmod(b, SIDE))
            pairs.append((p * PLANE + b, target * PLANE + y * SIDE + x))
    return lax.ppermute(value, AXES, pairs)


def along_x(value, step):
    return permuted(value, lambda p, y, x: (p, y, x ^ step))


def along_y(value, step):
    return permuted(value, lambda p, y, x: (p, y ^ step, x))


def turn_messages(message, last):
    if last % 2 == 0:
        far = permuted(message, lambda p, y, x: (p ^ 1, y ^ 1, x))
        near = permuted(message, lambda p, y, x: (p ^ 1, y, x))
    else:
        far = permuted(message, lambda p, y, x: (p + 1, partner(p, y), x), [last])
        near = permuted(message, lambda p, y, x: (p + 1, y, x), [last])
    return far, near


def tie(values, *others):
    return lax.optimization_barrier((values, others))[0]


def kernel_call(body, place, operands, out_shapes, flops=0):
    out_bytes = sum(s.size * s.dtype.itemsize for s in out_shapes)
    in_bytes = sum(o.size * o.dtype.itemsize for o in operands)
    whole = pl.BlockSpec(memory_space=pltpu.VMEM)
    return pl.pallas_call(
        body,
        out_shape=out_shapes,
        in_specs=[pl.BlockSpec(memory_space=pltpu.SMEM)] + [whole] * len(operands),
        out_specs=[whole] * len(out_shapes),
        compiler_params=pltpu.CompilerParams(vmem_limit_bytes=24 * 1024 * 1024),
        cost_estimate=pl.CostEstimate(
            flops=flops, bytes_accessed=in_bytes + out_bytes, transcendentals=0
        ),
    )(place, *operands)


def block_of(index, size):
    return pl.ds(pl.multiple_of(index * size, size), size)


def split_link(place, link, keep, give):
    size = keep.shape[1] // 2
    for half in range(2):
        keep[:, half * size : (half + 1) * size] = link[:, block_of(place[half], size)]
        give[:, half * size : (half + 1) * size] = link[:, block_of(place[2 + half], size)]


def assemble_link(place, *refs):
    *pieces, out = refs
    size = pieces[0].shape[0]
    for step in range(SIDE):
        for half in range(2):
            target = block_of(half * SIDE + (place[0] ^ step), size)
            out[target, :] = pieces[2 * step + half][...]


def schur_kernel(place, *refs):
    separator, *pieces, schur, narrow = refs
    size = schur.shape[0]
    for step in range(SIDE):
        for k in range(SIDE):
            columns = block_of(k * place[1] + (place[0] ^ step) * place[2], size)
            value = separator[:, columns] - pieces[step][:, k * size : (k + 1) * size].astype(f32)
            schur[:, columns] = value
            narrow[:, columns] = value.astype(bf16)


def finish_kernel(place, narrow, weight, *refs):
    *pieces, sweep, residual = refs
    rows, nodes = narrow.shape
    share = pieces[0].shape[0]
    iterate = jnp.concatenate([piece[:, :nodes] for piece in pieces], axis=0)
    terms = lax.dot_general(
        iterate, narrow[...], (((1,), (1,)), ((), ())), preferred_element_type=f32
    )
    for step in range(SIDE):
        extra = [
            pieces[step][:, nodes + k * rows : nodes + (k + 1) * rows].astype(f32) for k in range(3)
        ]
        value = extra[1] + extra[2]
        target = block_of(place[0] ^ step, share)
        sweep[target, :] = value
        residual[target, :] = (
            value / weight[...] - terms[step * share : (step + 1) * share] - extra[0]
        )


def gather_groups(along_reduce):
    groups = []
    for p in range(PARTITIONS):
        for k in range(SIDE):
            if (p % 2 == 0) == along_reduce:
                groups.append([p * PLANE + k * SIDE + x for x in range(SIDE)])
            else:
                groups.append([p * PLANE + y * SIDE + k for y in range(SIDE)])
    return groups


def gathered(array, along_reduce):
    return lax.all_gather(
        array, AXES, axis=0, tiled=True, axis_index_groups=gather_groups(along_reduce)
    )


def along_reduce(value, step):
    return permuted(
        value, lambda p, y, x: (p, y, x ^ step) if p % 2 == 0 else (p, y ^ step, x)
    )


def shards(interior_inverse, coupling, separator, link, source, weights):
    inverse_rows, coupling_rows, separator_rows = interior_inverse[0], coupling[0], separator[0]
    link_rows, source_rows, weight_row = link[0], source[0], weights[0]
    rows, nodes = link_rows.shape
    keys = source_rows.shape[0]
    share = keys // SIDE
    line = SIDE * rows
    half = 2 * line
    shape = jax.ShapeDtypeStruct
    p = lax.axis_index("tm").astype(jnp.int32)
    b = lax.axis_index("blk").astype(jnp.int32)
    y, x = b >> 2, b & 3
    even = (p & 1) == 0
    r = jnp.where(even, x, y)
    pair = y >> 1
    ring = ((y + 1) >> 1) & 1
    out_place = jnp.where(even, y & 1, pair)
    in_place = jnp.where(even, pair, y & 1)
    in_low = jnp.where(even, ring, 2 * pair)
    in_high = jnp.where(even, 3 - ring, 2 * pair + 1)
    away_low = jnp.where(even, 1 - ring, 2 - 2 * pair)
    away_high = jnp.where(even, 2 + ring, 3 - 2 * pair)
    place = jnp.stack([x, y])

    coupling_in = gathered(coupling_rows, False)

    def ordered(pieces):
        stacked = jnp.stack(pieces)
        return [
            lax.dynamic_index_in_dim(stacked, x ^ k, 0, keepdims=False) for k in range(SIDE)
        ]

    def spread_x(array):
        return [array] + [along_x(array, step) for step in (1, 2, 3)]

    def exchange_x(chunk):
        return [chunk(0)] + [along_x(chunk(step), step) for step in (1, 2, 3)]

    keep, give = kernel_call(
        split_link,
        jnp.stack([in_low, in_high, away_low, away_high]),
        [link_rows],
        [shape((rows, half), bf16)] * 2,
    )
    got = permuted(give, lambda p, y, x: (p, partner(p, y), x))
    started = weight_row[None, :] * source_rows

    def source_chunk(step):
        part = lax.dynamic_slice(started, ((x ^ step) * share, 0), (share, rows))
        return jnp.concatenate([part, jnp.broadcast_to(weight_row[None, :], (8, rows))], axis=0)

    line_values = jnp.concatenate(ordered(exchange_x(source_chunk)), axis=1)
    keep, got, line_values = tie((keep, got, line_values))
    line_weights = line_values[share : share + 1]
    two = jnp.where(
        out_place == 0, jnp.concatenate([keep, got]), jnp.concatenate([got, keep])
    )
    coupling_late = tie(coupling_rows, two)
    turned = jnp.where(
        even,
        coupling_late,
        coupling_late.reshape(rows, SIDE, SIDE, rows).transpose(0, 2, 1, 3).reshape(rows, nodes),
    )
    outer = gathered(jnp.concatenate([inverse_rows, turned], axis=1), True)
    left, right = along_x(two, 1), along_x(two, 3)
    pieces = [
        two[:rows],
        two[rows:],
        left[:rows],
        left[rows:],
        along_x(left[:rows], 3),
        along_x(right[rows:], 1),
        right[:rows],
        right[rows:],
    ]
    away_weights = permuted(line_weights, lambda p, y, x: (p, partner(p, y), x))
    (block,) = kernel_call(assemble_link, place, pieces, [shape((half, half), bf16)])
    weight_half = jnp.where(
        out_place == 0,
        jnp.concatenate([line_weights, away_weights], axis=1),
        jnp.concatenate([away_weights, line_weights], axis=1),
    )
    zeros = jnp.zeros((share, line), f32)
    own = jnp.where(
        out_place == 0,
        jnp.concatenate([line_values[:share], zeros], axis=1),
        jnp.concatenate([zeros, line_values[:share]], axis=1),
    )

    own = tie(own, turned)

    message = own.astype(bf16)
    final = message
    for turn in range(1, PARTITIONS):
        far, near = turn_messages(message, turn - 1)
        previous = (far.astype(f32) + near.astype(f32)).astype(bf16)
        if turn == 10:
            outer, coupling_in = tie((outer, coupling_in), message)
            inner = lax.dot_general(
                outer[:, :nodes], coupling_in, (((1,), (1,)), ((), ())), preferred_element_type=f32
            ).astype(bf16)
            inner_all = gathered(inner, False)
            own = tie(own, inner)
        product = lax.dot_general(
            previous, block, (((1,), (1,)), ((), ())), preferred_element_type=f32
        )
        message = (own - weight_half * product).astype(bf16)
        final = jnp.where(p == turn, message, final)

    total = final.astype(f32) + permuted(
        final, lambda p, y, x: (p, partner(p, y), x)
    ).astype(f32)
    rounded = total.astype(bf16)

    back = jnp.dot(rounded, block, preferred_element_type=f32)
    mine = lax.dynamic_slice(back, (0, in_place * line), (share, line))
    theirs = lax.dynamic_slice(back, (0, (1 - in_place) * line), (share, line)).astype(bf16)
    rest = permuted(
        jnp.concatenate([rounded, theirs], axis=1), lambda p, y, x: (p, other(p, y), x)
    )
    inner_all = tie(inner_all, rounded)
    folded = jnp.dot(outer[:, nodes:], inner_all, preferred_element_type=f32).astype(bf16)

    rest = tie(rest, folded)
    following = permuted(
        (mine + rest[:, half:].astype(f32)).astype(bf16),
        lambda p, y, x: ((p - 1) % PARTITIONS, y, x),
    )
    following = jnp.where(p < PARTITIONS - 1, following, jnp.zeros_like(following))

    m0, m1, r0, r1 = rounded[:, :line], rounded[:, line:], rest[:, :line], rest[:, line:half]
    lines = jnp.where(
        even,
        jnp.where(
            pair == 0,
            jnp.concatenate([m0, m1, r0, r1], axis=1),
            jnp.concatenate([r0, r1, m0, m1], axis=1),
        ),
        jnp.where(
            ring == 0,
            jnp.concatenate([m0, r0, r1, m1], axis=1),
            jnp.concatenate([r0, m0, m1, r1], axis=1),
        ),
    )
    sweep_line = lax.dynamic_slice(total, (0, out_place * line), (share, line))
    sweep_high = sweep_line.astype(bf16)
    sweep_low = (sweep_line - sweep_high.astype(f32)).astype(bf16)

    def last_chunk(step):
        start = (0, (x ^ step) * rows)
        extra = [
            lax.dynamic_slice(array, start, (share, rows))
            for array in (following, sweep_high, sweep_low)
        ]
        return jnp.concatenate([lines] + extra, axis=1)

    last = exchange_x(last_chunk)

    def folded_chunk(step):
        return lax.dynamic_slice(folded, ((r ^ step) * rows, 0), (rows, line))

    back_rows = [folded_chunk(0)] + [along_reduce(folded_chunk(s), s) for s in (1, 2, 3)]
    schur_rows, narrow = kernel_call(
        schur_kernel,
        jnp.stack([r, jnp.where(even, SIDE, 1), jnp.where(even, 1, SIDE)]),
        [separator_rows] + back_rows,
        [shape((rows, nodes), f32), shape((rows, nodes), bf16)],
    )
    sweep, residual = kernel_call(
        finish_kernel,
        place,
        [narrow, weight_row[None, :]] + last,
        [shape((keys, rows), f32)] * 2,
        flops=2 * keys * rows * nodes,
    )
    return schur_rows[None], sweep[None], residual[None]


def solution(mesh):
    in_specs = (
        P("tm", "blk", None),
        P("tm", "blk", None),
        P("tm", "blk", None),
        P("tm", "blk", None),
        P("tm", None, "blk"),
        P("tm", "blk"),
    )
    out_specs = (P("tm", "blk", None), P("tm", None, "blk"), P("tm", None, "blk"))
    return jax.shard_map(shards, mesh=mesh, in_specs=in_specs, out_specs=out_specs, check_vma=False)
```

```python
import jax
import jax.numpy as jnp
from jax import lax
from jax.experimental import pallas as pl
from jax.experimental.pallas import tpu as pltpu
from jax.sharding import PartitionSpec as P

AXES = ("tm", "blk")
SIDE = 4
PLANE = SIDE * SIDE
PARTITIONS = 16
f32, bf16 = jnp.float32, jnp.bfloat16


def partner(p, y):
    return y ^ 1 if p % 2 == 0 else y ^ 3


def other(p, y):
    return y ^ 3 if p % 2 == 0 else y ^ 1


def permuted(value, rule, partitions=range(PARTITIONS)):
    pairs = []
    for p in partitions:
        for b in range(PLANE):
            target, y, x = rule(p, *divmod(b, SIDE))
            pairs.append((p * PLANE + b, target * PLANE + y * SIDE + x))
    return lax.ppermute(value, AXES, pairs)


def along_x(value, step):
    return permuted(value, lambda p, y, x: (p, y, x ^ step))


def along_y(value, step):
    return permuted(value, lambda p, y, x: (p, y ^ step, x))


def turn_messages(message, last):
    if last % 2 == 0:
        far = permuted(message, lambda p, y, x: (p ^ 1, y ^ 1, x))
        near = permuted(message, lambda p, y, x: (p ^ 1, y, x))
    else:
        far = permuted(message, lambda p, y, x: (p + 1, partner(p, y), x), [last])
        near = permuted(message, lambda p, y, x: (p + 1, y, x), [last])
    return far, near


def tie(values, *others):
    return lax.optimization_barrier((values, others))[0]


def kernel_call(body, place, operands, out_shapes, flops=0):
    out_bytes = sum(s.size * s.dtype.itemsize for s in out_shapes)
    in_bytes = sum(o.size * o.dtype.itemsize for o in operands)
    whole = pl.BlockSpec(memory_space=pltpu.VMEM)
    return pl.pallas_call(
        body,
        out_shape=out_shapes,
        in_specs=[pl.BlockSpec(memory_space=pltpu.SMEM)] + [whole] * len(operands),
        out_specs=[whole] * len(out_shapes),
        compiler_params=pltpu.CompilerParams(vmem_limit_bytes=24 * 1024 * 1024),
        cost_estimate=pl.CostEstimate(
            flops=flops, bytes_accessed=in_bytes + out_bytes, transcendentals=0
        ),
    )(place, *operands)


def block_of(index, size):
    return pl.ds(pl.multiple_of(index * size, size), size)


def split_link(place, link, keep, give):
    size = keep.shape[1] // 2
    for half in range(2):
        keep[:, half * size : (half + 1) * size] = link[:, block_of(place[half], size)]
        give[:, half * size : (half + 1) * size] = link[:, block_of(place[2 + half], size)]


def assemble_link(place, *refs):
    *pieces, out = refs
    size = pieces[0].shape[0]
    for step in range(SIDE):
        for half in range(2):
            target = block_of(half * SIDE + (place[0] ^ step), size)
            out[target, :] = pieces[2 * step + half][...]


def schur_kernel(place, *refs):
    separator, *pieces, schur, narrow = refs
    size = schur.shape[0]
    for step in range(SIDE):
        for k in range(SIDE):
            columns = block_of(k * place[1] + (place[0] ^ step) * place[2], size)
            value = separator[:, columns] - pieces[step][:, k * size : (k + 1) * size].astype(f32)
            schur[:, columns] = value
            narrow[:, columns] = value.astype(bf16)


def finish_kernel(place, narrow, weight, *refs):
    *pieces, sweep, residual = refs
    rows, nodes = narrow.shape
    share = pieces[0].shape[0]
    iterate = jnp.concatenate([piece[:, :nodes] for piece in pieces], axis=0)
    terms = lax.dot_general(
        iterate, narrow[...], (((1,), (1,)), ((), ())), preferred_element_type=f32
    )
    for step in range(SIDE):
        extra = [
            pieces[step][:, nodes + k * rows : nodes + (k + 1) * rows].astype(f32) for k in range(3)
        ]
        value = extra[1] + extra[2]
        target = block_of(place[0] ^ step, share)
        sweep[target, :] = value
        residual[target, :] = (
            value / weight[...] - terms[step * share : (step + 1) * share] - extra[0]
        )


def gather_groups(along_reduce):
    groups = []
    for p in range(PARTITIONS):
        for k in range(SIDE):
            if (p % 2 == 0) == along_reduce:
                groups.append([p * PLANE + k * SIDE + x for x in range(SIDE)])
            else:
                groups.append([p * PLANE + y * SIDE + k for y in range(SIDE)])
    return groups


def gathered(array, along_reduce):
    return lax.all_gather(
        array, AXES, axis=0, tiled=True, axis_index_groups=gather_groups(along_reduce)
    )


def along_reduce(value, step):
    return permuted(
        value, lambda p, y, x: (p, y, x ^ step) if p % 2 == 0 else (p, y ^ step, x)
    )


def shards(interior_inverse, coupling, separator, link, source, weights):
    inverse_rows, coupling_rows, separator_rows = interior_inverse[0], coupling[0], separator[0]
    link_rows, source_rows, weight_row = link[0], source[0], weights[0]
    rows, nodes = link_rows.shape
    keys = source_rows.shape[0]
    share = keys // SIDE
    line = SIDE * rows
    half = 2 * line
    shape = jax.ShapeDtypeStruct
    p = lax.axis_index("tm").astype(jnp.int32)
    b = lax.axis_index("blk").astype(jnp.int32)
    y, x = b >> 2, b & 3
    even = (p & 1) == 0
    r = jnp.where(even, x, y)
    pair = y >> 1
    ring = ((y + 1) >> 1) & 1
    out_place = jnp.where(even, y & 1, pair)
    in_place = jnp.where(even, pair, y & 1)
    in_low = jnp.where(even, ring, 2 * pair)
    in_high = jnp.where(even, 3 - ring, 2 * pair + 1)
    away_low = jnp.where(even, 1 - ring, 2 - 2 * pair)
    away_high = jnp.where(even, 2 + ring, 3 - 2 * pair)
    place = jnp.stack([x, y])

    coupling_in = gathered(coupling_rows, False)

    def ordered(pieces):
        stacked = jnp.stack(pieces)
        return [
            lax.dynamic_index_in_dim(stacked, x ^ k, 0, keepdims=False) for k in range(SIDE)
        ]

    def spread_x(array):
        return [array] + [along_x(array, step) for step in (1, 2, 3)]

    def exchange_x(chunk):
        return [chunk(0)] + [along_x(chunk(step), step) for step in (1, 2, 3)]

    keep, give = kernel_call(
        split_link,
        jnp.stack([in_low, in_high, away_low, away_high]),
        [link_rows],
        [shape((rows, half), bf16)] * 2,
    )
    got = permuted(give, lambda p, y, x: (p, partner(p, y), x))
    started = weight_row[None, :] * source_rows

    def source_chunk(step):
        part = lax.dynamic_slice(started, ((x ^ step) * share, 0), (share, rows))
        return jnp.concatenate([part, jnp.broadcast_to(weight_row[None, :], (8, rows))], axis=0)

    line_values = jnp.concatenate(ordered(exchange_x(source_chunk)), axis=1)
    keep, got, line_values = tie((keep, got, line_values))
    line_weights = line_values[share : share + 1]
    two = jnp.where(
        out_place == 0, jnp.concatenate([keep, got]), jnp.concatenate([got, keep])
    )
    left, right = along_x(two, 1), along_x(two, 3)
    coupling_late = tie(coupling_rows, right)
    turned = jnp.where(
        even,
        coupling_late,
        coupling_late.reshape(rows, SIDE, SIDE, rows).transpose(0, 2, 1, 3).reshape(rows, nodes),
    )
    outer = gathered(jnp.concatenate([inverse_rows, turned], axis=1), True)
    pieces = [
        two[:rows],
        two[rows:],
        left[:rows],
        left[rows:],
        along_x(left[:rows], 3),
        along_x(right[rows:], 1),
        right[:rows],
        right[rows:],
    ]
    away_weights = permuted(line_weights, lambda p, y, x: (p, partner(p, y), x))
    (block,) = kernel_call(assemble_link, place, pieces, [shape((half, half), bf16)])
    weight_half = jnp.where(
        out_place == 0,
        jnp.concatenate([line_weights, away_weights], axis=1),
        jnp.concatenate([away_weights, line_weights], axis=1),
    )
    zeros = jnp.zeros((share, line), f32)
    own = jnp.where(
        out_place == 0,
        jnp.concatenate([line_values[:share], zeros], axis=1),
        jnp.concatenate([zeros, line_values[:share]], axis=1),
    )

    own = tie(own, turned)

    message = own.astype(bf16)
    final = message
    for turn in range(1, PARTITIONS):
        far, near = turn_messages(message, turn - 1)
        previous = (far.astype(f32) + near.astype(f32)).astype(bf16)
        if turn == 10:
            outer, coupling_in = tie((outer, coupling_in), message)
            inner = lax.dot_general(
                outer[:, :nodes], coupling_in, (((1,), (1,)), ((), ())), preferred_element_type=f32
            ).astype(bf16)
            inner_all = gathered(inner, False)
            own = tie(own, inner)
        product = lax.dot_general(
            previous, block, (((1,), (1,)), ((), ())), preferred_element_type=f32
        )
        message = (own - weight_half * product).astype(bf16)
        final = jnp.where(p == turn, message, final)

    total = final.astype(f32) + permuted(
        final, lambda p, y, x: (p, partner(p, y), x)
    ).astype(f32)
    rounded = total.astype(bf16)

    back = jnp.dot(rounded, block, preferred_element_type=f32)
    mine = lax.dynamic_slice(back, (0, in_place * line), (share, line))
    theirs = lax.dynamic_slice(back, (0, (1 - in_place) * line), (share, line)).astype(bf16)
    rest = permuted(
        jnp.concatenate([rounded, theirs], axis=1), lambda p, y, x: (p, other(p, y), x)
    )
    inner_all = tie(inner_all, rounded)
    folded = jnp.dot(outer[:, nodes:], inner_all, preferred_element_type=f32).astype(bf16)

    rest = tie(rest, folded)
    following = permuted(
        (mine + rest[:, half:].astype(f32)).astype(bf16),
        lambda p, y, x: ((p - 1) % PARTITIONS, y, x),
    )
    following = jnp.where(p < PARTITIONS - 1, following, jnp.zeros_like(following))

    m0, m1, r0, r1 = rounded[:, :line], rounded[:, line:], rest[:, :line], rest[:, line:half]
    lines = jnp.where(
        even,
        jnp.where(
            pair == 0,
            jnp.concatenate([m0, m1, r0, r1], axis=1),
            jnp.concatenate([r0, r1, m0, m1], axis=1),
        ),
        jnp.where(
            ring == 0,
            jnp.concatenate([m0, r0, r1, m1], axis=1),
            jnp.concatenate([r0, m0, m1, r1], axis=1),
        ),
    )
    sweep_line = lax.dynamic_slice(total, (0, out_place * line), (share, line))
    sweep_high = sweep_line.astype(bf16)
    sweep_low = (sweep_line - sweep_high.astype(f32)).astype(bf16)

    def last_chunk(step):
        start = (0, (x ^ step) * rows)
        extra = [
            lax.dynamic_slice(array, start, (share, rows))
            for array in (following, sweep_high, sweep_low)
        ]
        return jnp.concatenate([lines] + extra, axis=1)

    last = exchange_x(last_chunk)

    def folded_chunk(step):
        return lax.dynamic_slice(folded, ((r ^ step) * rows, 0), (rows, line))

    back_rows = [folded_chunk(0)] + [along_reduce(folded_chunk(s), s) for s in (1, 2, 3)]
    schur_rows, narrow = kernel_call(
        schur_kernel,
        jnp.stack([r, jnp.where(even, SIDE, 1), jnp.where(even, 1, SIDE)]),
        [separator_rows] + back_rows,
        [shape((rows, nodes), f32), shape((rows, nodes), bf16)],
    )
    sweep, residual = kernel_call(
        finish_kernel,
        place,
        [narrow, weight_row[None, :]] + last,
        [shape((keys, rows), f32)] * 2,
        flops=2 * keys * rows * nodes,
    )
    return schur_rows[None], sweep[None], residual[None]


def solution(mesh):
    in_specs = (
        P("tm", "blk", None),
        P("tm", "blk", None),
        P("tm", "blk", None),
        P("tm", "blk", None),
        P("tm", None, "blk"),
        P("tm", "blk"),
    )
    out_specs = (P("tm", "blk", None), P("tm", None, "blk"), P("tm", None, "blk"))
    return jax.shard_map(shards, mesh=mesh, in_specs=in_specs, out_specs=out_specs, check_vma=False)
```
